32 devices in a mesh: mode: 4 (over y, core), ex: 2 (over x), ey: 4 (over z).
Axes of the slice: x: 2, y: 2, z: 4, core: 2. Of those that a mesh axis runs over, the one named last changes fastest.
Arguments:
- forcing: float32 [64, 81, 2048], P('mode', None, ('ex', 'ey')), may hold values from -6 to 6
- eigen_basis: float32 [7, 7], replicated, may hold values from -2 to 2
- eigen_values: float32 [7], replicated, may hold values from 1 to 20
- coupling: float32 [32, 49], replicated, may hold values from -0.875 to 0.875
- inverse_blocks: float32 [64, 256, 256], P('mode'), may hold values from -0.0625 to 0.0625
- slots: int32 [32, 2048], P(None, ('ex', 'ey')), may hold values from 0 to 255
- sides: int32 [8, 256], P(('ex', 'ey')), may hold values from 0 to 4
- partners: int32 [8, 256], P(('ex', 'ey')), may hold values from 0 to 255
Outputs:
- interior: float32 [64, 49, 2048], P('mode', None, ('ex', 'ey'))
- interface: float32 [64, 8, 256], P('mode', ('ex', 'ey'))
The draws below stay inside these ranges and needn't reach their ends.
Inputs may be any that keep to these rules, and one draw needn't show every extreme that they name: slots of one quadrilateral name unknowns of its own group. `sides`: 0 means not shared; 1 to 4 name the neighbour at +ex, -ex, +ey, -ey.
All inputs are finite; a program needn't handle non-finite values.
Results may differ from the reference program's by a relative error of at most 0.000075.
Values sent between devices are 32-bit elements; how exact they have to be, the bound alone decides.
No kernel may reach another device: no remote copies, remote signals or barrier semaphores. Data moves between devices by JAX's collectives and lax.ppermute only.
A program may use at most 64 MiB of HBM per device.

```python
import math
import jax
import jax.numpy as jnp
import numpy as np
from jax import lax

PLANES = 64
NODES = 81
INNER = 49
RIM = 32
EL_DEV = 256
NI = 256
GROUPS = 8
ELEMS = 2048
N_EX = 2
N_EY = 4


def plant(entries, stream_key, low, top_value):
    extent = entries.shape
    spot = [jax.random.randint(jax.random.fold_in(stream_key, axis), (), 0, extent[axis]) for axis in range(len(extent))]
    entries = entries.at[tuple(spot)].set(low)
    longest = extent.index(max(extent))
    spot[longest] = (spot[longest] + 1) % extent[longest]
    return entries.at[tuple(spot)].set(top_value)


def levels(own_key, dims, split, smallest, high):
    def one(position, parts):
        heights = jax.random.uniform(jax.random.fold_in(jax.random.fold_in(own_key, 6), position), (parts,), jnp.float32, smallest / len(split), high / len(split))
        return jnp.repeat(jnp.exp(heights), dims[position] // parts).reshape((-1,) + (1,) * (len(dims) - position - 1))

    level = one(*split[0])
    for cut in split[1:]:
        level = level * one(*cut)
    return level


def scatter_about(stream_key, extent, scale, most, shards=(), kind=jnp.bfloat16):
    loudness = levels(stream_key, extent, shards, -0.22, 0.18) if shards else 1.0
    values = jax.random.normal(stream_key, extent, jnp.float32) * scale * loudness
    return jnp.minimum(jnp.maximum(values, -most), most).astype(kind)


def setup_inputs(seed: int = 0) -> dict:
    key_list = jax.random.split(jax.random.key(seed), 9)
    forcing = scatter_about(key_list[0], (PLANES, NODES, ELEMS), 1.0, 6.0, ((0, 4), (2, 8)), jnp.float32)
    eigen_basis = scatter_about(key_list[1], (7, 7), 7 ** -0.5, 2.0, (), jnp.float32)
    eigen_values = jnp.clip(jnp.exp(jax.random.uniform(key_list[2], (7,), jnp.float32, math.log(1.0), math.log(20.0))), 1.0, 20.0)
    coupling = scatter_about(key_list[3], (RIM, INNER), INNER ** -0.5, 0.875, (), jnp.float32)
    inverse_blocks = scatter_about(key_list[4], (PLANES, NI, NI), (32 * NI) ** -0.5, 0.0625, ((0, 4),), jnp.float32)
    slots = plant(jax.random.randint(key_list[5], (RIM, ELEMS), 0, NI), jax.random.fold_in(key_list[5], 1), 0, NI - 1).astype(jnp.int32)
    sides = plant(jax.random.randint(key_list[6], (GROUPS, NI), 0, 5), jax.random.fold_in(key_list[6], 1), 0, 4).astype(jnp.int32)
    partners = plant(jax.random.randint(key_list[7], (GROUPS, NI), 0, NI), jax.random.fold_in(key_list[7], 1), 0, NI - 1).astype(jnp.int32)
    return dict(forcing=forcing, eigen_basis=eigen_basis, eigen_values=eigen_values, coupling=coupling, inverse_blocks=inverse_blocks, slots=slots, sides=sides, partners=partners)


helm_base = 0.5
wave_unit = 1.0 / 64.0

def is_inner(node_id):
    return 1 <= node_id // 9 <= 7 and 1 <= node_id % 9 <= 7

def node_lists():
    inner_nodes = np.array([node_id for node_id in range(81) if is_inner(node_id)], dtype=np.int32)
    rim_nodes = np.array([node_id for node_id in range(81) if not is_inner(node_id)], dtype=np.int32)
    return (inner_nodes, rim_nodes)

def wave_numbers(row_ids, count):
    return jnp.where(row_ids == 1, count // 2, row_ids // 2).astype(jnp.int32)

def dft_table(count):
    row_ids = jnp.arange(count, dtype=jnp.int32)
    wave_ids = wave_numbers(row_ids, count)
    phase_ids = wave_ids[:, None] * row_ids[None, :] % count
    angles = 2.0 * math.pi / count * phase_ids.astype(jnp.float32)
    odd_rows = (row_ids % 2 == 1) & (row_ids != 1)
    scales = jnp.where(row_ids <= 1, math.sqrt(1.0 / count), math.sqrt(2.0 / count)).astype(jnp.float32)
    return jnp.where(odd_rows[:, None], jnp.sin(angles), jnp.cos(angles)) * scales[:, None]

def mode_shifts(row_ids, count):
    waves = wave_numbers(row_ids, count).astype(jnp.float32) * wave_unit
    return helm_base + waves * waves

def fast_solve(values, eigen_basis, eigen_values, shifts):
    kron_basis = jnp.kron(eigen_basis, eigen_basis)
    pair_sums = (eigen_values[:, None] + eigen_values[None, :]).reshape(-1)
    spectra = jnp.einsum('ji,rje->rie', kron_basis, values, precision=lax.Precision.HIGHEST)
    spectra = spectra / (pair_sums[None, :, None] + shifts[:, None, None])
    return jnp.einsum('ij,rje->rie', kron_basis, spectra, precision=lax.Precision.HIGHEST)

def reference(forcing, eigen_basis, eigen_values, coupling, inverse_blocks, slots, sides, partners):
    inner_nodes, rim_nodes = node_lists()
    table = dft_table(PLANES)
    spectral = jnp.einsum('rp,pne->rne', table, forcing, precision=lax.Precision.HIGHEST)
    shifts = mode_shifts(jnp.arange(PLANES, dtype=jnp.int32), PLANES)
    solved = fast_solve(spectral[:, inner_nodes, :], eigen_basis, eigen_values, shifts)
    rim_residual = spectral[:, rim_nodes, :] - jnp.einsum('ji,rie->rje', coupling, solved, precision=lax.Precision.HIGHEST)
    group_of = jnp.arange(ELEMS, dtype=jnp.int32) // EL_DEV
    targets = (slots + group_of[None, :] * NI).reshape(-1).astype(jnp.int32)
    flat_rim = jnp.moveaxis(rim_residual, 0, -1).reshape(-1, PLANES)
    local_sums = jax.ops.segment_sum(flat_rim, targets, num_segments=GROUPS * NI)
    group_grid = local_sums.reshape(N_EX, N_EY, NI, PLANES)
    padded = jnp.pad(group_grid, ((1, 1), (1, 1), (0, 0), (0, 0)))
    neighbours = (padded[2:, 1:-1], padded[:-2, 1:-1], padded[1:-1, 2:], padded[1:-1, :-2])
    partner_grid = jnp.broadcast_to(partners.reshape(N_EX, N_EY, NI, 1), (N_EX, N_EY, NI, PLANES))
    side_grid = sides.reshape(N_EX, N_EY, NI)
    assembled = group_grid
    for side_code, neighbour in enumerate(neighbours):
        picked = jnp.take_along_axis(neighbour, partner_grid, axis=2)
        assembled = assembled + jnp.where((side_grid == side_code + 1)[..., None], picked, jnp.zeros_like(picked))
    assembled = assembled.reshape(GROUPS, NI, PLANES)
    interface = jnp.einsum('rst,gtr->rgs', inverse_blocks, assembled, precision=lax.Precision.HIGHEST)
    boundary = interface.reshape(PLANES, GROUPS * NI)[:, targets].reshape(PLANES, RIM, ELEMS)
    lifted = jnp.einsum('ji,rje->rie', coupling, boundary, precision=lax.Precision.HIGHEST)
    interior = solved - fast_solve(lifted, eigen_basis, eigen_values, shifts)
    return (interior, interface)
```

```python
import functools
import math

import jax
import jax.numpy as jnp
import numpy as np
from jax import lax
from jax.experimental import pallas as pl
from jax.experimental.pallas import tpu as pltpu
from jax.sharding import PartitionSpec as P

helm_base = 0.5
wave_unit = 1.0 / 64.0
f32, bf16 = jnp.float32, jnp.bfloat16
TILE = 8
CORES = 2
RAW_TILES = 2


def is_inner(node_id):
    return 1 <= node_id // 9 <= 7 and 1 <= node_id % 9 <= 7


def node_lists():
    inner_nodes = np.array([node_id for node_id in range(81) if is_inner(node_id)], dtype=np.int32)
    rim_nodes = np.array(
        [node_id for node_id in range(81) if not is_inner(node_id)], dtype=np.int32
    )
    return (inner_nodes, rim_nodes)


def wave_ids(count):
    rows = np.arange(count)
    return np.where(rows == 1, count // 2, rows // 2)


def table_np(count):
    rows = np.arange(count)
    angles = 2.0 * math.pi / count * (wave_ids(count)[:, None] * rows[None, :] % count)
    odd = (rows % 2 == 1) & (rows != 1)
    scales = np.where(rows <= 1, math.sqrt(1.0 / count), math.sqrt(2.0 / count))
    return np.where(odd[:, None], np.sin(angles), np.cos(angles)) * scales[:, None]


def split_np(table):
    high = table.astype(np.float32).astype(jnp.bfloat16)
    low = (table - high.astype(np.float64)).astype(np.float32).astype(jnp.bfloat16)
    return np.stack([high, low])


def pair_tables(count, share):
    table = table_np(count)
    devices = count // share
    near, far, shifts = [], [], []
    for dev in range(devices):
        rows = lambda d: slice(d * share, (d + 1) * share)
        mate, across = dev ^ 1, dev ^ CORES
        order = lambda d: np.concatenate([table[:, rows(d)], table[:, rows(d ^ 1)]], axis=1)
        chip, other = order(dev), order(across)
        near.append(np.concatenate([chip[rows(across)], chip[rows(dev)]]))
        far.append(other[rows(dev)])
        shifts.append((wave_ids(count)[rows(dev)] * wave_unit) ** 2 + helm_base)
    return np.stack(near), np.stack(far), np.stack(shifts)


def split(values):
    high = values.astype(bf16)
    return high, (values - high.astype(f32)).astype(bf16)


def dot(left, right):
    return jnp.dot(left, right, preferred_element_type=f32)


def dot_t(left, right):
    return lax.dot_general(left, right, (((1,), (1,)), ((), ())), preferred_element_type=f32)


def dot3(left_parts, right):
    stacked, high = left_parts
    right_high, right_low = split(right)
    both = dot(stacked, right_high)
    rows = high.shape[0]
    return both[:rows] + both[rows:] + dot(high, right_low)


def stacked(matrix):
    high, low = split(matrix)
    return jnp.concatenate([high, low], axis=0), high


def iota(shape, dim):
    return lax.broadcasted_iota(jnp.int32, shape, dim)


def digits(index, base, most):
    lead = jnp.zeros_like(index)
    for step in range(1, most):
        lead = lead + (index >= step * base).astype(jnp.int32)
    return lead, index - lead * base


def spread(basis_ref, row_digit, col_digit, flip):
    size = basis_ref.shape[0]
    out = jnp.zeros(jnp.broadcast_shapes(row_digit.shape, col_digit.shape), f32)
    for c in range(size):
        line = jnp.zeros(col_digit.shape, f32)
        for a in range(size):
            entry = basis_ref[c, a] if flip else basis_ref[a, c]
            line = jnp.where(col_digit == a, entry, line)
        out = jnp.where(row_digit == c, line, out)
    return out


def kron_rows(basis_ref, rows, nodes, all_nodes, flip=False, first=0):
    size = basis_ref.shape[0]
    row_ids = iota((rows, 1), 0) + first
    c, d = digits(row_ids, size, size + 2)
    col_ids = iota((1, nodes), 1)
    if all_nodes:
        a, b = digits(col_ids, size + 2, size + 2)
        a, b = a - 1, b - 1
    else:
        a, b = digits(col_ids, size, size + 2)
    b = jnp.where((a >= 0) & (a < size), b, -1)
    d = jnp.where(c < size, d, -1)
    return spread(basis_ref, c, a, flip) * spread(basis_ref, d, b, flip)


def member(slots_row, unknowns):
    ids = iota((unknowns, slots_row.shape[1]), 0)
    return jnp.where(ids == slots_row, 1.0, 0.0).astype(bf16)


def stack_split(values):
    high, low = split(values)
    return jnp.concatenate([high, low], axis=0)


def fold(values):
    half = values.shape[0] // 2
    return values[:half] + values[half:]


def raw_kernel(forcing, basis, out):
    rows = out.shape[1]
    lift = stacked(kron_rows(basis, rows, forcing.shape[1], True))
    for plane in range(forcing.shape[0]):
        out[plane] = dot3(lift, forcing[plane])


def near_kernel(dev, own, mate, basis, slots, near, small, out, mid, rem, raw, lifted, *, rim_nodes, inner):
    share, nodes, elems = own.shape
    rows = lifted.shape[1]
    unknowns = out.shape[1]
    raw_rows = raw.shape[1]
    mid_rows = mid.shape[1]
    lift = stacked(kron_rows(basis, rows, nodes, True))
    for part, source in enumerate((own, mate)):
        for plane in range(share):
            lifted[part * share + plane] = dot3(lift, source[plane])
    total = jnp.zeros((4 * share, unknowns), f32)
    for j, node in enumerate(rim_nodes):
        both = jnp.concatenate([own[:, int(node), :], mate[:, int(node), :]], axis=0)
        total = total + dot_t(stack_split(both), member(slots[j : j + 1, :], unknowns))
    condensed = fold(total)
    near_high, near_low = near[0], near[1]
    near_parts = jnp.concatenate([near_high, near_low], axis=0), near_high
    half = share * TILE
    for tile in range((raw_rows + mid_rows) // TILE):
        block = lifted[:, tile * TILE : (tile + 1) * TILE, :].reshape(2 * share * TILE, elems)
        if tile * TILE < raw_rows:
            parts = jnp.concatenate([near_high[half:], near_low[half:]], axis=0), near_high[half:]
            raw[:, tile * TILE : (tile + 1) * TILE, :] = dot3(parts, block).reshape(share, TILE, elems)
        else:
            spectra = dot3(near_parts, block)
            place = slice(tile * TILE - raw_rows, (tile + 1) * TILE - raw_rows)
            out_rows = spectra[:half].reshape(share, TILE, elems)
            for r in range(share):
                out[r * mid_rows + place.start : r * mid_rows + place.stop, :] = out_rows[r]
            mid[:, place, :] = spectra[half:].reshape(share, TILE, elems)
    small_parts = jnp.concatenate([small[0], small[1]], axis=0), small[0]
    tail = [lifted[:, row, :] for row in range(raw_rows + mid_rows, inner)] + [condensed]
    for i, block in enumerate(tail):
        spectra = dot3(small_parts, block)
        start = share * (mid_rows + i)
        out[start : start + share, :] = spectra[:share]
        rem[i] = spectra[share:]


def far_kernel(dev, raw, first, second, far, out):
    share, rows, elems = raw.shape
    parts = jnp.concatenate([far[0], far[1]], axis=0), far[0]
    for tile in range(rows // TILE):
        place = slice(tile * TILE, (tile + 1) * TILE)
        block = jnp.concatenate([first[:, place, :], second[:, place, :]], axis=0)
        block = block.reshape(2 * share * TILE, elems)
        out[:, place, :] = raw[:, place, :] + dot3(parts, block).reshape(share, TILE, elems)


def inverse_diagonal(values, shifts, mode, rows, lanes):
    size = values.shape[0]
    c, d = digits(iota((rows, lanes), 0), size, size + 2)
    total = jnp.zeros((rows, lanes), f32)
    for i in range(size):
        total = total + jnp.where(c == i, values[i], 0.0) + jnp.where(d == i, values[i], 0.0)
    return 1.0 / (total + shifts[mode])


def solve_kernel(raw, mid, rem, received, shifts, basis, values, coupling, slots, spectral, sums, coupled):
    share, mid_rows, elems = mid.shape
    raw_rows = raw.shape[1]
    rows = spectral.shape[1]
    rim, inner = coupling.shape
    unknowns = sums.shape[1]
    split_at = raw_rows + mid_rows
    for r in range(share):
        spectral[r, :raw_rows, :] = raw[r]
        spectral[r, raw_rows:split_at, :] = mid[r] + received[r * mid_rows : (r + 1) * mid_rows, :]
    spectral[:, split_at:, :] = jnp.zeros((share, rows - split_at, elems), f32)
    remaining = inner - split_at
    for i in range(remaining):
        start = share * (mid_rows + i)
        spectral[:, split_at + i, :] = rem[i] + received[start : start + share, :]
    start = share * (mid_rows + remaining)
    condensed = rem[remaining] + received[start : start + share, :]
    lift = kron_rows(basis, inner, rows, False, flip=True)
    couple = stacked(jnp.dot(coupling[...], lift, precision=lax.Precision.HIGHEST, preferred_element_type=f32))
    for r in range(share):
        inverse = inverse_diagonal(values, shifts, r, rows, 128)
        inverse = jnp.concatenate([inverse] * (elems // 128), axis=1)
        coupled[r] = dot3(couple, spectral[r] * inverse)
    total = jnp.zeros((2 * share, unknowns), f32)
    for j in range(rim):
        total = total + dot_t(stack_split(coupled[:, j, :]), member(slots[j : j + 1, :], unknowns))
    sums[...] = condensed - fold(total)


def back_kernel(*refs, neighbours):
    sums, near = refs[0], refs[1 : 1 + neighbours]
    codes, sides, partners, inverse, slots, spectral, shifts, basis, values, coupling = refs[1 + neighbours : 11 + neighbours]
    interior, interface, boundary = refs[11 + neighbours :]
    share, unknowns = sums.shape
    rows, elems = spectral.shape[1:]
    rim, inner = coupling.shape
    pick = member(partners[...], unknowns)
    stack = jnp.concatenate([part for ref in near for part in split(ref[...])], axis=0)
    picked = dot(stack, pick)
    assembled = sums[...]
    for i in range(neighbours):
        block = picked[2 * share * i : 2 * share * (i + 1)]
        assembled = assembled + jnp.where(sides[...] == codes[i], fold(block), 0.0)
    asm_high, asm_low = split(assembled)
    lines = []
    for r in range(share):
        inv_high, inv_low = split(inverse[r])
        full = dot_t(jnp.concatenate([asm_high, asm_low], axis=0), inv_high)
        product = full[:share] + full[share:] + dot_t(asm_high, inv_low)
        lines.append(product[r : r + 1])
    solved = jnp.concatenate(lines, axis=0)
    interface[...] = solved
    solved_parts = stack_split(solved)
    for j in range(rim):
        boundary[:, j, :] = fold(dot(solved_parts, member(slots[j : j + 1, :], unknowns)))
    lift = kron_rows(basis, inner, rows, False, flip=True)
    couple = jnp.dot(coupling[...], lift, precision=lax.Precision.HIGHEST, preferred_element_type=f32)
    couple_t = stacked(couple.T)
    lift_parts = stacked(jnp.concatenate([lift, jnp.zeros((rows - inner, rows), f32)], axis=0))
    for r in range(share):
        pull = dot3(couple_t, boundary[r])
        inverse_d = inverse_diagonal(values, shifts, r, rows, 128)
        inverse_d = jnp.concatenate([inverse_d] * (elems // 128), axis=1)
        interior[r] = dot3(lift_parts, (spectral[r] - pull) * inverse_d)[:inner]


VMEM = pl.BlockSpec(memory_space=pltpu.VMEM)
SMEM = pl.BlockSpec(memory_space=pltpu.SMEM)


def params():
    return pltpu.CompilerParams(vmem_limit_bytes=48 * 2**20)


def shape(*dims):
    return jax.ShapeDtypeStruct(dims, f32)


def swaps(block, axis):
    count = lax.axis_size(axis)
    even = 1 - lax.axis_index(axis) % 2
    got = []
    for first in range(2):
        pairs = [(i, i + 1) for i in range(first, count - 1, 2)]
        if pairs:
            moves = pairs + [(b, a) for a, b in pairs]
            ahead = even if first == 0 else 1 - even
            got.append((lax.ppermute(block, axis, moves), 1 - ahead))
    return got


def paired(forcing, eigen_basis, eigen_values, coupling, inverse_blocks, slots, sides, partners):
    inner_nodes, rim_nodes = node_lists()
    share, nodes, elems = forcing.shape
    unknowns = inverse_blocks.shape[1]
    modes = lax.axis_size("mode")
    inner, rim = len(inner_nodes), len(rim_nodes)
    rows = -(-inner // TILE) * TILE
    raw_rows = RAW_TILES * TILE
    mid_rows = inner // TILE * TILE - raw_rows
    remaining = inner - raw_rows - mid_rows
    me = lax.axis_index("mode")
    near, far, shift_table = pair_tables(modes * share, share)
    eye = np.eye(TILE)
    near_big = np.stack([split_np(np.kron(t, eye)) for t in near])
    near_small = np.stack([split_np(t) for t in near])
    far_big = np.stack([split_np(np.kron(t, eye)) for t in far])
    shifts = lax.dynamic_index_in_dim(jnp.asarray(shift_table, f32), me, 0, keepdims=False)
    index = me.reshape(1).astype(jnp.int32)

    mates = [(i, i ^ 1) for i in range(modes)]
    across = [(i, i ^ CORES) for i in range(modes)]

    mate_forcing = lax.ppermute(forcing, "mode", mates)
    raw_out = pl.pallas_call(
        raw_kernel,
        out_shape=shape(share, raw_rows, elems),
        in_specs=[VMEM, SMEM],
        out_specs=VMEM,
        compiler_params=params(),
        name="raw_rows",
    )(forcing, eigen_basis)
    raw_first = lax.ppermute(raw_out, "mode", across)

    def mine(*dims):
        return pl.BlockSpec((None,) + dims, lambda i, dev: (dev[0],) + (0,) * len(dims))

    def whole(*dims):
        return pl.BlockSpec(dims, lambda i, dev: (0,) * len(dims))

    big, small = near_big.shape[1:], near_small.shape[1:]
    out_rows = share * (mid_rows + remaining + 1)
    smem_grid = pl.BlockSpec(memory_space=pltpu.SMEM)
    send, mid, rem, raw_near = pl.pallas_call(
        functools.partial(near_kernel, rim_nodes=rim_nodes, inner=inner),
        out_shape=(
            shape(out_rows, elems),
            shape(share, mid_rows, elems),
            shape(remaining + 1, share, elems),
            shape(share, raw_rows, elems),
        ),
        grid_spec=pltpu.PrefetchScalarGridSpec(
            num_scalar_prefetch=1,
            grid=(1,),
            in_specs=[
                whole(*forcing.shape),
                whole(*forcing.shape),
                smem_grid,
                whole(*slots.shape),
                mine(*big),
                mine(*small),
            ],
            out_specs=(
                whole(out_rows, elems),
                whole(share, mid_rows, elems),
                whole(remaining + 1, share, elems),
                whole(share, raw_rows, elems),
            ),
            scratch_shapes=[pltpu.VMEM((2 * share, rows, elems), f32)],
        ),
        compiler_params=params(),
        name="near_spectra",
    )(index, forcing, mate_forcing, eigen_basis, slots, jnp.asarray(near_big), jnp.asarray(near_small))
    received = lax.ppermute(send, "mode", across)

    raw_second = lax.ppermute(raw_first, "mode", mates)
    raw = pl.pallas_call(
        far_kernel,
        out_shape=shape(share, raw_rows, elems),
        grid_spec=pltpu.PrefetchScalarGridSpec(
            num_scalar_prefetch=1,
            grid=(1,),
            in_specs=[whole(share, raw_rows, elems)] * 3 + [mine(*far_big.shape[1:])],
            out_specs=whole(share, raw_rows, elems),
        ),
        compiler_params=params(),
        name="far_spectra",
    )(index, raw_near, raw_first, raw_second, jnp.asarray(far_big))

    spectral, sums = pl.pallas_call(
        solve_kernel,
        out_shape=(shape(share, rows, elems), shape(share, unknowns)),
        in_specs=[VMEM] * 4 + [SMEM] * 3 + [VMEM] * 2,
        out_specs=(VMEM, VMEM),
        scratch_shapes=[pltpu.VMEM((share, rim, elems), f32)],
        compiler_params=params(),
        name="residual",
    )(raw, mid, rem, received, shifts, eigen_basis, eigen_values, coupling, slots)

    got = [(block, 1 + back) for block, back in swaps(sums, "ex")]
    got += [(block, 3 + back) for block, back in swaps(sums, "ey")]
    codes = jnp.stack([jnp.asarray(code, jnp.int32) for _, code in got])
    interior, interface = pl.pallas_call(
        functools.partial(back_kernel, neighbours=len(got)),
        out_shape=(shape(share, inner, elems), shape(share, unknowns)),
        in_specs=[VMEM] * (1 + len(got)) + [SMEM] + [VMEM] * 5 + [SMEM] * 3 + [VMEM],
        out_specs=(VMEM, VMEM),
        scratch_shapes=[pltpu.VMEM((share, rim, elems), f32)],
        compiler_params=params(),
        name="back_solve",
    )(
        sums,
        *[block for block, _ in got],
        codes,
        sides,
        partners,
        inverse_blocks,
        slots,
        spectral,
        shifts,
        eigen_basis,
        eigen_values,
        coupling,
    )
    return (interior, interface[:, None, :])


def extended(block, sides, width):
    for axis, dim in sides:
        count = lax.axis_size(axis)
        forward = [(i, i + 1) for i in range(count - 1)]
        backward = [(target, source) for source, target in forward]
        low = lax.ppermute(
            lax.slice_in_dim(block, block.shape[dim] - width, None, axis=dim), axis, forward
        )
        high = lax.ppermute(lax.slice_in_dim(block, 0, width, axis=dim), axis, backward)
        block = jnp.concatenate([low, block, high], axis=dim)
    return block


def wave_numbers(row_ids, count):
    return jnp.where(row_ids == 1, count // 2, row_ids // 2)


def dft_table(count):
    row_ids = jnp.arange(count, dtype=jnp.int32)
    wave_ids = wave_numbers(row_ids, count)
    phase_ids = wave_ids[:, None] * row_ids[None, :] % count
    angles = 2.0 * math.pi / count * phase_ids.astype(jnp.float32)
    odd_rows = (row_ids % 2 == 1) & (row_ids != 1)
    scales = jnp.where(row_ids <= 1, math.sqrt(1.0 / count), math.sqrt(2.0 / count)).astype(
        jnp.float32
    )
    return jnp.where(odd_rows[:, None], jnp.sin(angles), jnp.cos(angles)) * scales[:, None]


def mode_shifts(row_ids, count):
    waves = wave_numbers(row_ids, count).astype(jnp.float32) * wave_unit
    return helm_base + waves * waves


def fast_solve(values, eigen_basis, eigen_values, shifts):
    kron_basis = jnp.kron(eigen_basis, eigen_basis)
    pair_sums = (eigen_values[:, None] + eigen_values[None, :]).reshape(-1)
    spectra = jnp.einsum("ji,rje->rie", kron_basis, values, precision=lax.Precision.HIGHEST)
    spectra = spectra / (pair_sums[None, :, None] + shifts[:, None, None])
    return jnp.einsum("ij,rje->rie", kron_basis, spectra, precision=lax.Precision.HIGHEST)


def general(forcing, eigen_basis, eigen_values, coupling, inverse_blocks, slots, sides, partners):
    inner_nodes, rim_nodes = node_lists()
    plane_dev = forcing.shape[0]
    elem_dev = forcing.shape[2]
    unknowns = inverse_blocks.shape[1]
    modes_axis = lax.axis_size("mode")
    plane_count = modes_axis * plane_dev
    table = dft_table(plane_count)
    row_ids = lax.axis_index("mode") * plane_dev + jnp.arange(plane_dev, dtype=jnp.int32)
    shifts = mode_shifts(row_ids, plane_count)
    onehot = (slots.reshape(-1)[:, None] == jnp.arange(unknowns, dtype=jnp.int32)[None, :]).astype(
        jnp.float32
    )
    inner_width = len(inner_nodes) * elem_dev
    rim_planes = forcing[:, rim_nodes, :].reshape(plane_dev, -1)
    condensed = jnp.dot(rim_planes, onehot, precision=lax.Precision.HIGHEST)
    payload = jnp.concatenate(
        [forcing[:, inner_nodes, :].reshape(plane_dev, -1), condensed], axis=1
    )
    total_width = payload.shape[1]
    sectioned = payload.reshape(plane_dev, modes_axis, total_width // modes_axis)
    spectra = jnp.einsum(
        "rp,pkc->rkc",
        table,
        lax.all_to_all(sectioned, "mode", split_axis=1, concat_axis=0, tiled=True),
        precision=lax.Precision.HIGHEST,
    )
    spectral = lax.all_to_all(spectra, "mode", split_axis=0, concat_axis=1, tiled=True).reshape(
        plane_dev, total_width
    )
    inner_part = spectral[:, :inner_width].reshape(plane_dev, len(inner_nodes), elem_dev)
    condensed_hat = spectral[:, inner_width:]
    solved = fast_solve(inner_part, eigen_basis, eigen_values, shifts)
    coupled = jnp.einsum("ji,rie->rje", coupling, solved, precision=lax.Precision.HIGHEST)
    local_sums = condensed_hat - jnp.dot(
        coupled.reshape(plane_dev, -1), onehot, precision=lax.Precision.HIGHEST
    )
    padded = extended(local_sums.reshape(1, 1, -1), (("ex", 0), ("ey", 1)), 1)
    neighbours = (
        padded[2, 1].reshape(plane_dev, unknowns),
        padded[0, 1].reshape(plane_dev, unknowns),
        padded[1, 2].reshape(plane_dev, unknowns),
        padded[1, 0].reshape(plane_dev, unknowns),
    )
    assembled = local_sums
    for side_code, neighbour in enumerate(neighbours):
        picked = jnp.take(neighbour, partners[0], axis=1)
        assembled = assembled + jnp.where(
            (sides[0] == side_code + 1)[None, :], picked, jnp.zeros_like(picked)
        )
    interface = jnp.einsum("rst,rt->rs", inverse_blocks, assembled, precision=lax.Precision.HIGHEST)
    boundary = jnp.dot(interface, onehot.T, precision=lax.Precision.HIGHEST).reshape(
        plane_dev, len(rim_nodes), elem_dev
    )
    lifted = jnp.einsum("ji,rje->rie", coupling, boundary, precision=lax.Precision.HIGHEST)
    interior = solved - fast_solve(lifted, eigen_basis, eigen_values, shifts)
    return (interior, interface[:, None, :])


def on_device(*args):
    modes = lax.axis_size("mode")
    if modes == CORES * CORES:
        return paired(*args)
    return general(*args)


def solution(mesh):
    placed = (
        P("mode", None, ("ex", "ey")),
        P(),
        P(),
        P(),
        P("mode", None, None),
        P(None, ("ex", "ey")),
        P(("ex", "ey"), None),
        P(("ex", "ey"), None),
    )
    return jax.shard_map(
        on_device,
        mesh=mesh,
        in_specs=placed,
        out_specs=(P("mode", None, ("ex", "ey")), P("mode", ("ex", "ey"), None)),
        check_vma=False,
    )
```

```python
import functools
import math

import jax
import jax.numpy as jnp
import numpy as np
from jax import lax
from jax.experimental import pallas as pl
from jax.experimental.pallas import tpu as pltpu
from jax.sharding import PartitionSpec as P

helm_base = 0.5
wave_unit = 1.0 / 64.0
f32, bf16 = jnp.float32, jnp.bfloat16
TILE = 8
CORES = 2
SPAN = 256
LIMIT = 12 * 2**20


def is_inner(node_id):
    return 1 <= node_id // 9 <= 7 and 1 <= node_id % 9 <= 7


def node_lists():
    inner_nodes = np.array([node_id for node_id in range(81) if is_inner(node_id)], dtype=np.int32)
    rim_nodes = np.array(
        [node_id for node_id in range(81) if not is_inner(node_id)], dtype=np.int32
    )
    return (inner_nodes, rim_nodes)


def split(values):
    high = values.astype(bf16)
    return high, (values - high.astype(f32)).astype(bf16)


def stack_split(values):
    return jnp.concatenate(split(values), axis=0)


def dot(left, right):
    return jnp.dot(left, right, preferred_element_type=f32)


def exact(left, right):
    return jnp.dot(left, right, preferred_element_type=f32, precision=lax.Precision.HIGHEST)


def dot_t(left, right):
    return lax.dot_general(left, right, (((1,), (1,)), ((), ())), preferred_element_type=f32)


def fold(values):
    half = values.shape[0] // 2
    return values[:half] + values[half:]


def dot3(left, high, low):
    return fold(dot(left, high)) + dot(left[: left.shape[0] // 2], low)


def iota(shape, dim):
    return lax.broadcasted_iota(jnp.int32, shape, dim)


def chosen(values, line):
    rows, width = values.shape
    lanes = 128
    out = []
    for start in range(0, line.shape[1], lanes):
        index = jnp.broadcast_to(line[:, start : start + lanes], (rows, lanes))
        place = index % lanes
        block = jnp.take_along_axis(values[:, :lanes], place, axis=1)
        for first in range(lanes, width, lanes):
            other = jnp.take_along_axis(values[:, first : first + lanes], place, axis=1)
            block = jnp.where(index >= first, other, block)
        out.append(block)
    return jnp.concatenate(out, axis=1)


def member(line, unknowns):
    return jnp.where(iota((unknowns, line.shape[1]), 0) == line, 1.0, 0.0).astype(bf16)


def weighted(scalars, blocks):
    total = scalars[0] * blocks[0]
    for scalar, block in zip(scalars[1:], blocks[1:]):
        total = total + scalar * block
    return total


def kron_matrix(basis):
    size = basis.shape[0]
    count = size * size

    def digits(index):
        lead = jnp.zeros_like(index)
        for step in range(1, size):
            lead = lead + (index >= step * size).astype(jnp.int32)
        return lead, index - lead * size

    def spread(row_digit, col_digit):
        out = jnp.zeros((count, count), f32)
        for i in range(size):
            line = jnp.zeros((1, count), f32)
            for j in range(size):
                line = jnp.where(col_digit == j, basis[i, j], line)
            out = jnp.where(row_digit == i, line, out)
        return out

    (a, b), (c, d) = digits(iota((count, 1), 0)), digits(iota((1, count), 1))
    return spread(a, c) * spread(b, d)


def wave_of(row, count):
    return jnp.where(row == 1, count // 2, row // 2)


def dft_blocks(device, devices, share, rows_of, cols_of):
    count = devices * share
    tall, width = share * len(rows_of), share * len(cols_of)
    copies = SPAN // width

    def index_of(ids, offsets):
        part = ids // share
        owner = jnp.where(part == 0, device ^ offsets[0], 0)
        for i, offset in enumerate(offsets[1:]):
            owner = jnp.where(part == i + 1, device ^ offset, owner)
        return owner * share + ids % share

    row = index_of(iota((tall, SPAN), 0), rows_of)
    plane = index_of(iota((tall, SPAN), 1) % width, cols_of)
    angle = 2.0 * math.pi / count * (wave_of(row, count) * plane % count).astype(f32)
    odd = (row % 2 == 1) & (row != 1)
    scale = jnp.where(row <= 1, math.sqrt(1.0 / count), math.sqrt(2.0 / count))
    block = jnp.where(odd, jnp.sin(angle), jnp.cos(angle)) * scale
    full = jnp.concatenate([block] * copies, axis=0)
    same = iota(full.shape, 0) // tall == iota(full.shape, 1) // width
    return stack_split(jnp.where(same, full, 0.0))


def corner(left, rows, cols):
    height = left.shape[0] // 2
    if (rows, cols) == (height, left.shape[1]):
        return left
    return jnp.concatenate([left[:rows, :cols], left[height : height + rows, :cols]], axis=0)


def octet(block, part):
    rows, _, elems = block.shape
    return block[:, part * TILE : (part + 1) * TILE, :].reshape(rows * TILE, elems)


def take_kernel(nodes, out, ready):
    lines, side = out.shape[:2]
    move = pltpu.make_async_copy(nodes.at[1 : 1 + lines, 1 : 1 + side], out, ready)
    move.start()
    move.wait()


def near_kernel(dev, own, mate, slots, send, keep, *, devices, nodes, rim_nodes):
    _, share, elems = own.shape
    unknowns = send.shape[2]
    pair = 2 * share
    left = dft_blocks(dev[0], devices, share, (CORES, 0), (0, 1))
    total = jnp.zeros((2 * pair, unknowns), f32)
    for j, node in enumerate(rim_nodes):
        both = jnp.concatenate([own[node], mate[node]], axis=0)
        total = total + dot_t(stack_split(both), member(slots[j : j + 1, :], unknowns))
    spectra = dot3(corner(left, pair, pair), *split(fold(total)))
    send[len(nodes)] = spectra[:share]
    keep[len(nodes)] = spectra[share:]
    group = left.shape[1] // pair
    for first in range(0, len(nodes), group):
        part = nodes[first : first + group]
        block = jnp.concatenate([ref[node] for node in part for ref in (own, mate)], axis=0)
        rows = block.shape[0]
        spectra = dot3(corner(left, rows, rows), *split(block))
        for k in range(len(part)):
            send[first + k] = spectra[pair * k : pair * k + share]
            keep[first + k] = spectra[pair * k + share : pair * (k + 1)]


def prepare_kernel(
    dev, basis, values, coupling, slots, after, lead, rest, lead_solve, rest_solve, pull, where, modes, *, devices
):
    del after
    size = basis.shape[0]
    rim, inner = coupling.shape
    elems = slots.shape[1]
    octets = lead.shape[0]
    first = lead.shape[2]
    edge = inner * TILE
    kron = kron_matrix(basis)
    couple = exact(coupling[...], kron)
    left = stack_split(jnp.concatenate([kron, couple], axis=0))
    right = jnp.concatenate([kron, couple], axis=0).T
    total = right.shape[1]
    n = iota((inner, total), 0)
    sums = jnp.zeros(n.shape, f32)
    for c in range(size):
        sums = sums + jnp.where((n >= c * size) & (n < (c + 1) * size), values[c], 0.0)
        for d in range(size):
            sums = sums + jnp.where(n == c * size + d, values[d], 0.0)
    for r in range(octets * TILE):
        wave = wave_of(dev[0] * (octets * TILE) + r, devices * octets * TILE).astype(f32) * wave_unit
        modes[r, :total, :] = dot3(left, *split(right / (sums + (helm_base + wave * wave))))
    spread = jnp.where(iota((total, total * TILE), 0) == iota((total, total * TILE), 1) // TILE, 1.0, 0.0).astype(bf16)

    def widened(matrix):
        rows = matrix.shape[0]
        out = []
        for half in split(matrix):
            full = dot(half, spread)
            same = iota(full.shape, 0) % TILE == iota(full.shape, 1) % TILE
            out.append(jnp.where(same, full, 0.0).astype(bf16))
        return out

    for part in range(octets):
        block = jnp.transpose(modes[part * TILE : (part + 1) * TILE], (1, 0, 2))[:total]
        high, low = widened(block.reshape(total * TILE, total))

        def put(out, rows, cols):
            out[part] = jnp.concatenate([high[rows, cols], low[rows, cols]], axis=0)

        put(lead, slice(edge, None), slice(0, first))
        put(rest, slice(edge, None), slice(first, edge))
        put(lead_solve, slice(0, edge), slice(0, first))
        put(rest_solve, slice(0, edge), slice(first, edge))
        put(pull, slice(0, edge), slice(edge, None))
    columns = slots[...].astype(f32).T
    ids = iota((elems, where.shape[1]), 1).astype(f32)
    for j in range(rim):
        where[j * elems : (j + 1) * elems, :] = jnp.where(ids == columns[:, j : j + 1], 1.0, 0.0).astype(bf16)


def far_kernel(dev, own, mate, first, second, lead, lead_solve, coupled, solved, spectral, *, devices, nodes):
    share, elems = first.shape[1:]
    left = dft_blocks(dev[0], devices, share, (0,), (0, 1, CORES, CORES + 1))
    group = left.shape[1] // (4 * share)
    for start in range(0, len(nodes), group):
        rows = range(start, min(start + group, len(nodes)))
        block = jnp.concatenate([x for k in rows for x in (own[nodes[k]], mate[nodes[k]], first[k], second[k])], axis=0)
        spectra = dot3(corner(left, share * len(rows), 4 * share * len(rows)), *split(block))
        for i, k in enumerate(rows):
            spectral[k] = spectra[share * i : share * (i + 1)]
    for part in range(share // TILE):
        block = split(octet(spectral[...], part))
        for table, out in ((lead, coupled), (lead_solve, solved)):
            out[:, part * TILE : (part + 1) * TILE, :] = dot3(table[part], *block).reshape(-1, TILE, elems)


def residual_kernel(keep, received, lead, rest, where, spectral, sums):
    rows, share, elems = spectral.shape
    rim = lead.shape[0]
    spectral[...] = keep[:rows] + received[:rows]
    parts = []
    for part in range(share // TILE):
        block = dot3(rest[part], *split(octet(spectral[...], part)))
        parts.append(block.reshape(rim, TILE, elems) + octet(lead[...], part).reshape(rim, TILE, elems))
    coupled = jnp.concatenate(parts, axis=1)
    line = jnp.concatenate([stack_split(coupled[j]) for j in range(rim)], axis=1)
    sums[...] = keep[rows] + received[rows] - fold(dot(line, where[...]))


def solved_kernel(lead, rest, table, inverse, solved, held, ready):
    parts = ready.shape[0]
    size = inverse.shape[0] // parts
    moves = [
        pltpu.make_async_copy(inverse.at[i * size : (i + 1) * size], held.at[i * size : (i + 1) * size], ready.at[i])
        for i in range(parts)
    ]
    for move in moves:
        move.start()
    inner, share, elems = solved.shape
    for part in range(share // TILE):
        block = dot3(table[part], *split(octet(rest[...], part))).reshape(inner, TILE, elems)
        place = slice(part * TILE, (part + 1) * TILE)
        solved[:, place, :] = lead[:, place, :] + block
    for move in moves:
        move.wait()


def back_kernel(group, sums, *refs, codes):
    neighbours = len(codes)
    near = refs[:neighbours]
    sides, partners, inverse, slots, pull, solved, interior, interface = refs[neighbours:]
    share, unknowns = sums.shape
    inner, _, elems = interior.shape
    rim = slots.shape[0]
    assembled = sums[...]
    for i in range(neighbours):
        code = jnp.int32(codes[i][0])
        for g, other in enumerate(codes[i][1:], 1):
            code = jnp.where(group[0] == g, other, code)
        assembled = assembled + jnp.where(sides[...] == code, chosen(near[i][...], partners[...]), 0.0)
    lines = []
    for r in range(share):
        line = jnp.sum(inverse[r] * assembled[r : r + 1, :], axis=1).reshape(1, unknowns)
        interface[r] = line
        lines.append(line)
    values = jnp.concatenate(lines, axis=0)
    boundary = [chosen(values, slots[j : j + 1, :]) for j in range(rim)]
    for part in range(share // TILE):
        place = slice(part * TILE, (part + 1) * TILE)
        block = jnp.concatenate([block[place] for block in boundary], axis=0)
        lifted = dot3(pull[part], *split(block)).reshape(inner, TILE, elems)
        interior[:, place, :] = solved[:, place, :] - lifted


VMEM = pl.BlockSpec(memory_space=pltpu.VMEM)
ANY = pl.BlockSpec(memory_space=pl.ANY)
SMEM = pl.BlockSpec(memory_space=pltpu.SMEM)


def shape(*dims, dtype=f32):
    return jax.ShapeDtypeStruct(dims, dtype)


def kernel_call(body, outs, ins, name, micros, scratch=()):
    in_specs, arrays = [], []
    for item in ins:
        place, array = item if isinstance(item, tuple) else ("", item)
        in_specs.append({"smem": SMEM, "any": ANY}.get(place, VMEM))
        if place in ("any", "hbm", "vmem"):
            array = pltpu.with_memory_space_constraint(array, pltpu.VMEM if place == "vmem" else pltpu.HBM)
        arrays.append(array)
    return pl.pallas_call(
        body,
        out_shape=outs,
        in_specs=in_specs,
        out_specs=(VMEM,) * len(outs) if isinstance(outs, tuple) else VMEM,
        scratch_shapes=scratch,
        compiler_params=pltpu.CompilerParams(vmem_limit_bytes=LIMIT),
        cost_estimate=pl.CostEstimate(flops=0, transcendentals=0, bytes_accessed=int(micros * 3e6)),
        name=name,
    )(*arrays)


def exchanges(block):
    wide, tall = lax.axis_size("ex"), lax.axis_size("ey")
    group = lambda x, y: x * tall + y
    rounds = []
    for first in range(min(2, tall - 1)):
        pairs = {group(x, y): group(x, y + 1) for x in range(wide) for y in range(first, tall - 1, 2)}
        rounds.append(pairs)
    if len(rounds) == 2:
        busy = set(rounds[1]) | set(rounds[1].values())
        for y in range(tall):
            for x in range(0, wide - 1, 2):
                if not {group(x, y), group(x + 1, y)} & busy:
                    rounds[1][group(x, y)] = group(x + 1, y)
    for first in range(min(2, wide - 1)):
        rounds.append({group(x, y): group(x + 1, y) for x in range(first, wide - 1, 2) for y in range(tall)})
    got, known = [], set()
    for pairs in rounds:
        moves = [*pairs.items(), *((b, a) for a, b in pairs.items())]
        code = [-1] * (wide * tall)
        for a, b in moves:
            if (a, b) not in known:
                known.add((a, b))
                near = abs(a - b) == 1
                code[b] = (3 if near else 1) + (1 if a < b else 0)
        got.append((lax.ppermute(block, ("ex", "ey"), moves), tuple(code)))
    return got


def paired(forcing, eigen_basis, eigen_values, coupling, inverse_blocks, slots, sides, partners):
    inner_nodes, rim_nodes = node_lists()
    share, nodes, elems = forcing.shape
    unknowns = inverse_blocks.shape[1]
    modes = lax.axis_size("mode")
    inner, rim = len(inner_nodes), len(rim_nodes)
    side = round(math.sqrt(nodes))
    lines = -(-(inner - SPAN // TILE) // (side - 2))
    raw_rows = lines * (side - 2)
    rest_rows = inner - raw_rows
    octets = share // TILE
    dev = ("smem", lax.axis_index("mode").astype(jnp.int32).reshape(1))
    mates = [(i, i ^ 1) for i in range(modes)]
    across = [(i, i ^ CORES) for i in range(modes)]
    planes = jnp.transpose(forcing, (1, 0, 2))
    basis = ("smem", eigen_basis)
    raw_nodes = [int(node) for node in inner_nodes[:raw_rows]]
    rest_nodes = [int(node) for node in inner_nodes[raw_rows:]]

    own_raw = kernel_call(
        take_kernel,
        shape(lines, side - 2, share, elems),
        [("any", planes.reshape(side, side, share, elems))],
        "raw_rows",
        0.5,
        [pltpu.SemaphoreType.DMA],
    ).reshape(raw_rows, share, elems)
    planes, own_raw = lax.optimization_barrier((planes, own_raw))
    first = lax.ppermute(own_raw, "mode", across)
    mate_planes = lax.ppermute(planes, "mode", mates)
    send, keep = kernel_call(
        functools.partial(near_kernel, devices=modes, nodes=rest_nodes, rim_nodes=[int(node) for node in rim_nodes]),
        (shape(rest_rows + 1, share, elems), shape(rest_rows + 1, share, elems)),
        [dev, ("hbm", planes), mate_planes, ("hbm", slots)],
        "near_spectra",
        2.5,
    )
    received = lax.ppermute(send, "mode", across)
    tall = 2 * TILE
    lead, rest, lead_solve, rest_solve, pull, where = kernel_call(
        functools.partial(prepare_kernel, devices=modes),
        (
            shape(octets, tall * rim, raw_rows * TILE, dtype=bf16),
            shape(octets, tall * rim, rest_rows * TILE, dtype=bf16),
            shape(octets, tall * inner, raw_rows * TILE, dtype=bf16),
            shape(octets, tall * inner, rest_rows * TILE, dtype=bf16),
            shape(octets, tall * inner, rim * TILE, dtype=bf16),
            shape(rim * elems, unknowns, dtype=bf16),
        ),
        [dev, basis, ("smem", eigen_values), ("hbm", coupling), ("hbm", slots), keep],
        "prepare",
        4.0,
        [pltpu.VMEM((share, -(-(inner + rim) // TILE) * TILE, inner + rim), f32)],
    )
    second = lax.ppermute(first, "mode", mates)
    coupled_raw, solved_raw, _ = kernel_call(
        functools.partial(far_kernel, devices=modes, nodes=raw_nodes),
        (shape(rim, share, elems), shape(inner, share, elems), shape(raw_rows, share, elems)),
        [dev, ("hbm", planes), mate_planes, first, second, lead, lead_solve],
        "far_spectra",
        1.0,
    )
    spectral, sums = kernel_call(
        residual_kernel,
        (shape(rest_rows, share, elems), shape(share, unknowns)),
        [("vmem", x) for x in (keep, received, coupled_raw, rest, where)],
        "residual",
        1.5,
    )
    got = exchanges(sums)
    group = lax.axis_index(("ex", "ey")).astype(jnp.int32).reshape(1)
    solved, inverse_held = kernel_call(
        solved_kernel,
        (shape(inner, share, elems), shape(*inverse_blocks.shape)),
        [solved_raw, spectral, rest_solve, ("any", inverse_blocks)],
        "solved",
        1.0,
        [pltpu.SemaphoreType.DMA((4,))],
    )
    interior, interface = kernel_call(
        functools.partial(back_kernel, codes=[codes for _, codes in got]),
        (shape(inner, share, elems), shape(share, 1, unknowns)),
        [("smem", group), sums, *[block for block, _ in got], sides, partners, ("vmem", inverse_held), slots, ("vmem", pull), ("vmem", solved)],
        "back_solve",
        2.0,
    )
    return (jnp.transpose(interior, (1, 0, 2)), interface)


def extended(block, sides, width):
    for axis, dim in sides:
        count = lax.axis_size(axis)
        forward = [(i, i + 1) for i in range(count - 1)]
        backward = [(target, source) for source, target in forward]
        low = lax.ppermute(
            lax.slice_in_dim(block, block.shape[dim] - width, None, axis=dim), axis, forward
        )
        high = lax.ppermute(lax.slice_in_dim(block, 0, width, axis=dim), axis, backward)
        block = jnp.concatenate([low, block, high], axis=dim)
    return block


def wave_numbers(row_ids, count):
    return jnp.where(row_ids == 1, count // 2, row_ids // 2)


def dft_table(count):
    row_ids = jnp.arange(count, dtype=jnp.int32)
    wave_ids = wave_numbers(row_ids, count)
    phase_ids = wave_ids[:, None] * row_ids[None, :] % count
    angles = 2.0 * math.pi / count * phase_ids.astype(jnp.float32)
    odd_rows = (row_ids % 2 == 1) & (row_ids != 1)
    scales = jnp.where(row_ids <= 1, math.sqrt(1.0 / count), math.sqrt(2.0 / count)).astype(
        jnp.float32
    )
    return jnp.where(odd_rows[:, None], jnp.sin(angles), jnp.cos(angles)) * scales[:, None]


def mode_shifts(row_ids, count):
    waves = wave_numbers(row_ids, count).astype(jnp.float32) * wave_unit
    return helm_base + waves * waves


def fast_solve(values, eigen_basis, eigen_values, shifts):
    kron_basis = jnp.kron(eigen_basis, eigen_basis)
    pair_sums = (eigen_values[:, None] + eigen_values[None, :]).reshape(-1)
    spectra = jnp.einsum("ji,rje->rie", kron_basis, values, precision=lax.Precision.HIGHEST)
    spectra = spectra / (pair_sums[None, :, None] + shifts[:, None, None])
    return jnp.einsum("ij,rje->rie", kron_basis, spectra, precision=lax.Precision.HIGHEST)


def general(forcing, eigen_basis, eigen_values, coupling, inverse_blocks, slots, sides, partners):
    inner_nodes, rim_nodes = node_lists()
    plane_dev = forcing.shape[0]
    elem_dev = forcing.shape[2]
    unknowns = inverse_blocks.shape[1]
    modes_axis = lax.axis_size("mode")
    plane_count = modes_axis * plane_dev
    table = dft_table(plane_count)
    row_ids = lax.axis_index("mode") * plane_dev + jnp.arange(plane_dev, dtype=jnp.int32)
    shifts = mode_shifts(row_ids, plane_count)
    onehot = (slots.reshape(-1)[:, None] == jnp.arange(unknowns, dtype=jnp.int32)[None, :]).astype(
        jnp.float32
    )
    inner_width = len(inner_nodes) * elem_dev
    rim_planes = forcing[:, rim_nodes, :].reshape(plane_dev, -1)
    condensed = jnp.dot(rim_planes, onehot, precision=lax.Precision.HIGHEST)
    payload = jnp.concatenate(
        [forcing[:, inner_nodes, :].reshape(plane_dev, -1), condensed], axis=1
    )
    total_width = payload.shape[1]
    sectioned = payload.reshape(plane_dev, modes_axis, total_width // modes_axis)
    spectra = jnp.einsum(
        "rp,pkc->rkc",
        table,
        lax.all_to_all(sectioned, "mode", split_axis=1, concat_axis=0, tiled=True),
        precision=lax.Precision.HIGHEST,
    )
    spectral = lax.all_to_all(spectra, "mode", split_axis=0, concat_axis=1, tiled=True).reshape(
        plane_dev, total_width
    )
    inner_part = spectral[:, :inner_width].reshape(plane_dev, len(inner_nodes), elem_dev)
    condensed_hat = spectral[:, inner_width:]
    solved = fast_solve(inner_part, eigen_basis, eigen_values, shifts)
    coupled = jnp.einsum("ji,rie->rje", coupling, solved, precision=lax.Precision.HIGHEST)
    local_sums = condensed_hat - jnp.dot(
        coupled.reshape(plane_dev, -1), onehot, precision=lax.Precision.HIGHEST
    )
    padded = extended(local_sums.reshape(1, 1, -1), (("ex", 0), ("ey", 1)), 1)
    neighbours = (
        padded[2, 1].reshape(plane_dev, unknowns),
        padded[0, 1].reshape(plane_dev, unknowns),
        padded[1, 2].reshape(plane_dev, unknowns),
        padded[1, 0].reshape(plane_dev, unknowns),
    )
    assembled = local_sums
    for side_code, neighbour in enumerate(neighbours):
        picked = jnp.take(neighbour, partners[0], axis=1)
        assembled = assembled + jnp.where(
            (sides[0] == side_code + 1)[None, :], picked, jnp.zeros_like(picked)
        )
    interface = jnp.einsum("rst,rt->rs", inverse_blocks, assembled, precision=lax.Precision.HIGHEST)
    boundary = jnp.dot(interface, onehot.T, precision=lax.Precision.HIGHEST).reshape(
        plane_dev, len(rim_nodes), elem_dev
    )
    lifted = jnp.einsum("ji,rje->rie", coupling, boundary, precision=lax.Precision.HIGHEST)
    interior = solved - fast_solve(lifted, eigen_basis, eigen_values, shifts)
    return (interior, interface[:, None, :])


def on_device(*args):
    modes = lax.axis_size("mode")
    if modes == CORES * CORES:
        return paired(*args)
    return general(*args)


def solution(mesh):
    placed = (
        P("mode", None, ("ex", "ey")),
        P(),
        P(),
        P(),
        P("mode", None, None),
        P(None, ("ex", "ey")),
        P(("ex", "ey"), None),
        P(("ex", "ey"), None),
    )
    return jax.shard_map(
        on_device,
        mesh=mesh,
        in_specs=placed,
        out_specs=(P("mode", None, ("ex", "ey")), P("mode", ("ex", "ey"), None)),
        check_vma=False,
    )
```

```python
import functools
import math

import jax
import jax.numpy as jnp
import numpy as np
from jax import lax
from jax.experimental import pallas as pl
from jax.experimental.pallas import tpu as pltpu
from jax.sharding import PartitionSpec as P

helm_base = 0.5
wave_unit = 1.0 / 64.0
f32, bf16 = jnp.float32, jnp.bfloat16
TILE = 8
CORES = 2
SPAN = 256
LIMIT = 12 * 2**20


def is_inner(node_id):
    return 1 <= node_id // 9 <= 7 and 1 <= node_id % 9 <= 7


def node_lists():
    inner_nodes = np.array([node_id for node_id in range(81) if is_inner(node_id)], dtype=np.int32)
    rim_nodes = np.array(
        [node_id for node_id in range(81) if not is_inner(node_id)], dtype=np.int32
    )
    return (inner_nodes, rim_nodes)


def split(values):
    high = values.astype(bf16)
    return high, (values - high.astype(f32)).astype(bf16)


def stack_split(values):
    return jnp.concatenate(split(values), axis=0)


def dot(left, right):
    return jnp.dot(left, right, preferred_element_type=f32)


def exact(left, right):
    return jnp.dot(left, right, preferred_element_type=f32, precision=lax.Precision.HIGHEST)


def dot_t(left, right):
    return lax.dot_general(left, right, (((1,), (1,)), ((), ())), preferred_element_type=f32)


def fold(values):
    half = values.shape[0] // 2
    return values[:half] + values[half:]


def dot3(left, high, low):
    return fold(dot(left, high)) + dot(left[: left.shape[0] // 2], low)


def iota(shape, dim):
    return lax.broadcasted_iota(jnp.int32, shape, dim)


def chosen(blocks, line):
    lanes = 128
    width = blocks[0].shape[1]
    out = [[] for _ in blocks]
    for start in range(0, line.shape[1], lanes):
        index = jnp.broadcast_to(line[:, start : start + lanes], (TILE, lanes))
        place = index & (lanes - 1)
        beyond = [index >= first for first in range(lanes, width, lanes)]
        for block, parts in zip(blocks, out):
            found = jnp.take_along_axis(block[:, :lanes], place, axis=1)
            for i, mask in enumerate(beyond):
                first = (i + 1) * lanes
                found = jnp.where(mask, jnp.take_along_axis(block[:, first : first + lanes], place, axis=1), found)
            parts.append(found)
    return [jnp.concatenate(parts, axis=1) for parts in out]


def member(line, unknowns):
    return jnp.where(iota((unknowns, line.shape[1]), 0) == line, 1.0, 0.0).astype(bf16)


def weighted(scalars, blocks):
    total = scalars[0] * blocks[0]
    for scalar, block in zip(scalars[1:], blocks[1:]):
        total = total + scalar * block
    return total


def kron_matrix(basis):
    size = basis.shape[0]
    count = size * size

    def digits(index):
        lead = jnp.zeros_like(index)
        for step in range(1, size):
            lead = lead + (index >= step * size).astype(jnp.int32)
        return lead, index - lead * size

    def spread(row_digit, col_digit):
        out = jnp.zeros((count, count), f32)
        for i in range(size):
            line = jnp.zeros((1, count), f32)
            for j in range(size):
                line = jnp.where(col_digit == j, basis[i, j], line)
            out = jnp.where(row_digit == i, line, out)
        return out

    (a, b), (c, d) = digits(iota((count, 1), 0)), digits(iota((1, count), 1))
    return spread(a, c) * spread(b, d)


def wave_of(row, count):
    return jnp.where(row == 1, count // 2, row // 2)


def dft_blocks(device, devices, share, rows_of, cols_of):
    count = devices * share
    tall, width = share * len(rows_of), share * len(cols_of)
    copies = SPAN // width

    def index_of(ids, offsets):
        part = ids // share
        owner = jnp.where(part == 0, device ^ offsets[0], 0)
        for i, offset in enumerate(offsets[1:]):
            owner = jnp.where(part == i + 1, device ^ offset, owner)
        return owner * share + ids % share

    row = index_of(iota((tall, SPAN), 0), rows_of)
    plane = index_of(iota((tall, SPAN), 1) % width, cols_of)
    angle = 2.0 * math.pi / count * (wave_of(row, count) * plane % count).astype(f32)
    odd = (row % 2 == 1) & (row != 1)
    scale = jnp.where(row <= 1, math.sqrt(1.0 / count), math.sqrt(2.0 / count))
    block = jnp.where(odd, jnp.sin(angle), jnp.cos(angle)) * scale
    full = jnp.concatenate([block] * copies, axis=0)
    same = iota(full.shape, 0) // tall == iota(full.shape, 1) // width
    return stack_split(jnp.where(same, full, 0.0))


def corner(left, rows, cols):
    height = left.shape[0] // 2
    if (rows, cols) == (height, left.shape[1]):
        return left
    return jnp.concatenate([left[:rows, :cols], left[height : height + rows, :cols]], axis=0)


def octet(block, part):
    rows, _, elems = block.shape
    return block[:, part * TILE : (part + 1) * TILE, :].reshape(rows * TILE, elems)


def take_kernel(nodes, out, ready):
    lines, side = out.shape[:2]
    move = pltpu.make_async_copy(nodes.at[1 : 1 + lines, 1 : 1 + side], out, ready)
    move.start()
    move.wait()


def near_kernel(own, mate, slots, send, keep, *, devices, nodes, rim_nodes):
    _, share, elems = own.shape
    unknowns = send.shape[2]
    pair = 2 * share
    left = dft_blocks(lax.axis_index("mode"), devices, share, (CORES, 0), (0, 1))
    total = jnp.zeros((2 * pair, unknowns), f32)
    for j, node in enumerate(rim_nodes):
        both = jnp.concatenate([own[node], mate[node]], axis=0)
        total = total + dot_t(stack_split(both), member(slots[j : j + 1, :], unknowns))
    spectra = dot3(corner(left, pair, pair), *split(fold(total)))
    send[len(nodes)] = spectra[:share]
    keep[len(nodes)] = spectra[share:]
    group = left.shape[1] // pair
    for first in range(0, len(nodes), group):
        part = nodes[first : first + group]
        block = jnp.concatenate([ref[node] for node in part for ref in (own, mate)], axis=0)
        rows = block.shape[0]
        spectra = dot3(corner(left, rows, rows), *split(block))
        for k in range(len(part)):
            send[first + k] = spectra[pair * k : pair * k + share]
            keep[first + k] = spectra[pair * k + share : pair * (k + 1)]


def prepare_kernel(
    basis, values, coupling, slots, after, lead, rest, lead_solve, rest_solve, pull, where, modes, *, devices
):
    del after
    size = basis.shape[0]
    rim, inner = coupling.shape
    elems = slots.shape[1]
    octets = lead.shape[0]
    first = lead.shape[2]
    edge = inner * TILE
    kron = kron_matrix(basis)
    couple = exact(coupling[...], kron)
    left = stack_split(jnp.concatenate([kron, couple], axis=0))
    right = jnp.concatenate([kron, couple], axis=0).T
    total = right.shape[1]
    n = iota((inner, total), 0)
    sums = jnp.zeros(n.shape, f32)
    for c in range(size):
        sums = sums + jnp.where((n >= c * size) & (n < (c + 1) * size), values[c], 0.0)
        for d in range(size):
            sums = sums + jnp.where(n == c * size + d, values[d], 0.0)
    for r in range(octets * TILE):
        wave = wave_of(lax.axis_index("mode") * (octets * TILE) + r, devices * octets * TILE).astype(f32) * wave_unit
        modes[r, :total, :] = dot3(left, *split(right / (sums + (helm_base + wave * wave))))
    spread = jnp.where(iota((total, total * TILE), 0) == iota((total, total * TILE), 1) // TILE, 1.0, 0.0).astype(bf16)

    def widened(matrix):
        rows = matrix.shape[0]
        out = []
        for half in split(matrix):
            full = dot(half, spread)
            same = iota(full.shape, 0) % TILE == iota(full.shape, 1) % TILE
            out.append(jnp.where(same, full, 0.0).astype(bf16))
        return out

    for part in range(octets):
        block = jnp.transpose(modes[part * TILE : (part + 1) * TILE], (1, 0, 2))[:total]
        high, low = widened(block.reshape(total * TILE, total))

        def put(out, rows, cols):
            out[part] = jnp.concatenate([high[rows, cols], low[rows, cols]], axis=0)

        put(lead, slice(edge, None), slice(0, first))
        put(rest, slice(edge, None), slice(first, edge))
        put(lead_solve, slice(0, edge), slice(0, first))
        put(rest_solve, slice(0, edge), slice(first, edge))
        put(pull, slice(0, edge), slice(edge, None))
    columns = slots[...].astype(f32).T
    ids = iota((elems, where.shape[1]), 1).astype(f32)
    for j in range(rim):
        where[j * elems : (j + 1) * elems, :] = jnp.where(ids == columns[:, j : j + 1], 1.0, 0.0).astype(bf16)


def far_kernel(own, mate, first, second, lead, lead_solve, coupled, solved, spectral, *, devices, nodes):
    share, elems = first.shape[1:]
    left = dft_blocks(lax.axis_index("mode"), devices, share, (0,), (0, 1, CORES, CORES + 1))
    group = left.shape[1] // (4 * share)
    for start in range(0, len(nodes), group):
        rows = range(start, min(start + group, len(nodes)))
        block = jnp.concatenate([x for k in rows for x in (own[nodes[k]], mate[nodes[k]], first[k], second[k])], axis=0)
        spectra = dot3(corner(left, share * len(rows), 4 * share * len(rows)), *split(block))
        for i, k in enumerate(rows):
            spectral[k] = spectra[share * i : share * (i + 1)]
    for part in range(share // TILE):
        block = split(octet(spectral[...], part))
        for table, out in ((lead, coupled), (lead_solve, solved)):
            out[:, part * TILE : (part + 1) * TILE, :] = dot3(table[part], *block).reshape(-1, TILE, elems)


def residual_kernel(keep, received, lead, rest, where, spectral, sums):
    rows, share, elems = spectral.shape
    rim = lead.shape[0]
    spectral[...] = keep[:rows] + received[:rows]
    parts = []
    for part in range(share // TILE):
        block = dot3(rest[part], *split(octet(spectral[...], part)))
        parts.append(block.reshape(rim, TILE, elems) + octet(lead[...], part).reshape(rim, TILE, elems))
    coupled = jnp.concatenate(parts, axis=1)
    line = jnp.concatenate([stack_split(coupled[j]) for j in range(rim)], axis=1)
    sums[...] = keep[rows] + received[rows] - fold(dot(line, where[...]))


def solved_kernel(lead, rest, table, solved):
    inner, share, elems = solved.shape
    for part in range(share // TILE):
        block = dot3(table[part], *split(octet(rest[...], part))).reshape(inner, TILE, elems)
        place = slice(part * TILE, (part + 1) * TILE)
        solved[:, place, :] = lead[:, place, :] + block


def back_kernel(sums, *refs, codes):
    neighbours = len(codes)
    near = refs[:neighbours]
    sides, partners, inverse, slots, pull, solved, interior, interface = refs[neighbours:]
    share, unknowns = sums.shape
    inner, _, elems = interior.shape
    rim = slots.shape[0]
    group = lax.axis_index("ex") * lax.axis_size("ey") + lax.axis_index("ey")
    octets = [slice(start, start + TILE) for start in range(0, share, TILE)]
    assembled = [sums[place] for place in octets]
    for i in range(neighbours):
        code = jnp.int32(codes[i][0])
        for g, other in enumerate(codes[i][1:], 1):
            code = jnp.where(group == g, other, code)
        picked = chosen([near[i][place] for place in octets], partners[...])
        assembled = [part + jnp.where(sides[...] == code, new, 0.0) for part, new in zip(assembled, picked)]
    values = []
    for place, part in zip(octets, assembled):
        lines = []
        for r in range(TILE):
            line = jnp.sum(inverse[place.start + r] * part[r : r + 1, :], axis=1).reshape(1, unknowns)
            interface[place.start + r] = line
            lines.append(line)
        values.append(jnp.concatenate(lines, axis=0))
    boundary = [chosen(values, slots[j : j + 1, :]) for j in range(rim)]
    for part, place in enumerate(octets):
        block = jnp.concatenate([blocks[part] for blocks in boundary], axis=0)
        lifted = dot3(pull[part], *split(block)).reshape(inner, TILE, elems)
        interior[:, place, :] = solved[:, place, :] - lifted


VMEM = pl.BlockSpec(memory_space=pltpu.VMEM)
ANY = pl.BlockSpec(memory_space=pl.ANY)
SMEM = pl.BlockSpec(memory_space=pltpu.SMEM)


def shape(*dims, dtype=f32):
    return jax.ShapeDtypeStruct(dims, dtype)


def kernel_call(body, outs, ins, name, micros, scratch=()):
    in_specs, arrays = [], []
    for item in ins:
        place, array = item if isinstance(item, tuple) else ("", item)
        in_specs.append({"smem": SMEM, "any": ANY}.get(place, VMEM))
        if place in ("any", "hbm", "vmem"):
            array = pltpu.with_memory_space_constraint(array, pltpu.VMEM if place == "vmem" else pltpu.HBM)
        arrays.append(array)
    return pl.pallas_call(
        body,
        out_shape=outs,
        in_specs=in_specs,
        out_specs=(VMEM,) * len(outs) if isinstance(outs, tuple) else VMEM,
        scratch_shapes=scratch,
        compiler_params=pltpu.CompilerParams(vmem_limit_bytes=LIMIT),
        cost_estimate=pl.CostEstimate(flops=0, transcendentals=0, bytes_accessed=int(micros * 3e6)),
        name=name,
    )(*arrays)


def exchanges(block):
    wide, tall = lax.axis_size("ex"), lax.axis_size("ey")
    group = lambda x, y: x * tall + y
    rounds = []
    for first in range(min(2, tall - 1)):
        pairs = {group(x, y): group(x, y + 1) for x in range(wide) for y in range(first, tall - 1, 2)}
        rounds.append(pairs)
    if len(rounds) == 2:
        busy = set(rounds[1]) | set(rounds[1].values())
        for y in range(tall):
            for x in range(0, wide - 1, 2):
                if not {group(x, y), group(x + 1, y)} & busy:
                    rounds[1][group(x, y)] = group(x + 1, y)
    for first in range(min(2, wide - 1)):
        rounds.append({group(x, y): group(x + 1, y) for x in range(first, wide - 1, 2) for y in range(tall)})
    got, known = [], set()
    for pairs in rounds:
        moves = [*pairs.items(), *((b, a) for a, b in pairs.items())]
        code = [-1] * (wide * tall)
        for a, b in moves:
            if (a, b) not in known:
                known.add((a, b))
                near = abs(a - b) == 1
                code[b] = (3 if near else 1) + (1 if a < b else 0)
        got.append((lax.ppermute(block, ("ex", "ey"), moves), tuple(code)))
    return got


def paired(forcing, eigen_basis, eigen_values, coupling, inverse_blocks, slots, sides, partners):
    inner_nodes, rim_nodes = node_lists()
    share, nodes, elems = forcing.shape
    unknowns = inverse_blocks.shape[1]
    modes = lax.axis_size("mode")
    inner, rim = len(inner_nodes), len(rim_nodes)
    side = round(math.sqrt(nodes))
    lines = -(-(inner - SPAN // TILE) // (side - 2))
    raw_rows = lines * (side - 2)
    rest_rows = inner - raw_rows
    octets = share // TILE
    mates = [(i, i ^ 1) for i in range(modes)]
    across = [(i, i ^ CORES) for i in range(modes)]
    planes = jnp.transpose(forcing, (1, 0, 2))
    basis = ("smem", eigen_basis)
    raw_nodes = [int(node) for node in inner_nodes[:raw_rows]]
    rest_nodes = [int(node) for node in inner_nodes[raw_rows:]]

    own_raw = kernel_call(
        take_kernel,
        shape(lines, side - 2, share, elems),
        [("any", planes.reshape(side, side, share, elems))],
        "raw_rows",
        0.5,
        [pltpu.SemaphoreType.DMA],
    ).reshape(raw_rows, share, elems)
    planes, own_raw = lax.optimization_barrier((planes, own_raw))
    first = lax.ppermute(own_raw, "mode", across)
    mate_planes = lax.ppermute(planes, "mode", mates)
    send, keep = kernel_call(
        functools.partial(near_kernel, devices=modes, nodes=rest_nodes, rim_nodes=[int(node) for node in rim_nodes]),
        (shape(rest_rows + 1, share, elems), shape(rest_rows + 1, share, elems)),
        [("hbm", planes), mate_planes, ("hbm", slots)],
        "near_spectra",
        2.5,
    )
    received = lax.ppermute(send, "mode", across)
    tall = 2 * TILE
    lead, rest, lead_solve, rest_solve, pull, where = kernel_call(
        functools.partial(prepare_kernel, devices=modes),
        (
            shape(octets, tall * rim, raw_rows * TILE, dtype=bf16),
            shape(octets, tall * rim, rest_rows * TILE, dtype=bf16),
            shape(octets, tall * inner, raw_rows * TILE, dtype=bf16),
            shape(octets, tall * inner, rest_rows * TILE, dtype=bf16),
            shape(octets, tall * inner, rim * TILE, dtype=bf16),
            shape(rim * elems, unknowns, dtype=bf16),
        ),
        [basis, ("smem", eigen_values), ("hbm", coupling), ("hbm", slots), keep],
        "prepare",
        4.0,
        [pltpu.VMEM((share, -(-(inner + rim) // TILE) * TILE, inner + rim), f32)],
    )
    second = lax.ppermute(first, "mode", mates)
    coupled_raw, solved_raw, _ = kernel_call(
        functools.partial(far_kernel, devices=modes, nodes=raw_nodes),
        (shape(rim, share, elems), shape(inner, share, elems), shape(raw_rows, share, elems)),
        [("hbm", planes), mate_planes, first, second, lead, lead_solve],
        "far_spectra",
        1.0,
    )
    spectral, sums = kernel_call(
        residual_kernel,
        (shape(rest_rows, share, elems), shape(share, unknowns)),
        [("vmem", x) for x in (keep, received, coupled_raw, rest, where)],
        "residual",
        1.5,
    )
    got = exchanges(sums)
    solved = kernel_call(
        solved_kernel, shape(inner, share, elems), [solved_raw, spectral, rest_solve], "solved", 1.0
    )
    interior, interface = kernel_call(
        functools.partial(back_kernel, codes=[codes for _, codes in got]),
        (shape(inner, share, elems), shape(share, 1, unknowns)),
        [sums, *[block for block, _ in got], sides, partners, inverse_blocks, slots, pull, solved],
        "back_solve",
        2.0,
    )
    return (jnp.transpose(interior, (1, 0, 2)), interface)


def extended(block, sides, width):
    for axis, dim in sides:
        count = lax.axis_size(axis)
        forward = [(i, i + 1) for i in range(count - 1)]
        backward = [(target, source) for source, target in forward]
        low = lax.ppermute(
            lax.slice_in_dim(block, block.shape[dim] - width, None, axis=dim), axis, forward
        )
        high = lax.ppermute(lax.slice_in_dim(block, 0, width, axis=dim), axis, backward)
        block = jnp.concatenate([low, block, high], axis=dim)
    return block


def wave_numbers(row_ids, count):
    return jnp.where(row_ids == 1, count // 2, row_ids // 2)


def dft_table(count):
    row_ids = jnp.arange(count, dtype=jnp.int32)
    wave_ids = wave_numbers(row_ids, count)
    phase_ids = wave_ids[:, None] * row_ids[None, :] % count
    angles = 2.0 * math.pi / count * phase_ids.astype(jnp.float32)
    odd_rows = (row_ids % 2 == 1) & (row_ids != 1)
    scales = jnp.where(row_ids <= 1, math.sqrt(1.0 / count), math.sqrt(2.0 / count)).astype(
        jnp.float32
    )
    return jnp.where(odd_rows[:, None], jnp.sin(angles), jnp.cos(angles)) * scales[:, None]


def mode_shifts(row_ids, count):
    waves = wave_numbers(row_ids, count).astype(jnp.float32) * wave_unit
    return helm_base + waves * waves


def fast_solve(values, eigen_basis, eigen_values, shifts):
    kron_basis = jnp.kron(eigen_basis, eigen_basis)
    pair_sums = (eigen_values[:, None] + eigen_values[None, :]).reshape(-1)
    spectra = jnp.einsum("ji,rje->rie", kron_basis, values, precision=lax.Precision.HIGHEST)
    spectra = spectra / (pair_sums[None, :, None] + shifts[:, None, None])
    return jnp.einsum("ij,rje->rie", kron_basis, spectra, precision=lax.Precision.HIGHEST)


def general(forcing, eigen_basis, eigen_values, coupling, inverse_blocks, slots, sides, partners):
    inner_nodes, rim_nodes = node_lists()
    plane_dev = forcing.shape[0]
    elem_dev = forcing.shape[2]
    unknowns = inverse_blocks.shape[1]
    modes_axis = lax.axis_size("mode")
    plane_count = modes_axis * plane_dev
    table = dft_table(plane_count)
    row_ids = lax.axis_index("mode") * plane_dev + jnp.arange(plane_dev, dtype=jnp.int32)
    shifts = mode_shifts(row_ids, plane_count)
    onehot = (slots.reshape(-1)[:, None] == jnp.arange(unknowns, dtype=jnp.int32)[None, :]).astype(
        jnp.float32
    )
    inner_width = len(inner_nodes) * elem_dev
    rim_planes = forcing[:, rim_nodes, :].reshape(plane_dev, -1)
    condensed = jnp.dot(rim_planes, onehot, precision=lax.Precision.HIGHEST)
    payload = jnp.concatenate(
        [forcing[:, inner_nodes, :].reshape(plane_dev, -1), condensed], axis=1
    )
    total_width = payload.shape[1]
    sectioned = payload.reshape(plane_dev, modes_axis, total_width // modes_axis)
    spectra = jnp.einsum(
        "rp,pkc->rkc",
        table,
        lax.all_to_all(sectioned, "mode", split_axis=1, concat_axis=0, tiled=True),
        precision=lax.Precision.HIGHEST,
    )
    spectral = lax.all_to_all(spectra, "mode", split_axis=0, concat_axis=1, tiled=True).reshape(
        plane_dev, total_width
    )
    inner_part = spectral[:, :inner_width].reshape(plane_dev, len(inner_nodes), elem_dev)
    condensed_hat = spectral[:, inner_width:]
    solved = fast_solve(inner_part, eigen_basis, eigen_values, shifts)
    coupled = jnp.einsum("ji,rie->rje", coupling, solved, precision=lax.Precision.HIGHEST)
    local_sums = condensed_hat - jnp.dot(
        coupled.reshape(plane_dev, -1), onehot, precision=lax.Precision.HIGHEST
    )
    padded = extended(local_sums.reshape(1, 1, -1), (("ex", 0), ("ey", 1)), 1)
    neighbours = (
        padded[2, 1].reshape(plane_dev, unknowns),
        padded[0, 1].reshape(plane_dev, unknowns),
        padded[1, 2].reshape(plane_dev, unknowns),
        padded[1, 0].reshape(plane_dev, unknowns),
    )
    assembled = local_sums
    for side_code, neighbour in enumerate(neighbours):
        picked = jnp.take(neighbour, partners[0], axis=1)
        assembled = assembled + jnp.where(
            (sides[0] == side_code + 1)[None, :], picked, jnp.zeros_like(picked)
        )
    interface = jnp.einsum("rst,rt->rs", inverse_blocks, assembled, precision=lax.Precision.HIGHEST)
    boundary = jnp.dot(interface, onehot.T, precision=lax.Precision.HIGHEST).reshape(
        plane_dev, len(rim_nodes), elem_dev
    )
    lifted = jnp.einsum("ji,rje->rie", coupling, boundary, precision=lax.Precision.HIGHEST)
    interior = solved - fast_solve(lifted, eigen_basis, eigen_values, shifts)
    return (interior, interface[:, None, :])


def on_device(*args):
    modes = lax.axis_size("mode")
    if modes == CORES * CORES:
        return paired(*args)
    return general(*args)


def solution(mesh):
    placed = (
        P("mode", None, ("ex", "ey")),
        P(),
        P(),
        P(),
        P("mode", None, None),
        P(None, ("ex", "ey")),
        P(("ex", "ey"), None),
        P(("ex", "ey"), None),
    )
    return jax.shard_map(
        on_device,
        mesh=mesh,
        in_specs=placed,
        out_specs=(P("mode", None, ("ex", "ey")), P("mode", ("ex", "ey"), None)),
        check_vma=False,
    )
```

```python
import functools
import math

import jax
import jax.numpy as jnp
import numpy as np
from jax import lax
from jax.experimental import pallas as pl
from jax.experimental.pallas import tpu as pltpu
from jax.sharding import PartitionSpec as P

helm_base = 0.5
wave_unit = 1.0 / 64.0
f32, bf16 = jnp.float32, jnp.bfloat16
TILE = 8
CORES = 2
SPAN = 256
LIMIT = 12 * 2**20


def is_inner(node_id):
    return 1 <= node_id // 9 <= 7 and 1 <= node_id % 9 <= 7


def node_lists():
    inner_nodes = np.array([node_id for node_id in range(81) if is_inner(node_id)], dtype=np.int32)
    rim_nodes = np.array(
        [node_id for node_id in range(81) if not is_inner(node_id)], dtype=np.int32
    )
    return (inner_nodes, rim_nodes)


def split(values):
    high = values.astype(bf16)
    return high, (values - high.astype(f32)).astype(bf16)


def stack_split(values):
    return jnp.concatenate(split(values), axis=0)


def dot(left, right):
    return jnp.dot(left, right, preferred_element_type=f32)


def exact(left, right):
    return jnp.dot(left, right, preferred_element_type=f32, precision=lax.Precision.HIGHEST)


def dot_t(left, right):
    return lax.dot_general(left, right, (((1,), (1,)), ((), ())), preferred_element_type=f32)


def fold(values):
    half = values.shape[0] // 2
    return values[:half] + values[half:]


def dot3(left, high, low):
    return fold(dot(left, high)) + dot(left[: left.shape[0] // 2], low)


def iota(shape, dim):
    return lax.broadcasted_iota(jnp.int32, shape, dim)


def chosen(blocks, line):
    lanes = 128
    width = blocks[0].shape[1]
    out = [[] for _ in blocks]
    for start in range(0, line.shape[1], lanes):
        index = jnp.broadcast_to(line[:, start : start + lanes], (TILE, lanes))
        place = index & (lanes - 1)
        beyond = [index >= first for first in range(lanes, width, lanes)]
        for block, parts in zip(blocks, out):
            found = jnp.take_along_axis(block[:, :lanes], place, axis=1)
            for i, mask in enumerate(beyond):
                first = (i + 1) * lanes
                found = jnp.where(mask, jnp.take_along_axis(block[:, first : first + lanes], place, axis=1), found)
            parts.append(found)
    return [jnp.concatenate(parts, axis=1) for parts in out]


def member(line, unknowns):
    return jnp.where(iota((unknowns, line.shape[1]), 0) == line, 1.0, 0.0).astype(bf16)


def weighted(scalars, blocks):
    total = scalars[0] * blocks[0]
    for scalar, block in zip(scalars[1:], blocks[1:]):
        total = total + scalar * block
    return total


def kron_matrix(basis):
    size = basis.shape[0]
    count = size * size

    def digits(index):
        lead = jnp.zeros_like(index)
        for step in range(1, size):
            lead = lead + (index >= step * size).astype(jnp.int32)
        return lead, index - lead * size

    def spread(row_digit, col_digit):
        out = jnp.zeros((count, count), f32)
        for i in range(size):
            line = jnp.zeros((1, count), f32)
            for j in range(size):
                line = jnp.where(col_digit == j, basis[i, j], line)
            out = jnp.where(row_digit == i, line, out)
        return out

    (a, b), (c, d) = digits(iota((count, 1), 0)), digits(iota((1, count), 1))
    return spread(a, c) * spread(b, d)


def wave_of(row, count):
    return jnp.where(row == 1, count // 2, row // 2)


def dft_blocks(device, devices, share, rows_of, cols_of):
    count = devices * share
    tall, width = share * len(rows_of), share * len(cols_of)
    copies = SPAN // width

    def index_of(ids, offsets):
        part = ids // share
        owner = jnp.where(part == 0, device ^ offsets[0], 0)
        for i, offset in enumerate(offsets[1:]):
            owner = jnp.where(part == i + 1, device ^ offset, owner)
        return owner * share + ids % share

    row = index_of(iota((tall, SPAN), 0), rows_of)
    plane = index_of(iota((tall, SPAN), 1) % width, cols_of)
    angle = 2.0 * math.pi / count * (wave_of(row, count) * plane % count).astype(f32)
    odd = (row % 2 == 1) & (row != 1)
    scale = jnp.where(row <= 1, math.sqrt(1.0 / count), math.sqrt(2.0 / count))
    block = jnp.where(odd, jnp.sin(angle), jnp.cos(angle)) * scale
    full = jnp.concatenate([block] * copies, axis=0)
    same = iota(full.shape, 0) // tall == iota(full.shape, 1) // width
    return stack_split(jnp.where(same, full, 0.0))


def corner(left, rows, cols):
    height = left.shape[0] // 2
    if (rows, cols) == (height, left.shape[1]):
        return left
    return jnp.concatenate([left[:rows, :cols], left[height : height + rows, :cols]], axis=0)


def octet(block, part):
    rows, _, elems = block.shape
    return block[:, part * TILE : (part + 1) * TILE, :].reshape(rows * TILE, elems)


def take_kernel(nodes, out, ready):
    lines, side = out.shape[:2]
    move = pltpu.make_async_copy(nodes.at[1 : 1 + lines, 1 : 1 + side], out, ready)
    move.start()
    move.wait()


def prepare_kernel(
    basis, values, coupling, slots, planes, residual, lead, rest, pull, where, held, modes, ready, *, devices
):
    move = pltpu.make_async_copy(planes, held, ready)
    move.start()
    size = basis.shape[0]
    rim, inner = coupling.shape
    elems = slots.shape[1]
    octets = lead.shape[0]
    share = octets * TILE
    first = lead.shape[2]
    edge = inner * TILE
    kron = kron_matrix(basis)
    couple = exact(coupling[...], kron)
    left = stack_split(jnp.concatenate([kron, couple], axis=0))
    right = jnp.concatenate([kron, couple], axis=0).T
    total = right.shape[1]
    n = iota((inner, total), 0)
    sums = jnp.zeros(n.shape, f32)
    for c in range(size):
        sums = sums + jnp.where((n >= c * size) & (n < (c + 1) * size), values[c], 0.0)
        for d in range(size):
            sums = sums + jnp.where(n == c * size + d, values[d], 0.0)
    device = lax.axis_index("mode")
    for r in range(2 * share):
        owner = device ^ CORES if r < share else device
        wave = wave_of(owner * share + r % share, devices * share).astype(f32) * wave_unit
        modes[r, :total, :] = dot3(left, *split(right / (sums + (helm_base + wave * wave))))
    spread = jnp.where(iota((total, total * TILE), 0) == iota((total, total * TILE), 1) // TILE, 1.0, 0.0).astype(bf16)

    def widened(matrix, cols):
        out = []
        for half in split(matrix):
            full = dot(half, spread[:, :cols])
            same = iota(full.shape, 0) % TILE == iota(full.shape, 1) % TILE
            out.append(jnp.where(same, full, 0.0).astype(bf16))
        return out

    for part in range(2 * octets):
        block = jnp.transpose(modes[part * TILE : (part + 1) * TILE], (1, 0, 2))[:total]
        block = block.reshape(total * TILE, total)
        if part < octets:
            residual[part] = jnp.concatenate(widened(block[edge:], edge), axis=0)
            continue
        high, low = widened(block, total * TILE)

        def put(out, place, rows, cols):
            out[place] = jnp.concatenate([high[rows, cols], low[rows, cols]], axis=0)

        put(residual, part, slice(edge, None), slice(0, edge))
        put(lead, part - octets, slice(0, edge), slice(0, first))
        put(rest, part - octets, slice(0, edge), slice(first, edge))
        put(pull, part - octets, slice(0, edge), slice(edge, None))
    columns = slots[...].astype(f32).T
    ids = iota((elems, where.shape[1]), 1).astype(f32)
    for j in range(rim):
        where[j * elems : (j + 1) * elems, :] = jnp.where(ids == columns[:, j : j + 1], 1.0, 0.0).astype(bf16)
    move.wait()


def near_kernel(
    own, mate, where, table, sums_out, sums_own, send, keep, spectra, *, devices, inner_nodes, rim_nodes
):
    _, share, elems = own.shape
    pair = 2 * share
    inner, rim = len(inner_nodes), len(rim_nodes)
    raw_rows = inner - send.shape[0]
    left = dft_blocks(lax.axis_index("mode"), devices, share, (CORES, 0), (0, 1))
    group = left.shape[1] // pair
    base = 0
    for nodes in (inner_nodes, rim_nodes):
        for first in range(0, len(nodes), group):
            part = nodes[first : first + group]
            block = jnp.concatenate([ref[node] for node in part for ref in (own, mate)], axis=0)
            rows = block.shape[0]
            out = dot3(corner(left, rows, rows), *split(block)).reshape(len(part), pair, elems)
            spectra[base + first : base + first + len(part)] = out
        base += len(nodes)
    send[...] = spectra[raw_rows:inner, :share, :]
    keep[...] = spectra[:inner, share:, :]
    parts = []
    for part in range(pair // TILE):
        place = slice(part * TILE, (part + 1) * TILE)
        block = spectra[:inner, place, :].reshape(inner * TILE, elems)
        coupled = dot3(table[part], *split(block)).reshape(rim, TILE, elems)
        parts.append(spectra[inner:, place, :] - coupled)
    residual = jnp.concatenate(parts, axis=1)
    line = jnp.concatenate([stack_split(residual[j]) for j in range(rim)], axis=1)
    sums = fold(dot(line, where[...]))
    sums_out[...] = sums[:share]
    sums_own[...] = sums[share:]


def far_kernel(keep, first, second, lead, rest, solved, spectral, *, devices):
    rows, share, elems = first.shape
    inner = keep.shape[0]
    left = dft_blocks(lax.axis_index("mode"), devices, share, (0,), (CORES, CORES + 1))
    group = left.shape[1] // (2 * share)
    for start in range(0, rows, group):
        part = range(start, min(start + group, rows))
        block = jnp.concatenate([x for k in part for x in (first[k], second[k])], axis=0)
        out = dot3(corner(left, share * len(part), 2 * share * len(part)), *split(block))
        spectral[start : start + len(part)] = keep[start : start + len(part)] + out.reshape(-1, share, elems)
    for part in range(share // TILE):
        place = slice(part * TILE, (part + 1) * TILE)
        block = dot3(lead[part], *split(octet(spectral[...], part)))
        block = block + dot3(rest[part], *split(keep[rows:, place, :].reshape(-1, elems)))
        solved[:, place, :] = block.reshape(inner, TILE, elems)


def back_kernel(sums, *refs, codes):
    neighbours = len(codes)
    near = refs[:neighbours]
    sides, partners, inverse, slots, pull, solved, interior, interface = refs[neighbours:]
    share, unknowns = sums.shape
    inner, _, elems = interior.shape
    rim = slots.shape[0]
    group = lax.axis_index("ex") * lax.axis_size("ey") + lax.axis_index("ey")
    octets = [slice(start, start + TILE) for start in range(0, share, TILE)]
    assembled = [sums[place] for place in octets]
    for i in range(neighbours):
        code = jnp.int32(codes[i][0])
        for g, other in enumerate(codes[i][1:], 1):
            code = jnp.where(group == g, other, code)
        picked = chosen([near[i][place] for place in octets], partners[...])
        assembled = [part + jnp.where(sides[...] == code, new, 0.0) for part, new in zip(assembled, picked)]
    values = []
    for place, part in zip(octets, assembled):
        lines = []
        for r in range(TILE):
            line = jnp.sum(inverse[place.start + r] * part[r : r + 1, :], axis=1).reshape(1, unknowns)
            interface[place.start + r] = line
            lines.append(line)
        values.append(jnp.concatenate(lines, axis=0))
    boundary = [chosen(values, slots[j : j + 1, :]) for j in range(rim)]
    for part, place in enumerate(octets):
        block = jnp.concatenate([blocks[part] for blocks in boundary], axis=0)
        lifted = dot3(pull[part], *split(block)).reshape(inner, TILE, elems)
        interior[:, place, :] = solved[:, place, :] - lifted


def final_kernel(base, received, rest, interior):
    inner, share, elems = interior.shape
    for part in range(share // TILE):
        place = slice(part * TILE, (part + 1) * TILE)
        block = dot3(rest[part], *split(octet(received[...], part)))
        interior[:, place, :] = base[:, place, :] + block.reshape(inner, TILE, elems)


VMEM = pl.BlockSpec(memory_space=pltpu.VMEM)
ANY = pl.BlockSpec(memory_space=pl.ANY)
SMEM = pl.BlockSpec(memory_space=pltpu.SMEM)


def shape(*dims, dtype=f32):
    return jax.ShapeDtypeStruct(dims, dtype)


def kernel_call(body, outs, ins, name, micros, scratch=()):
    in_specs, arrays = [], []
    for item in ins:
        place, array = item if isinstance(item, tuple) else ("", item)
        in_specs.append({"smem": SMEM, "any": ANY}.get(place, VMEM))
        if place:
            array = pltpu.with_memory_space_constraint(array, pltpu.VMEM if place == "vmem" else pltpu.HBM)
        arrays.append(array)
    return pl.pallas_call(
        body,
        out_shape=outs,
        in_specs=in_specs,
        out_specs=(VMEM,) * len(outs) if isinstance(outs, tuple) else VMEM,
        scratch_shapes=scratch,
        compiler_params=pltpu.CompilerParams(vmem_limit_bytes=LIMIT),
        cost_estimate=pl.CostEstimate(flops=0, transcendentals=0, bytes_accessed=int(micros * 3e6)),
        name=name,
    )(*arrays)


def exchanges(block):
    wide, tall = lax.axis_size("ex"), lax.axis_size("ey")
    group = lambda x, y: x * tall + y
    rounds = []
    for first in range(min(2, tall - 1)):
        pairs = {group(x, y): group(x, y + 1) for x in range(wide) for y in range(first, tall - 1, 2)}
        rounds.append(pairs)
    if len(rounds) == 2:
        busy = set(rounds[1]) | set(rounds[1].values())
        for y in range(tall):
            for x in range(0, wide - 1, 2):
                if not {group(x, y), group(x + 1, y)} & busy:
                    rounds[1][group(x, y)] = group(x + 1, y)
    for first in range(min(2, wide - 1)):
        rounds.append({group(x, y): group(x + 1, y) for x in range(first, wide - 1, 2) for y in range(tall)})
    got, known = [], set()
    for pairs in rounds:
        moves = [*pairs.items(), *((b, a) for a, b in pairs.items())]
        code = [-1] * (wide * tall)
        for a, b in moves:
            if (a, b) not in known:
                known.add((a, b))
                near = abs(a - b) == 1
                code[b] = (3 if near else 1) + (1 if a < b else 0)
        got.append((lax.ppermute(block, ("ex", "ey"), moves), tuple(code)))
    return got


def paired(forcing, eigen_basis, eigen_values, coupling, inverse_blocks, slots, sides, partners):
    inner_nodes, rim_nodes = node_lists()
    share, nodes, elems = forcing.shape
    unknowns = inverse_blocks.shape[1]
    modes = lax.axis_size("mode")
    inner, rim = len(inner_nodes), len(rim_nodes)
    side = round(math.sqrt(nodes))
    lines = -(-(inner - SPAN // TILE) // (side - 2))
    raw_rows = lines * (side - 2)
    rest_rows = inner - raw_rows
    octets = share // TILE
    mates = [(i, i ^ 1) for i in range(modes)]
    across = [(i, i ^ CORES) for i in range(modes)]
    planes = jnp.transpose(forcing, (1, 0, 2))
    basis = ("smem", eigen_basis)
    own_raw = kernel_call(
        take_kernel,
        shape(lines, side - 2, share, elems),
        [("any", planes.reshape(side, side, share, elems))],
        "raw_rows",
        0.5,
        [pltpu.SemaphoreType.DMA],
    ).reshape(raw_rows, share, elems)
    planes, own_raw = lax.optimization_barrier((planes, own_raw))
    first = lax.ppermute(own_raw, "mode", across)
    mate_planes = lax.ppermute(planes, "mode", mates)
    tall = 2 * TILE
    table, lead, rest, pull, where, own_planes = kernel_call(
        functools.partial(prepare_kernel, devices=modes),
        (
            shape(2 * octets, tall * rim, inner * TILE, dtype=bf16),
            shape(octets, tall * inner, raw_rows * TILE, dtype=bf16),
            shape(octets, tall * inner, rest_rows * TILE, dtype=bf16),
            shape(octets, tall * inner, rim * TILE, dtype=bf16),
            shape(rim * elems, unknowns, dtype=bf16),
            shape(*planes.shape),
        ),
        [basis, ("smem", eigen_values), ("hbm", coupling), ("hbm", slots), ("any", planes)],
        "prepare",
        4.0,
        [
            pltpu.VMEM((2 * share, -(-(inner + rim) // TILE) * TILE, inner + rim), f32),
            pltpu.SemaphoreType.DMA,
        ],
    )
    sums_out, sums_own, send, keep = kernel_call(
        functools.partial(
            near_kernel,
            devices=modes,
            inner_nodes=[int(node) for node in inner_nodes],
            rim_nodes=[int(node) for node in rim_nodes],
        ),
        (
            shape(share, unknowns),
            shape(share, unknowns),
            shape(rest_rows, share, elems),
            shape(inner, share, elems),
        ),
        [own_planes, mate_planes, where, table],
        "near_spectra",
        3.0,
        [pltpu.VMEM((nodes, 2 * share, elems), f32)],
    )
    sums_in, send = lax.optimization_barrier((lax.ppermute(sums_out, "mode", across), send))
    sums = sums_own + sums_in
    received = lax.ppermute(send, "mode", across)
    second = lax.ppermute(first, "mode", mates)
    solved = kernel_call(
        functools.partial(far_kernel, devices=modes),
        shape(inner, share, elems),
        [keep, first, second, lead, rest],
        "far_spectra",
        1.5,
        [pltpu.VMEM((raw_rows, share, elems), f32)],
    )
    got = exchanges(sums)
    base, interface = kernel_call(
        functools.partial(back_kernel, codes=[codes for _, codes in got]),
        (shape(inner, share, elems), shape(share, 1, unknowns)),
        [sums, *[block for block, _ in got], sides, partners, inverse_blocks, slots, pull, solved],
        "back_solve",
        2.0,
    )
    interior = kernel_call(
        final_kernel, shape(inner, share, elems), [base, ("vmem", received), rest], "interior_solve", 1.0
    )
    return (jnp.transpose(interior, (1, 0, 2)), interface)


def extended(block, sides, width):
    for axis, dim in sides:
        count = lax.axis_size(axis)
        forward = [(i, i + 1) for i in range(count - 1)]
        backward = [(target, source) for source, target in forward]
        low = lax.ppermute(
            lax.slice_in_dim(block, block.shape[dim] - width, None, axis=dim), axis, forward
        )
        high = lax.ppermute(lax.slice_in_dim(block, 0, width, axis=dim), axis, backward)
        block = jnp.concatenate([low, block, high], axis=dim)
    return block


def wave_numbers(row_ids, count):
    return jnp.where(row_ids == 1, count // 2, row_ids // 2)


def dft_table(count):
    row_ids = jnp.arange(count, dtype=jnp.int32)
    wave_ids = wave_numbers(row_ids, count)
    phase_ids = wave_ids[:, None] * row_ids[None, :] % count
    angles = 2.0 * math.pi / count * phase_ids.astype(jnp.float32)
    odd_rows = (row_ids % 2 == 1) & (row_ids != 1)
    scales = jnp.where(row_ids <= 1, math.sqrt(1.0 / count), math.sqrt(2.0 / count)).astype(
        jnp.float32
    )
    return jnp.where(odd_rows[:, None], jnp.sin(angles), jnp.cos(angles)) * scales[:, None]


def mode_shifts(row_ids, count):
    waves = wave_numbers(row_ids, count).astype(jnp.float32) * wave_unit
    return helm_base + waves * waves


def fast_solve(values, eigen_basis, eigen_values, shifts):
    kron_basis = jnp.kron(eigen_basis, eigen_basis)
    pair_sums = (eigen_values[:, None] + eigen_values[None, :]).reshape(-1)
    spectra = jnp.einsum("ji,rje->rie", kron_basis, values, precision=lax.Precision.HIGHEST)
    spectra = spectra / (pair_sums[None, :, None] + shifts[:, None, None])
    return jnp.einsum("ij,rje->rie", kron_basis, spectra, precision=lax.Precision.HIGHEST)


def general(forcing, eigen_basis, eigen_values, coupling, inverse_blocks, slots, sides, partners):
    inner_nodes, rim_nodes = node_lists()
    plane_dev = forcing.shape[0]
    elem_dev = forcing.shape[2]
    unknowns = inverse_blocks.shape[1]
    modes_axis = lax.axis_size("mode")
    plane_count = modes_axis * plane_dev
    table = dft_table(plane_count)
    row_ids = lax.axis_index("mode") * plane_dev + jnp.arange(plane_dev, dtype=jnp.int32)
    shifts = mode_shifts(row_ids, plane_count)
    onehot = (slots.reshape(-1)[:, None] == jnp.arange(unknowns, dtype=jnp.int32)[None, :]).astype(
        jnp.float32
    )
    inner_width = len(inner_nodes) * elem_dev
    rim_planes = forcing[:, rim_nodes, :].reshape(plane_dev, -1)
    condensed = jnp.dot(rim_planes, onehot, precision=lax.Precision.HIGHEST)
    payload = jnp.concatenate(
        [forcing[:, inner_nodes, :].reshape(plane_dev, -1), condensed], axis=1
    )
    total_width = payload.shape[1]
    sectioned = payload.reshape(plane_dev, modes_axis, total_width // modes_axis)
    spectra = jnp.einsum(
        "rp,pkc->rkc",
        table,
        lax.all_to_all(sectioned, "mode", split_axis=1, concat_axis=0, tiled=True),
        precision=lax.Precision.HIGHEST,
    )
    spectral = lax.all_to_all(spectra, "mode", split_axis=0, concat_axis=1, tiled=True).reshape(
        plane_dev, total_width
    )
    inner_part = spectral[:, :inner_width].reshape(plane_dev, len(inner_nodes), elem_dev)
    condensed_hat = spectral[:, inner_width:]
    solved = fast_solve(inner_part, eigen_basis, eigen_values, shifts)
    coupled = jnp.einsum("ji,rie->rje", coupling, solved, precision=lax.Precision.HIGHEST)
    local_sums = condensed_hat - jnp.dot(
        coupled.reshape(plane_dev, -1), onehot, precision=lax.Precision.HIGHEST
    )
    padded = extended(local_sums.reshape(1, 1, -1), (("ex", 0), ("ey", 1)), 1)
    neighbours = (
        padded[2, 1].reshape(plane_dev, unknowns),
        padded[0, 1].reshape(plane_dev, unknowns),
        padded[1, 2].reshape(plane_dev, unknowns),
        padded[1, 0].reshape(plane_dev, unknowns),
    )
    assembled = local_sums
    for side_code, neighbour in enumerate(neighbours):
        picked = jnp.take(neighbour, partners[0], axis=1)
        assembled = assembled + jnp.where(
            (sides[0] == side_code + 1)[None, :], picked, jnp.zeros_like(picked)
        )
    interface = jnp.einsum("rst,rt->rs", inverse_blocks, assembled, precision=lax.Precision.HIGHEST)
    boundary = jnp.dot(interface, onehot.T, precision=lax.Precision.HIGHEST).reshape(
        plane_dev, len(rim_nodes), elem_dev
    )
    lifted = jnp.einsum("ji,rje->rie", coupling, boundary, precision=lax.Precision.HIGHEST)
    interior = solved - fast_solve(lifted, eigen_basis, eigen_values, shifts)
    return (interior, interface[:, None, :])


def on_device(*args):
    modes = lax.axis_size("mode")
    if modes == CORES * CORES:
        return paired(*args)
    return general(*args)


def solution(mesh):
    placed = (
        P("mode", None, ("ex", "ey")),
        P(),
        P(),
        P(),
        P("mode", None, None),
        P(None, ("ex", "ey")),
        P(("ex", "ey"), None),
        P(("ex", "ey"), None),
    )
    return jax.shard_map(
        on_device,
        mesh=mesh,
        in_specs=placed,
        out_specs=(P("mode", None, ("ex", "ey")), P("mode", ("ex", "ey"), None)),
        check_vma=False,
    )
```

```python
import functools
import math

import jax
import jax.numpy as jnp
import numpy as np
from jax import lax
from jax.experimental import pallas as pl
from jax.experimental.pallas import tpu as pltpu
from jax.sharding import PartitionSpec as P

helm_base = 0.5
wave_unit = 1.0 / 64.0
f32, bf16 = jnp.float32, jnp.bfloat16
TILE = 8
CORES = 2
SPAN = 256
RAW_SHARE = 51
LIMIT = 12 * 2**20


def is_inner(node_id):
    return 1 <= node_id // 9 <= 7 and 1 <= node_id % 9 <= 7


def node_lists():
    inner_nodes = np.array([node_id for node_id in range(81) if is_inner(node_id)], dtype=np.int32)
    rim_nodes = np.array(
        [node_id for node_id in range(81) if not is_inner(node_id)], dtype=np.int32
    )
    return (inner_nodes, rim_nodes)


def split(values):
    high = values.astype(bf16)
    return high, (values - high.astype(f32)).astype(bf16)


def stack_split(values):
    return jnp.concatenate(split(values), axis=0)


def dot(left, right):
    return jnp.dot(left, right, preferred_element_type=f32)


def exact(left, right):
    return jnp.dot(left, right, preferred_element_type=f32, precision=lax.Precision.HIGHEST)


def dot_t(left, right):
    return lax.dot_general(left, right, (((1,), (1,)), ((), ())), preferred_element_type=f32)


def fold(values):
    half = values.shape[0] // 2
    return values[:half] + values[half:]


def dot3(left, high, low):
    return fold(dot(left, high)) + dot(left[: left.shape[0] // 2], low)


def iota(shape, dim):
    return lax.broadcasted_iota(jnp.int32, shape, dim)


def chosen(blocks, line):
    lanes = 128
    width = blocks[0].shape[1]
    out = [[] for _ in blocks]
    for start in range(0, line.shape[1], lanes):
        index = jnp.broadcast_to(line[:, start : start + lanes], (TILE, lanes))
        place = index & (lanes - 1)
        beyond = [index >= first for first in range(lanes, width, lanes)]
        for block, parts in zip(blocks, out):
            found = jnp.take_along_axis(block[:, :lanes], place, axis=1)
            for i, mask in enumerate(beyond):
                first = (i + 1) * lanes
                found = jnp.where(mask, jnp.take_along_axis(block[:, first : first + lanes], place, axis=1), found)
            parts.append(found)
    return [jnp.concatenate(parts, axis=1) for parts in out]


def member(line, unknowns):
    return jnp.where(iota((unknowns, line.shape[1]), 0) == line, 1.0, 0.0).astype(bf16)


def weighted(scalars, blocks):
    total = scalars[0] * blocks[0]
    for scalar, block in zip(scalars[1:], blocks[1:]):
        total = total + scalar * block
    return total


def kron_matrix(basis):
    size = basis.shape[0]
    count = size * size

    def digits(index):
        lead = jnp.zeros_like(index)
        for step in range(1, size):
            lead = lead + (index >= step * size).astype(jnp.int32)
        return lead, index - lead * size

    def spread(row_digit, col_digit):
        out = jnp.zeros((count, count), f32)
        for i in range(size):
            line = jnp.zeros((1, count), f32)
            for j in range(size):
                line = jnp.where(col_digit == j, basis[i, j], line)
            out = jnp.where(row_digit == i, line, out)
        return out

    (a, b), (c, d) = digits(iota((count, 1), 0)), digits(iota((1, count), 1))
    return spread(a, c) * spread(b, d)


def wave_of(row, count):
    return jnp.where(row == 1, count // 2, row // 2)


def dft_blocks(device, devices, share, rows_of, cols_of):
    count = devices * share
    tall, width = share * len(rows_of), share * len(cols_of)
    copies = SPAN // width

    def index_of(ids, offsets):
        part = ids // share
        owner = jnp.where(part == 0, device ^ offsets[0], 0)
        for i, offset in enumerate(offsets[1:]):
            owner = jnp.where(part == i + 1, device ^ offset, owner)
        return owner * share + ids % share

    row = index_of(iota((tall, SPAN), 0), rows_of)
    plane = index_of(iota((tall, SPAN), 1) % width, cols_of)
    angle = 2.0 * math.pi / count * (wave_of(row, count) * plane % count).astype(f32)
    odd = (row % 2 == 1) & (row != 1)
    scale = jnp.where(row <= 1, math.sqrt(1.0 / count), math.sqrt(2.0 / count))
    block = jnp.where(odd, jnp.sin(angle), jnp.cos(angle)) * scale
    full = jnp.concatenate([block] * copies, axis=0)
    same = iota(full.shape, 0) // tall == iota(full.shape, 1) // width
    return stack_split(jnp.where(same, full, 0.0))


def corner(left, rows, cols):
    height = left.shape[0] // 2
    if (rows, cols) == (height, left.shape[1]):
        return left
    return jnp.concatenate([left[:rows, :cols], left[height : height + rows, :cols]], axis=0)


def octet(block, part):
    rows, _, elems = block.shape
    return block[:, part * TILE : (part + 1) * TILE, :].reshape(rows * TILE, elems)


def take_kernel(nodes, *refs, wanted):
    count = (len(refs) - 2) // 2
    sources, out, copies, ready = refs[:count], refs[count], refs[count + 1 : -1], refs[-1]
    moves = [pltpu.make_async_copy(source, copy, ready.at[i]) for i, (source, copy) in enumerate(zip(sources, copies))]
    first = 0
    runs = []
    for node, length in wanted:
        run = pltpu.make_async_copy(nodes.at[node : node + length], out.at[first : first + length], ready.at[count + len(runs)])
        runs.append(run)
        first += length
    for move in runs + moves:
        move.start()
    for move in runs + moves:
        move.wait()


def per_mode(left, right, values, owner, share, devices, modes):
    size = values.shape[0]
    n = iota(right.shape, 0)
    sums = jnp.zeros(n.shape, f32)
    for c in range(size):
        sums = sums + jnp.where((n >= c * size) & (n < (c + 1) * size), values[c], 0.0)
        for d in range(size):
            sums = sums + jnp.where(n == c * size + d, values[d], 0.0)
    rows = left.shape[0] // 2
    for r in range(share):
        wave = wave_of(owner * share + r, devices * share).astype(f32) * wave_unit
        modes[r, :rows, :] = dot3(left, *split(right / (sums + (helm_base + wave * wave))))


def widened(modes, part, rows, cols):
    block = jnp.transpose(modes[part * TILE : (part + 1) * TILE], (1, 0, 2))[:rows, :, :cols]
    spread = jnp.where(iota((cols, cols * TILE), 0) == iota((cols, cols * TILE), 1) // TILE, 1.0, 0.0).astype(bf16)
    same = (iota((TILE, cols * TILE), 0) == iota((TILE, cols * TILE), 1) % TILE)[None]
    out = []
    for half in split(block.reshape(rows * TILE, cols)):
        full = dot(half, spread).reshape(rows, TILE, cols * TILE)
        out.append(jnp.where(same, full, 0.0).reshape(rows * TILE, cols * TILE).astype(bf16))
    return out


def tables_kernel(
    basis, values, coupling, planes, slots, table, lead, rest, pull, where, held, modes, ready, *, devices
):
    move = pltpu.make_async_copy(planes, held, ready)
    move.start()
    rim, inner = coupling.shape
    elems = slots.shape[1]
    octets, _, first = lead.shape
    edge = inner * TILE
    columns = slots[...].astype(f32).T
    ids = iota((elems, where.shape[1]), 1).astype(f32)
    for j in range(rim):
        where[j * elems : (j + 1) * elems, :] = jnp.where(ids == columns[:, j : j + 1], 1.0, 0.0).astype(bf16)
    kron = kron_matrix(basis)
    couple = exact(coupling[...], kron)
    device = lax.axis_index("mode")
    share = octets * TILE
    both = jnp.concatenate([couple, kron], axis=0)
    right = jnp.concatenate([kron, couple], axis=0).T
    per_mode(stack_split(couple), right, values, device ^ CORES, share, devices, modes)
    for part in range(octets):
        table[part] = jnp.concatenate(widened(modes, part, rim, inner), axis=0)
    per_mode(stack_split(both), right, values, device, share, devices, modes)
    top = rim * TILE
    for part in range(octets):
        halves = widened(modes, part, rim + inner, rim + inner)

        def put(out, place, rows, cols):
            out[place] = jnp.concatenate([half[rows, cols] for half in halves], axis=0)

        put(table, octets + part, slice(0, top), slice(0, edge))
        put(lead, part, slice(top, None), slice(0, first))
        put(rest, part, slice(top, None), slice(first, edge))
        put(pull, part, slice(top, None), slice(edge, None))
    move.wait()


def near_kernel(
    own, mate, where, table, sums_out, sums_own, send, keep, spectra, *, devices, inner_nodes, rim_nodes
):
    _, share, elems = own.shape
    pair = 2 * share
    inner, rim = len(inner_nodes), len(rim_nodes)
    raw_rows = inner - send.shape[0]
    left = dft_blocks(lax.axis_index("mode"), devices, share, (CORES, 0), (0, 1))
    group = left.shape[1] // pair
    base = 0
    for nodes in (inner_nodes, rim_nodes):
        for first in range(0, len(nodes), group):
            part = nodes[first : first + group]
            block = jnp.concatenate([ref[node] for node in part for ref in (own, mate)], axis=0)
            rows = block.shape[0]
            out = dot3(corner(left, rows, rows), *split(block)).reshape(len(part), pair, elems)
            spectra[base + first : base + first + len(part)] = out
        base += len(nodes)
    send[...] = spectra[raw_rows:inner, :share, :]
    keep[...] = spectra[:inner, share:, :]
    parts = []
    for part in range(pair // TILE):
        place = slice(part * TILE, (part + 1) * TILE)
        block = spectra[:inner, place, :].reshape(inner * TILE, elems)
        coupled = dot3(table[part], *split(block)).reshape(rim, TILE, elems)
        parts.append(spectra[inner:, place, :] - coupled)
    residual = jnp.concatenate(parts, axis=1)
    line = jnp.concatenate([stack_split(residual[j]) for j in range(rim)], axis=1)
    sums = fold(dot(line, where[...]))
    sums_out[...] = sums[:share]
    sums_own[...] = sums[share:]


def far_kernel(keep, first, second, lead, rest, solved, spectral, *, devices):
    rows, share, elems = first.shape
    inner = keep.shape[0]
    left = dft_blocks(lax.axis_index("mode"), devices, share, (0,), (CORES, CORES + 1))
    group = left.shape[1] // (2 * share)
    for start in range(0, rows, group):
        part = range(start, min(start + group, rows))
        block = jnp.concatenate([x for k in part for x in (first[k], second[k])], axis=0)
        out = dot3(corner(left, share * len(part), 2 * share * len(part)), *split(block))
        spectral[start : start + len(part)] = keep[start : start + len(part)] + out.reshape(-1, share, elems)
    for part in range(share // TILE):
        place = slice(part * TILE, (part + 1) * TILE)
        block = dot3(lead[part], *split(octet(spectral[...], part)))
        block = block + dot3(rest[part], *split(keep[rows:, place, :].reshape(-1, elems)))
        solved[:, place, :] = block.reshape(inner, TILE, elems)


def back_kernel(sums, *refs, codes):
    neighbours = len(codes)
    near = refs[:neighbours]
    sides, partners, inverse, slots, pull, solved, interior, interface = refs[neighbours:]
    share, unknowns = sums.shape
    inner, _, elems = interior.shape
    rim = slots.shape[0]
    group = lax.axis_index("ex") * lax.axis_size("ey") + lax.axis_index("ey")
    octets = [slice(start, start + TILE) for start in range(0, share, TILE)]
    assembled = [sums[place] for place in octets]
    for i in range(neighbours):
        code = jnp.int32(codes[i][0])
        for g, other in enumerate(codes[i][1:], 1):
            code = jnp.where(group == g, other, code)
        picked = chosen([near[i][place] for place in octets], partners[...])
        assembled = [part + jnp.where(sides[...] == code, new, 0.0) for part, new in zip(assembled, picked)]
    values = []
    for place, part in zip(octets, assembled):
        lines = []
        for r in range(TILE):
            line = jnp.sum(inverse[place.start + r] * part[r : r + 1, :], axis=1).reshape(1, unknowns)
            interface[place.start + r] = line
            lines.append(line)
        values.append(jnp.concatenate(lines, axis=0))
    boundary = [chosen(values, slots[j : j + 1, :]) for j in range(rim)]
    for part, place in enumerate(octets):
        block = jnp.concatenate([blocks[part] for blocks in boundary], axis=0)
        lifted = dot3(pull[part], *split(block)).reshape(inner, TILE, elems)
        interior[:, place, :] = solved[:, place, :] - lifted


def final_kernel(base, received, rest, interior):
    inner, share, elems = interior.shape
    for part in range(share // TILE):
        place = slice(part * TILE, (part + 1) * TILE)
        block = dot3(rest[part], *split(octet(received[...], part)))
        interior[:, place, :] = base[:, place, :] + block.reshape(inner, TILE, elems)


VMEM = pl.BlockSpec(memory_space=pltpu.VMEM)
ANY = pl.BlockSpec(memory_space=pl.ANY)
SMEM = pl.BlockSpec(memory_space=pltpu.SMEM)


def shape(*dims, dtype=f32):
    return jax.ShapeDtypeStruct(dims, dtype)


def kernel_call(body, outs, ins, name, micros, scratch=()):
    in_specs, arrays = [], []
    for item in ins:
        place, array = item if isinstance(item, tuple) else ("", item)
        in_specs.append({"smem": SMEM, "any": ANY}.get(place, VMEM))
        if place in ("any", "hbm", "vmem"):
            array = pltpu.with_memory_space_constraint(array, pltpu.VMEM if place == "vmem" else pltpu.HBM)
        arrays.append(array)
    return pl.pallas_call(
        body,
        out_shape=outs,
        in_specs=in_specs,
        out_specs=(VMEM,) * len(outs) if isinstance(outs, tuple) else VMEM,
        scratch_shapes=scratch,
        compiler_params=pltpu.CompilerParams(vmem_limit_bytes=LIMIT),
        cost_estimate=pl.CostEstimate(flops=0, transcendentals=0, bytes_accessed=int(micros * 3e6)),
        name=name,
    )(*arrays)


def exchanges(block):
    wide, tall = lax.axis_size("ex"), lax.axis_size("ey")
    group = lambda x, y: x * tall + y
    rounds = []
    for first in range(min(2, tall - 1)):
        pairs = {group(x, y): group(x, y + 1) for x in range(wide) for y in range(first, tall - 1, 2)}
        rounds.append(pairs)
    if len(rounds) == 2:
        busy = set(rounds[1]) | set(rounds[1].values())
        for y in range(tall):
            for x in range(0, wide - 1, 2):
                if not {group(x, y), group(x + 1, y)} & busy:
                    rounds[1][group(x, y)] = group(x + 1, y)
    for first in range(min(2, wide - 1)):
        rounds.append({group(x, y): group(x + 1, y) for x in range(first, wide - 1, 2) for y in range(tall)})
    got, known = [], set()
    for pairs in rounds:
        moves = [*pairs.items(), *((b, a) for a, b in pairs.items())]
        code = [-1] * (wide * tall)
        for a, b in moves:
            if (a, b) not in known:
                known.add((a, b))
                near = abs(a - b) == 1
                code[b] = (3 if near else 1) + (1 if a < b else 0)
        got.append((lax.ppermute(block, ("ex", "ey"), moves), tuple(code)))
    return got


def paired(forcing, eigen_basis, eigen_values, coupling, inverse_blocks, slots, sides, partners):
    inner_nodes, rim_nodes = node_lists()
    share, nodes, elems = forcing.shape
    unknowns = inverse_blocks.shape[1]
    modes = lax.axis_size("mode")
    inner, rim = len(inner_nodes), len(rim_nodes)
    side = round(math.sqrt(nodes))
    raw_rows = inner * RAW_SHARE // 100
    line = side - 2
    runs = [
        (int(inner_nodes[first]), min(line, raw_rows - first)) for first in range(0, raw_rows, line)
    ]
    rest_rows = inner - raw_rows
    octets = share // TILE
    mates = [(i, i ^ 1) for i in range(modes)]
    across = [(i, i ^ CORES) for i in range(modes)]
    planes = jnp.transpose(forcing, (1, 0, 2))
    small = [eigen_basis, eigen_values, coupling, slots]
    own_raw, *small = kernel_call(
        functools.partial(take_kernel, wanted=runs),
        (shape(raw_rows, share, elems), *[jax.ShapeDtypeStruct(x.shape, x.dtype) for x in small]),
        [("any", planes), *[("any", x) for x in small]],
        "raw_rows",
        0.5,
        [pltpu.SemaphoreType.DMA((len(small) + len(runs),))],
    )
    eigen_basis, eigen_values, coupling, slots_held = small
    basis, values = ("smem", eigen_basis), ("smem", eigen_values)
    planes, own_raw = lax.optimization_barrier((planes, own_raw))
    first = lax.ppermute(own_raw, "mode", across)
    mate_planes = lax.ppermute(planes, "mode", mates)
    tall = 2 * TILE
    table, lead, rest, pull, where, own_planes = kernel_call(
        functools.partial(tables_kernel, devices=modes),
        (
            shape(2 * octets, tall * rim, inner * TILE, dtype=bf16),
            shape(octets, tall * inner, raw_rows * TILE, dtype=bf16),
            shape(octets, tall * inner, rest_rows * TILE, dtype=bf16),
            shape(octets, tall * inner, rim * TILE, dtype=bf16),
            shape(rim * elems, unknowns, dtype=bf16),
            shape(*planes.shape),
        ),
        [basis, values, coupling, ("any", planes), slots_held],
        "tables",
        2.5,
        [pltpu.VMEM((share, -(-(inner + rim) // TILE) * TILE, inner + rim), f32), pltpu.SemaphoreType.DMA],
    )
    sums_out, sums_own, send, keep = kernel_call(
        functools.partial(
            near_kernel,
            devices=modes,
            inner_nodes=[int(node) for node in inner_nodes],
            rim_nodes=[int(node) for node in rim_nodes],
        ),
        (
            shape(share, unknowns),
            shape(share, unknowns),
            shape(rest_rows, share, elems),
            shape(inner, share, elems),
        ),
        [own_planes, mate_planes, where, table],
        "near_spectra",
        3.0,
        [pltpu.VMEM((nodes, 2 * share, elems), f32)],
    )
    sums_in, send = lax.optimization_barrier((lax.ppermute(sums_out, "mode", across), send))
    sums = sums_own + sums_in
    received = lax.ppermute(send, "mode", across)
    second = lax.ppermute(first, "mode", mates)
    solved = kernel_call(
        functools.partial(far_kernel, devices=modes),
        shape(inner, share, elems),
        [keep, first, second, lead, rest],
        "far_spectra",
        1.5,
        [pltpu.VMEM((raw_rows, share, elems), f32)],
    )
    got = exchanges(sums)
    base, interface = kernel_call(
        functools.partial(back_kernel, codes=[codes for _, codes in got]),
        (shape(inner, share, elems), shape(share, 1, unknowns)),
        [sums, *[block for block, _ in got], sides, partners, inverse_blocks, slots, pull, solved],
        "back_solve",
        2.0,
    )
    interior = kernel_call(
        final_kernel, shape(inner, share, elems), [base, ("vmem", received), rest], "interior_solve", 1.0
    )
    return (jnp.transpose(interior, (1, 0, 2)), interface)


def extended(block, sides, width):
    for axis, dim in sides:
        count = lax.axis_size(axis)
        forward = [(i, i + 1) for i in range(count - 1)]
        backward = [(target, source) for source, target in forward]
        low = lax.ppermute(
            lax.slice_in_dim(block, block.shape[dim] - width, None, axis=dim), axis, forward
        )
        high = lax.ppermute(lax.slice_in_dim(block, 0, width, axis=dim), axis, backward)
        block = jnp.concatenate([low, block, high], axis=dim)
    return block


def wave_numbers(row_ids, count):
    return jnp.where(row_ids == 1, count // 2, row_ids // 2)


def dft_table(count):
    row_ids = jnp.arange(count, dtype=jnp.int32)
    wave_ids = wave_numbers(row_ids, count)
    phase_ids = wave_ids[:, None] * row_ids[None, :] % count
    angles = 2.0 * math.pi / count * phase_ids.astype(jnp.float32)
    odd_rows = (row_ids % 2 == 1) & (row_ids != 1)
    scales = jnp.where(row_ids <= 1, math.sqrt(1.0 / count), math.sqrt(2.0 / count)).astype(
        jnp.float32
    )
    return jnp.where(odd_rows[:, None], jnp.sin(angles), jnp.cos(angles)) * scales[:, None]


def mode_shifts(row_ids, count):
    waves = wave_numbers(row_ids, count).astype(jnp.float32) * wave_unit
    return helm_base + waves * waves


def fast_solve(values, eigen_basis, eigen_values, shifts):
    kron_basis = jnp.kron(eigen_basis, eigen_basis)
    pair_sums = (eigen_values[:, None] + eigen_values[None, :]).reshape(-1)
    spectra = jnp.einsum("ji,rje->rie", kron_basis, values, precision=lax.Precision.HIGHEST)
    spectra = spectra / (pair_sums[None, :, None] + shifts[:, None, None])
    return jnp.einsum("ij,rje->rie", kron_basis, spectra, precision=lax.Precision.HIGHEST)


def general(forcing, eigen_basis, eigen_values, coupling, inverse_blocks, slots, sides, partners):
    inner_nodes, rim_nodes = node_lists()
    plane_dev = forcing.shape[0]
    elem_dev = forcing.shape[2]
    unknowns = inverse_blocks.shape[1]
    modes_axis = lax.axis_size("mode")
    plane_count = modes_axis * plane_dev
    table = dft_table(plane_count)
    row_ids = lax.axis_index("mode") * plane_dev + jnp.arange(plane_dev, dtype=jnp.int32)
    shifts = mode_shifts(row_ids, plane_count)
    onehot = (slots.reshape(-1)[:, None] == jnp.arange(unknowns, dtype=jnp.int32)[None, :]).astype(
        jnp.float32
    )
    inner_width = len(inner_nodes) * elem_dev
    rim_planes = forcing[:, rim_nodes, :].reshape(plane_dev, -1)
    condensed = jnp.dot(rim_planes, onehot, precision=lax.Precision.HIGHEST)
    payload = jnp.concatenate(
        [forcing[:, inner_nodes, :].reshape(plane_dev, -1), condensed], axis=1
    )
    total_width = payload.shape[1]
    sectioned = payload.reshape(plane_dev, modes_axis, total_width // modes_axis)
    spectra = jnp.einsum(
        "rp,pkc->rkc",
        table,
        lax.all_to_all(sectioned, "mode", split_axis=1, concat_axis=0, tiled=True),
        precision=lax.Precision.HIGHEST,
    )
    spectral = lax.all_to_all(spectra, "mode", split_axis=0, concat_axis=1, tiled=True).reshape(
        plane_dev, total_width
    )
    inner_part = spectral[:, :inner_width].reshape(plane_dev, len(inner_nodes), elem_dev)
    condensed_hat = spectral[:, inner_width:]
    solved = fast_solve(inner_part, eigen_basis, eigen_values, shifts)
    coupled = jnp.einsum("ji,rie->rje", coupling, solved, precision=lax.Precision.HIGHEST)
    local_sums = condensed_hat - jnp.dot(
        coupled.reshape(plane_dev, -1), onehot, precision=lax.Precision.HIGHEST
    )
    padded = extended(local_sums.reshape(1, 1, -1), (("ex", 0), ("ey", 1)), 1)
    neighbours = (
        padded[2, 1].reshape(plane_dev, unknowns),
        padded[0, 1].reshape(plane_dev, unknowns),
        padded[1, 2].reshape(plane_dev, unknowns),
        padded[1, 0].reshape(plane_dev, unknowns),
    )
    assembled = local_sums
    for side_code, neighbour in enumerate(neighbours):
        picked = jnp.take(neighbour, partners[0], axis=1)
        assembled = assembled + jnp.where(
            (sides[0] == side_code + 1)[None, :], picked, jnp.zeros_like(picked)
        )
    interface = jnp.einsum("rst,rt->rs", inverse_blocks, assembled, precision=lax.Precision.HIGHEST)
    boundary = jnp.dot(interface, onehot.T, precision=lax.Precision.HIGHEST).reshape(
        plane_dev, len(rim_nodes), elem_dev
    )
    lifted = jnp.einsum("ji,rje->rie", coupling, boundary, precision=lax.Precision.HIGHEST)
    interior = solved - fast_solve(lifted, eigen_basis, eigen_values, shifts)
    return (interior, interface[:, None, :])


def on_device(*args):
    modes = lax.axis_size("mode")
    if modes == CORES * CORES:
        return paired(*args)
    return general(*args)


def solution(mesh):
    placed = (
        P("mode", None, ("ex", "ey")),
        P(),
        P(),
        P(),
        P("mode", None, None),
        P(None, ("ex", "ey")),
        P(("ex", "ey"), None),
        P(("ex", "ey"), None),
    )
    return jax.shard_map(
        on_device,
        mesh=mesh,
        in_specs=placed,
        out_specs=(P("mode", None, ("ex", "ey")), P("mode", ("ex", "ey"), None)),
        check_vma=False,
    )
```

```python
import functools
import math

import jax
import jax.numpy as jnp
import numpy as np
from jax import lax
from jax.experimental import pallas as pl
from jax.experimental.pallas import tpu as pltpu
from jax.sharding import PartitionSpec as P

helm_base = 0.5
wave_unit = 1.0 / 64.0
f32, bf16 = jnp.float32, jnp.bfloat16
TILE = 8
CORES = 2
SPAN = 256
RUNS = 4
RAW_SHARE = 51
LIMIT = 12 * 2**20


def is_inner(node_id):
    return 1 <= node_id // 9 <= 7 and 1 <= node_id % 9 <= 7


def node_lists():
    inner_nodes = np.array([node_id for node_id in range(81) if is_inner(node_id)], dtype=np.int32)
    rim_nodes = np.array(
        [node_id for node_id in range(81) if not is_inner(node_id)], dtype=np.int32
    )
    return (inner_nodes, rim_nodes)


def split(values):
    high = values.astype(bf16)
    return high, (values - high.astype(f32)).astype(bf16)


def stack_split(values):
    return jnp.concatenate(split(values), axis=0)


def dot(left, right):
    return jnp.dot(left, right, preferred_element_type=f32)


def exact(left, right):
    return jnp.dot(left, right, preferred_element_type=f32, precision=lax.Precision.HIGHEST)


def dot_t(left, right):
    return lax.dot_general(left, right, (((1,), (1,)), ((), ())), preferred_element_type=f32)


def fold(values):
    half = values.shape[0] // 2
    return values[:half] + values[half:]


def dot3(left, high, low):
    return fold(dot(left, high)) + dot(left[: left.shape[0] // 2], low)


def iota(shape, dim):
    return lax.broadcasted_iota(jnp.int32, shape, dim)


def chosen(blocks, line):
    lanes = 128
    width = blocks[0].shape[1]
    out = [[] for _ in blocks]
    for start in range(0, line.shape[1], lanes):
        index = jnp.broadcast_to(line[:, start : start + lanes], (TILE, lanes))
        place = index & (lanes - 1)
        beyond = [index >= first for first in range(lanes, width, lanes)]
        for block, parts in zip(blocks, out):
            found = jnp.take_along_axis(block[:, :lanes], place, axis=1)
            for i, mask in enumerate(beyond):
                first = (i + 1) * lanes
                found = jnp.where(mask, jnp.take_along_axis(block[:, first : first + lanes], place, axis=1), found)
            parts.append(found)
    return [jnp.concatenate(parts, axis=1) for parts in out]


def member(line, unknowns):
    return jnp.where(iota((unknowns, line.shape[1]), 0) == line, 1.0, 0.0).astype(bf16)


def weighted(scalars, blocks):
    total = scalars[0] * blocks[0]
    for scalar, block in zip(scalars[1:], blocks[1:]):
        total = total + scalar * block
    return total


def kron_matrix(basis):
    size = basis.shape[0]
    count = size * size

    def digits(index):
        lead = jnp.zeros_like(index)
        for step in range(1, size):
            lead = lead + (index >= step * size).astype(jnp.int32)
        return lead, index - lead * size

    def spread(row_digit, col_digit):
        out = jnp.zeros((count, count), f32)
        for i in range(size):
            line = jnp.zeros((1, count), f32)
            for j in range(size):
                line = jnp.where(col_digit == j, basis[i, j], line)
            out = jnp.where(row_digit == i, line, out)
        return out

    (a, b), (c, d) = digits(iota((count, 1), 0)), digits(iota((1, count), 1))
    return spread(a, c) * spread(b, d)


def wave_of(row, count):
    return jnp.where(row == 1, count // 2, row // 2)


def dft_blocks(device, devices, share, rows_of, cols_of):
    count = devices * share
    tall, width = share * len(rows_of), share * len(cols_of)
    copies = SPAN // width

    def index_of(ids, offsets):
        part = ids // share
        owner = jnp.where(part == 0, device ^ offsets[0], 0)
        for i, offset in enumerate(offsets[1:]):
            owner = jnp.where(part == i + 1, device ^ offset, owner)
        return owner * share + ids % share

    row = index_of(iota((tall, SPAN), 0), rows_of)
    plane = index_of(iota((tall, SPAN), 1) % width, cols_of)
    angle = 2.0 * math.pi / count * (wave_of(row, count) * plane % count).astype(f32)
    odd = (row % 2 == 1) & (row != 1)
    scale = jnp.where(row <= 1, math.sqrt(1.0 / count), math.sqrt(2.0 / count))
    block = jnp.where(odd, jnp.sin(angle), jnp.cos(angle)) * scale
    full = jnp.concatenate([block] * copies, axis=0)
    same = iota(full.shape, 0) // tall == iota(full.shape, 1) // width
    return stack_split(jnp.where(same, full, 0.0))


def corner(left, rows, cols):
    height = left.shape[0] // 2
    if (rows, cols) == (height, left.shape[1]):
        return left
    return jnp.concatenate([left[:rows, :cols], left[height : height + rows, :cols]], axis=0)


def octet(block, part):
    rows, _, elems = block.shape
    return block[:, part * TILE : (part + 1) * TILE, :].reshape(rows * TILE, elems)


def take_kernel(nodes, *refs, wanted):
    count = (len(refs) - 2) // 2
    sources, out, copies, ready = refs[:count], refs[count], refs[count + 1 : -1], refs[-1]
    moves = [pltpu.make_async_copy(source, copy, ready.at[i]) for i, (source, copy) in enumerate(zip(sources, copies))]
    first = 0
    runs = []
    for node, length in wanted:
        run = pltpu.make_async_copy(nodes.at[node : node + length], out.at[first : first + length], ready.at[count + len(runs)])
        runs.append(run)
        first += length
    for move in runs + moves:
        move.start()
    for move in runs + moves:
        move.wait()


def per_mode(left, right, values, owner, share, devices, modes):
    size = values.shape[0]
    n = iota(right.shape, 0)
    sums = jnp.zeros(n.shape, f32)
    for c in range(size):
        sums = sums + jnp.where((n >= c * size) & (n < (c + 1) * size), values[c], 0.0)
        for d in range(size):
            sums = sums + jnp.where(n == c * size + d, values[d], 0.0)
    rows = left.shape[0] // 2
    for r in range(share):
        wave = wave_of(owner * share + r, devices * share).astype(f32) * wave_unit
        modes[r, :rows, :] = dot3(left, *split(right / (sums + (helm_base + wave * wave))))


def widened(modes, part, rows, cols):
    block = jnp.transpose(modes[part * TILE : (part + 1) * TILE], (1, 0, 2))[:rows, :, :cols]
    spread = jnp.where(iota((cols, cols * TILE), 0) == iota((cols, cols * TILE), 1) // TILE, 1.0, 0.0).astype(bf16)
    same = (iota((TILE, cols * TILE), 0) == iota((TILE, cols * TILE), 1) % TILE)[None]
    out = []
    for half in split(block.reshape(rows * TILE, cols)):
        full = dot(half, spread).reshape(rows, TILE, cols * TILE)
        out.append(jnp.where(same, full, 0.0).reshape(rows * TILE, cols * TILE).astype(bf16))
    return out


def tables_kernel(
    basis, values, coupling, planes, slots, table, lead, rest, pull, where, held, modes, ready, *, devices
):
    move = pltpu.make_async_copy(planes, held, ready)
    move.start()
    rim, inner = coupling.shape
    elems = slots.shape[1]
    octets, _, first = lead.shape
    edge = inner * TILE
    columns = slots[...].astype(f32).T
    ids = iota((elems, where.shape[1]), 1).astype(f32)
    for j in range(rim):
        where[j * elems : (j + 1) * elems, :] = jnp.where(ids == columns[:, j : j + 1], 1.0, 0.0).astype(bf16)
    kron = kron_matrix(basis)
    couple = exact(coupling[...], kron)
    device = lax.axis_index("mode")
    share = octets * TILE
    both = jnp.concatenate([couple, kron], axis=0)
    right = jnp.concatenate([kron, couple], axis=0).T
    per_mode(stack_split(couple), right, values, device ^ CORES, share, devices, modes)
    for part in range(octets):
        table[part] = jnp.concatenate(widened(modes, part, rim, inner), axis=0)
    per_mode(stack_split(both), right, values, device, share, devices, modes)
    top = rim * TILE
    for part in range(octets):
        halves = widened(modes, part, rim + inner, rim + inner)

        def put(out, place, rows, cols):
            out[place] = jnp.concatenate([half[rows, cols] for half in halves], axis=0)

        put(table, octets + part, slice(0, top), slice(0, edge))
        put(lead, part, slice(top, None), slice(0, first))
        put(rest, part, slice(top, None), slice(first, edge))
        put(pull, part, slice(top, None), slice(edge, None))
    move.wait()


def near_kernel(
    own, mate, where, table, sums_out, sums_own, send, keep, spectra, *, devices, inner_nodes, rim_nodes
):
    _, share, elems = own.shape
    pair = 2 * share
    inner, rim = len(inner_nodes), len(rim_nodes)
    raw_rows = inner - send.shape[0]
    left = dft_blocks(lax.axis_index("mode"), devices, share, (CORES, 0), (0, 1))
    group = left.shape[1] // pair
    base = 0
    for nodes in (inner_nodes, rim_nodes):
        for first in range(0, len(nodes), group):
            part = nodes[first : first + group]
            block = jnp.concatenate([ref[node] for node in part for ref in (own, mate)], axis=0)
            rows = block.shape[0]
            out = dot3(corner(left, rows, rows), *split(block)).reshape(len(part), pair, elems)
            spectra[base + first : base + first + len(part)] = out
        base += len(nodes)
    send[...] = spectra[raw_rows:inner, :share, :]
    keep[...] = spectra[:inner, share:, :]
    parts = []
    for part in range(pair // TILE):
        place = slice(part * TILE, (part + 1) * TILE)
        block = spectra[:inner, place, :].reshape(inner * TILE, elems)
        coupled = dot3(table[part], *split(block)).reshape(rim, TILE, elems)
        parts.append(spectra[inner:, place, :] - coupled)
    residual = jnp.concatenate(parts, axis=1)
    line = jnp.concatenate([stack_split(residual[j]) for j in range(rim)], axis=1)
    sums = fold(dot(line, where[...]))
    sums_out[...] = sums[:share]
    sums_own[...] = sums[share:]


def far_kernel(keep, first, second, lead, rest, solved, spectral, *, devices):
    rows, share, elems = first.shape
    inner = keep.shape[0]
    left = dft_blocks(lax.axis_index("mode"), devices, share, (0,), (CORES, CORES + 1))
    group = left.shape[1] // (2 * share)
    for start in range(0, rows, group):
        part = range(start, min(start + group, rows))
        block = jnp.concatenate([x for k in part for x in (first[k], second[k])], axis=0)
        out = dot3(corner(left, share * len(part), 2 * share * len(part)), *split(block))
        spectral[start : start + len(part)] = keep[start : start + len(part)] + out.reshape(-1, share, elems)
    for part in range(share // TILE):
        place = slice(part * TILE, (part + 1) * TILE)
        block = dot3(lead[part], *split(octet(spectral[...], part)))
        block = block + dot3(rest[part], *split(keep[rows:, place, :].reshape(-1, elems)))
        solved[:, place, :] = block.reshape(inner, TILE, elems)


def back_kernel(sums, *refs, codes):
    neighbours = len(codes)
    near = refs[:neighbours]
    sides, partners, inverse, slots, pull, solved, interior, interface = refs[neighbours:]
    share, unknowns = sums.shape
    inner, _, elems = interior.shape
    rim = slots.shape[0]
    group = lax.axis_index("ex") * lax.axis_size("ey") + lax.axis_index("ey")
    octets = [slice(start, start + TILE) for start in range(0, share, TILE)]
    assembled = [sums[place] for place in octets]
    for i in range(neighbours):
        code = jnp.int32(codes[i][0])
        for g, other in enumerate(codes[i][1:], 1):
            code = jnp.where(group == g, other, code)
        picked = chosen([near[i][place] for place in octets], partners[...])
        assembled = [part + jnp.where(sides[...] == code, new, 0.0) for part, new in zip(assembled, picked)]
    values = []
    for place, part in zip(octets, assembled):
        lines = []
        for r in range(TILE):
            line = jnp.sum(inverse[place.start + r] * part[r : r + 1, :], axis=1).reshape(1, unknowns)
            interface[place.start + r] = line
            lines.append(line)
        values.append(jnp.concatenate(lines, axis=0))
    boundary = [chosen(values, slots[j : j + 1, :]) for j in range(rim)]
    for part, place in enumerate(octets):
        block = jnp.concatenate([blocks[part] for blocks in boundary], axis=0)
        lifted = dot3(pull[part], *split(block)).reshape(inner, TILE, elems)
        interior[:, place, :] = solved[:, place, :] - lifted


def final_kernel(base, received, rest, out, interior, ready):
    inner, share, elems = interior.shape
    octets = range(share // TILE)
    blocks = [split(octet(received[...], part)) for part in octets]
    runs = ready.shape[0]
    size = -(-inner // runs)
    moves = []
    for i in range(runs):
        nodes = slice(i * size, min((i + 1) * size, inner))
        for part in octets:
            place = slice(part * TILE, (part + 1) * TILE)
            high, low = (
                rest[part, first + nodes.start * TILE : first + nodes.stop * TILE, :] for first in (0, inner * TILE)
            )
            product = dot(high, blocks[part][0]) + dot(low, blocks[part][0]) + dot(high, blocks[part][1])
            interior[nodes, place, :] = base[nodes, place, :] + product.reshape(-1, TILE, elems)
        moves.append(pltpu.make_async_copy(interior.at[nodes], out.at[nodes], ready.at[i]))
        moves[-1].start()
    for move in moves:
        move.wait()


VMEM = pl.BlockSpec(memory_space=pltpu.VMEM)
ANY = pl.BlockSpec(memory_space=pl.ANY)
SMEM = pl.BlockSpec(memory_space=pltpu.SMEM)


def shape(*dims, dtype=f32):
    return jax.ShapeDtypeStruct(dims, dtype)


def kernel_call(body, outs, ins, name, micros, scratch=(), out_specs=None):
    in_specs, arrays = [], []
    for item in ins:
        place, array = item if isinstance(item, tuple) else ("", item)
        in_specs.append({"smem": SMEM, "any": ANY}.get(place, VMEM))
        if place in ("any", "hbm", "vmem"):
            array = pltpu.with_memory_space_constraint(array, pltpu.VMEM if place == "vmem" else pltpu.HBM)
        arrays.append(array)
    return pl.pallas_call(
        body,
        out_shape=outs,
        in_specs=in_specs,
        out_specs=out_specs or ((VMEM,) * len(outs) if isinstance(outs, tuple) else VMEM),
        scratch_shapes=scratch,
        compiler_params=pltpu.CompilerParams(vmem_limit_bytes=LIMIT),
        cost_estimate=pl.CostEstimate(flops=0, transcendentals=0, bytes_accessed=int(micros * 3e6)),
        name=name,
    )(*arrays)


def exchanges(block):
    wide, tall = lax.axis_size("ex"), lax.axis_size("ey")
    group = lambda x, y: x * tall + y
    rounds = []
    for first in range(min(2, tall - 1)):
        pairs = {group(x, y): group(x, y + 1) for x in range(wide) for y in range(first, tall - 1, 2)}
        rounds.append(pairs)
    if len(rounds) == 2:
        busy = set(rounds[1]) | set(rounds[1].values())
        for y in range(tall):
            for x in range(0, wide - 1, 2):
                if not {group(x, y), group(x + 1, y)} & busy:
                    rounds[1][group(x, y)] = group(x + 1, y)
    for first in range(min(2, wide - 1)):
        rounds.append({group(x, y): group(x + 1, y) for x in range(first, wide - 1, 2) for y in range(tall)})
    got, known = [], set()
    for pairs in rounds:
        moves = [*pairs.items(), *((b, a) for a, b in pairs.items())]
        code = [-1] * (wide * tall)
        for a, b in moves:
            if (a, b) not in known:
                known.add((a, b))
                near = abs(a - b) == 1
                code[b] = (3 if near else 1) + (1 if a < b else 0)
        got.append((lax.ppermute(block, ("ex", "ey"), moves), tuple(code)))
    return got


def paired(forcing, eigen_basis, eigen_values, coupling, inverse_blocks, slots, sides, partners):
    inner_nodes, rim_nodes = node_lists()
    share, nodes, elems = forcing.shape
    unknowns = inverse_blocks.shape[1]
    modes = lax.axis_size("mode")
    inner, rim = len(inner_nodes), len(rim_nodes)
    side = round(math.sqrt(nodes))
    raw_rows = inner * RAW_SHARE // 100
    line = side - 2
    runs = [
        (int(inner_nodes[first]), min(line, raw_rows - first)) for first in range(0, raw_rows, line)
    ]
    rest_rows = inner - raw_rows
    octets = share // TILE
    mates = [(i, i ^ 1) for i in range(modes)]
    across = [(i, i ^ CORES) for i in range(modes)]
    planes = jnp.transpose(forcing, (1, 0, 2))
    small = [eigen_basis, eigen_values, coupling, slots]
    own_raw, *small = kernel_call(
        functools.partial(take_kernel, wanted=runs),
        (shape(raw_rows, share, elems), *[jax.ShapeDtypeStruct(x.shape, x.dtype) for x in small]),
        [("any", planes), *[("any", x) for x in small]],
        "raw_rows",
        0.5,
        [pltpu.SemaphoreType.DMA((len(small) + len(runs),))],
    )
    eigen_basis, eigen_values, coupling, slots_held = small
    basis, values = ("smem", eigen_basis), ("smem", eigen_values)
    planes, own_raw = lax.optimization_barrier((planes, own_raw))
    first = lax.ppermute(own_raw, "mode", across)
    mate_planes = lax.ppermute(planes, "mode", mates)
    tall = 2 * TILE
    table, lead, rest, pull, where, own_planes = kernel_call(
        functools.partial(tables_kernel, devices=modes),
        (
            shape(2 * octets, tall * rim, inner * TILE, dtype=bf16),
            shape(octets, tall * inner, raw_rows * TILE, dtype=bf16),
            shape(octets, tall * inner, rest_rows * TILE, dtype=bf16),
            shape(octets, tall * inner, rim * TILE, dtype=bf16),
            shape(rim * elems, unknowns, dtype=bf16),
            shape(*planes.shape),
        ),
        [basis, values, coupling, ("any", planes), slots_held],
        "tables",
        2.5,
        [pltpu.VMEM((share, -(-(inner + rim) // TILE) * TILE, inner + rim), f32), pltpu.SemaphoreType.DMA],
    )
    sums_out, sums_own, send, keep = kernel_call(
        functools.partial(
            near_kernel,
            devices=modes,
            inner_nodes=[int(node) for node in inner_nodes],
            rim_nodes=[int(node) for node in rim_nodes],
        ),
        (
            shape(share, unknowns),
            shape(share, unknowns),
            shape(rest_rows, share, elems),
            shape(inner, share, elems),
        ),
        [own_planes, mate_planes, where, table],
        "near_spectra",
        3.0,
        [pltpu.VMEM((nodes, 2 * share, elems), f32)],
    )
    sums_in, send = lax.optimization_barrier((lax.ppermute(sums_out, "mode", across), send))
    sums = sums_own + sums_in
    received = lax.ppermute(send, "mode", across)
    second = lax.ppermute(first, "mode", mates)
    solved = kernel_call(
        functools.partial(far_kernel, devices=modes),
        shape(inner, share, elems),
        [keep, first, second, lead, rest],
        "far_spectra",
        1.5,
        [pltpu.VMEM((raw_rows, share, elems), f32)],
    )
    got = exchanges(sums)
    base, interface = kernel_call(
        functools.partial(back_kernel, codes=[codes for _, codes in got]),
        (shape(inner, share, elems), shape(share, 1, unknowns)),
        [sums, *[block for block, _ in got], sides, partners, inverse_blocks, slots, pull, solved],
        "back_solve",
        2.0,
    )
    interior = kernel_call(
        final_kernel,
        shape(inner, share, elems),
        [base, ("vmem", received), rest],
        "interior_solve",
        1.0,
        [pltpu.VMEM((inner, share, elems), f32), pltpu.SemaphoreType.DMA((RUNS,))],
        out_specs=ANY,
    )
    return (jnp.transpose(interior, (1, 0, 2)), interface)


def extended(block, sides, width):
    for axis, dim in sides:
        count = lax.axis_size(axis)
        forward = [(i, i + 1) for i in range(count - 1)]
        backward = [(target, source) for source, target in forward]
        low = lax.ppermute(
            lax.slice_in_dim(block, block.shape[dim] - width, None, axis=dim), axis, forward
        )
        high = lax.ppermute(lax.slice_in_dim(block, 0, width, axis=dim), axis, backward)
        block = jnp.concatenate([low, block, high], axis=dim)
    return block


def wave_numbers(row_ids, count):
    return jnp.where(row_ids == 1, count // 2, row_ids // 2)


def dft_table(count):
    row_ids = jnp.arange(count, dtype=jnp.int32)
    wave_ids = wave_numbers(row_ids, count)
    phase_ids = wave_ids[:, None] * row_ids[None, :] % count
    angles = 2.0 * math.pi / count * phase_ids.astype(jnp.float32)
    odd_rows = (row_ids % 2 == 1) & (row_ids != 1)
    scales = jnp.where(row_ids <= 1, math.sqrt(1.0 / count), math.sqrt(2.0 / count)).astype(
        jnp.float32
    )
    return jnp.where(odd_rows[:, None], jnp.sin(angles), jnp.cos(angles)) * scales[:, None]


def mode_shifts(row_ids, count):
    waves = wave_numbers(row_ids, count).astype(jnp.float32) * wave_unit
    return helm_base + waves * waves


def fast_solve(values, eigen_basis, eigen_values, shifts):
    kron_basis = jnp.kron(eigen_basis, eigen_basis)
    pair_sums = (eigen_values[:, None] + eigen_values[None, :]).reshape(-1)
    spectra = jnp.einsum("ji,rje->rie", kron_basis, values, precision=lax.Precision.HIGHEST)
    spectra = spectra / (pair_sums[None, :, None] + shifts[:, None, None])
    return jnp.einsum("ij,rje->rie", kron_basis, spectra, precision=lax.Precision.HIGHEST)


def general(forcing, eigen_basis, eigen_values, coupling, inverse_blocks, slots, sides, partners):
    inner_nodes, rim_nodes = node_lists()
    plane_dev = forcing.shape[0]
    elem_dev = forcing.shape[2]
    unknowns = inverse_blocks.shape[1]
    modes_axis = lax.axis_size("mode")
    plane_count = modes_axis * plane_dev
    table = dft_table(plane_count)
    row_ids = lax.axis_index("mode") * plane_dev + jnp.arange(plane_dev, dtype=jnp.int32)
    shifts = mode_shifts(row_ids, plane_count)
    onehot = (slots.reshape(-1)[:, None] == jnp.arange(unknowns, dtype=jnp.int32)[None, :]).astype(
        jnp.float32
    )
    inner_width = len(inner_nodes) * elem_dev
    rim_planes = forcing[:, rim_nodes, :].reshape(plane_dev, -1)
    condensed = jnp.dot(rim_planes, onehot, precision=lax.Precision.HIGHEST)
    payload = jnp.concatenate(
        [forcing[:, inner_nodes, :].reshape(plane_dev, -1), condensed], axis=1
    )
    total_width = payload.shape[1]
    sectioned = payload.reshape(plane_dev, modes_axis, total_width // modes_axis)
    spectra = jnp.einsum(
        "rp,pkc->rkc",
        table,
        lax.all_to_all(sectioned, "mode", split_axis=1, concat_axis=0, tiled=True),
        precision=lax.Precision.HIGHEST,
    )
    spectral = lax.all_to_all(spectra, "mode", split_axis=0, concat_axis=1, tiled=True).reshape(
        plane_dev, total_width
    )
    inner_part = spectral[:, :inner_width].reshape(plane_dev, len(inner_nodes), elem_dev)
    condensed_hat = spectral[:, inner_width:]
    solved = fast_solve(inner_part, eigen_basis, eigen_values, shifts)
    coupled = jnp.einsum("ji,rie->rje", coupling, solved, precision=lax.Precision.HIGHEST)
    local_sums = condensed_hat - jnp.dot(
        coupled.reshape(plane_dev, -1), onehot, precision=lax.Precision.HIGHEST
    )
    padded = extended(local_sums.reshape(1, 1, -1), (("ex", 0), ("ey", 1)), 1)
    neighbours = (
        padded[2, 1].reshape(plane_dev, unknowns),
        padded[0, 1].reshape(plane_dev, unknowns),
        padded[1, 2].reshape(plane_dev, unknowns),
        padded[1, 0].reshape(plane_dev, unknowns),
    )
    assembled = local_sums
    for side_code, neighbour in enumerate(neighbours):
        picked = jnp.take(neighbour, partners[0], axis=1)
        assembled = assembled + jnp.where(
            (sides[0] == side_code + 1)[None, :], picked, jnp.zeros_like(picked)
        )
    interface = jnp.einsum("rst,rt->rs", inverse_blocks, assembled, precision=lax.Precision.HIGHEST)
    boundary = jnp.dot(interface, onehot.T, precision=lax.Precision.HIGHEST).reshape(
        plane_dev, len(rim_nodes), elem_dev
    )
    lifted = jnp.einsum("ji,rje->rie", coupling, boundary, precision=lax.Precision.HIGHEST)
    interior = solved - fast_solve(lifted, eigen_basis, eigen_values, shifts)
    return (interior, interface[:, None, :])


def on_device(*args):
    modes = lax.axis_size("mode")
    if modes == CORES * CORES:
        return paired(*args)
    return general(*args)


def solution(mesh):
    placed = (
        P("mode", None, ("ex", "ey")),
        P(),
        P(),
        P(),
        P("mode", None, None),
        P(None, ("ex", "ey")),
        P(("ex", "ey"), None),
        P(("ex", "ey"), None),
    )
    return jax.shard_map(
        on_device,
        mesh=mesh,
        in_specs=placed,
        out_specs=(P("mode", None, ("ex", "ey")), P("mode", ("ex", "ey"), None)),
        check_vma=False,
    )
```

```python
import functools
import math

import jax
import jax.numpy as jnp
import numpy as np
from jax import lax
from jax.experimental import pallas as pl
from jax.experimental.pallas import tpu as pltpu
from jax.sharding import PartitionSpec as P

helm_base = 0.5
wave_unit = 1.0 / 64.0
f32, bf16 = jnp.float32, jnp.bfloat16
TILE = 8
CORES = 2
SPAN = 256
RUNS = 4
RAW_SHARE = 51
LIMIT = 12 * 2**20


def is_inner(node_id):
    return 1 <= node_id // 9 <= 7 and 1 <= node_id % 9 <= 7


def node_lists():
    inner_nodes = np.array([node_id for node_id in range(81) if is_inner(node_id)], dtype=np.int32)
    rim_nodes = np.array(
        [node_id for node_id in range(81) if not is_inner(node_id)], dtype=np.int32
    )
    return (inner_nodes, rim_nodes)


def split(values):
    high = values.astype(bf16)
    return high, (values - high.astype(f32)).astype(bf16)


def stack_split(values):
    return jnp.concatenate(split(values), axis=0)


def dot(left, right):
    return jnp.dot(left, right, preferred_element_type=f32)


def exact(left, right):
    return jnp.dot(left, right, preferred_element_type=f32, precision=lax.Precision.HIGHEST)


def dot_t(left, right):
    return lax.dot_general(left, right, (((1,), (1,)), ((), ())), preferred_element_type=f32)


def fold(values):
    half = values.shape[0] // 2
    return values[:half] + values[half:]


def dot3(left, high, low):
    return fold(dot(left, high)) + dot(left[: left.shape[0] // 2], low)


def iota(shape, dim):
    return lax.broadcasted_iota(jnp.int32, shape, dim)


def chosen(blocks, line):
    lanes = 128
    width = blocks[0].shape[1]
    out = [[] for _ in blocks]
    for start in range(0, line.shape[1], lanes):
        index = jnp.broadcast_to(line[:, start : start + lanes], (TILE, lanes))
        place = index & (lanes - 1)
        beyond = [index >= first for first in range(lanes, width, lanes)]
        for block, parts in zip(blocks, out):
            found = jnp.take_along_axis(block[:, :lanes], place, axis=1)
            for i, mask in enumerate(beyond):
                first = (i + 1) * lanes
                found = jnp.where(mask, jnp.take_along_axis(block[:, first : first + lanes], place, axis=1), found)
            parts.append(found)
    return [jnp.concatenate(parts, axis=1) for parts in out]


def member(line, unknowns):
    return jnp.where(iota((unknowns, line.shape[1]), 0) == line, 1.0, 0.0).astype(bf16)


def weighted(scalars, blocks):
    total = scalars[0] * blocks[0]
    for scalar, block in zip(scalars[1:], blocks[1:]):
        total = total + scalar * block
    return total


def kron_matrix(basis):
    size = basis.shape[0]
    count = size * size

    def digits(index):
        lead = jnp.zeros_like(index)
        for step in range(1, size):
            lead = lead + (index >= step * size).astype(jnp.int32)
        return lead, index - lead * size

    def spread(row_digit, col_digit):
        out = jnp.zeros((count, count), f32)
        for i in range(size):
            line = jnp.zeros((1, count), f32)
            for j in range(size):
                line = jnp.where(col_digit == j, basis[i, j], line)
            out = jnp.where(row_digit == i, line, out)
        return out

    (a, b), (c, d) = digits(iota((count, 1), 0)), digits(iota((1, count), 1))
    return spread(a, c) * spread(b, d)


def wave_of(row, count):
    return jnp.where(row == 1, count // 2, row // 2)


def dft_blocks(device, devices, share, rows_of, cols_of):
    count = devices * share
    tall, width = share * len(rows_of), share * len(cols_of)
    copies = SPAN // width

    def index_of(ids, offsets):
        part = ids // share
        owner = jnp.where(part == 0, device ^ offsets[0], 0)
        for i, offset in enumerate(offsets[1:]):
            owner = jnp.where(part == i + 1, device ^ offset, owner)
        return owner * share + ids % share

    row = index_of(iota((tall, SPAN), 0), rows_of)
    plane = index_of(iota((tall, SPAN), 1) % width, cols_of)
    angle = 2.0 * math.pi / count * (wave_of(row, count) * plane % count).astype(f32)
    odd = (row % 2 == 1) & (row != 1)
    scale = jnp.where(row <= 1, math.sqrt(1.0 / count), math.sqrt(2.0 / count))
    block = jnp.where(odd, jnp.sin(angle), jnp.cos(angle)) * scale
    full = jnp.concatenate([block] * copies, axis=0)
    same = iota(full.shape, 0) // tall == iota(full.shape, 1) // width
    return stack_split(jnp.where(same, full, 0.0))


def corner(left, rows, cols):
    height = left.shape[0] // 2
    if (rows, cols) == (height, left.shape[1]):
        return left
    return jnp.concatenate([left[:rows, :cols], left[height : height + rows, :cols]], axis=0)


def octet(block, part):
    rows, _, elems = block.shape
    return block[:, part * TILE : (part + 1) * TILE, :].reshape(rows * TILE, elems)


def take_kernel(nodes, *refs, wanted):
    count = (len(refs) - 2) // 2
    sources, out, copies, ready = refs[:count], refs[count], refs[count + 1 : -1], refs[-1]
    moves = [pltpu.make_async_copy(source, copy, ready.at[i]) for i, (source, copy) in enumerate(zip(sources, copies))]
    first = 0
    runs = []
    for node, length in wanted:
        run = pltpu.make_async_copy(nodes.at[node : node + length], out.at[first : first + length], ready.at[count + len(runs)])
        runs.append(run)
        first += length
    for move in runs + moves:
        move.start()
    for move in runs + moves:
        move.wait()


def per_mode(left, right, values, owner, share, devices, modes):
    size = values.shape[0]
    n = iota(right.shape, 0)
    sums = jnp.zeros(n.shape, f32)
    for c in range(size):
        sums = sums + jnp.where((n >= c * size) & (n < (c + 1) * size), values[c], 0.0)
        for d in range(size):
            sums = sums + jnp.where(n == c * size + d, values[d], 0.0)
    rows = left.shape[0] // 2
    for r in range(share):
        wave = wave_of(owner * share + r, devices * share).astype(f32) * wave_unit
        modes[r, :rows, :] = dot3(left, *split(right / (sums + (helm_base + wave * wave))))


def widened(modes, part, rows, cols):
    block = jnp.transpose(modes[part * TILE : (part + 1) * TILE], (1, 0, 2))[:rows, :, :cols]
    spread = jnp.where(iota((cols, cols * TILE), 0) == iota((cols, cols * TILE), 1) // TILE, 1.0, 0.0).astype(bf16)
    same = (iota((TILE, cols * TILE), 0) == iota((TILE, cols * TILE), 1) % TILE)[None]
    out = []
    for half in split(block.reshape(rows * TILE, cols)):
        full = dot(half, spread).reshape(rows, TILE, cols * TILE)
        out.append(jnp.where(same, full, 0.0).reshape(rows * TILE, cols * TILE).astype(bf16))
    return out


def tables_kernel(
    basis, values, coupling, planes, slots, table, lead, rest, pull, where, held, modes, ready, *, devices
):
    move = pltpu.make_async_copy(planes, held, ready)
    move.start()
    rim, inner = coupling.shape
    elems = slots.shape[1]
    octets, _, first = lead.shape
    edge = inner * TILE
    columns = slots[...].astype(f32).T
    ids = iota((elems, where.shape[1]), 1).astype(f32)
    for j in range(rim):
        where[j * elems : (j + 1) * elems, :] = jnp.where(ids == columns[:, j : j + 1], 1.0, 0.0).astype(bf16)
    kron = kron_matrix(basis)
    couple = exact(coupling[...], kron)
    device = lax.axis_index("mode")
    share = octets * TILE
    spare = lead.shape[1] // (2 * TILE) - inner
    both = jnp.concatenate([couple, kron, jnp.zeros((spare, inner), f32)], axis=0)
    right = jnp.concatenate([kron, couple], axis=0).T
    per_mode(stack_split(couple), right, values, device ^ CORES, share, devices, modes)
    for part in range(octets):
        table[part] = jnp.concatenate(widened(modes, part, rim, inner), axis=0)
    per_mode(stack_split(both), right, values, device, share, devices, modes)
    top = rim * TILE
    for part in range(octets):
        halves = widened(modes, part, rim + inner + spare, rim + inner)

        def put(out, place, rows, cols):
            height = out.shape[1] // 2
            for i, half in enumerate(halves):
                out[place, i * height : (i + 1) * height, :] = half[rows, cols]

        put(table, octets + part, slice(0, top), slice(0, edge))
        put(lead, part, slice(top, None), slice(0, first))
        put(rest, part, slice(top, None), slice(first, edge))
        put(pull, part, slice(top, None), slice(edge, None))
    move.wait()


def near_kernel(
    own, mate, where, table, sums_out, sums_own, send, keep, spectra, *, devices, inner_nodes, rim_nodes
):
    _, share, elems = own.shape
    pair = 2 * share
    inner, rim = len(inner_nodes), len(rim_nodes)
    raw_rows = inner - send.shape[0]
    left = dft_blocks(lax.axis_index("mode"), devices, share, (CORES, 0), (0, 1))
    group = left.shape[1] // pair
    base = 0
    for nodes in (inner_nodes, rim_nodes):
        for first in range(0, len(nodes), group):
            part = nodes[first : first + group]
            block = jnp.concatenate([ref[node] for node in part for ref in (own, mate)], axis=0)
            rows = block.shape[0]
            out = dot3(corner(left, rows, rows), *split(block)).reshape(len(part), pair, elems)
            spectra[base + first : base + first + len(part)] = out
        base += len(nodes)
    send[...] = spectra[raw_rows:inner, :share, :]
    keep[...] = spectra[:inner, share:, :]
    parts = []
    for part in range(pair // TILE):
        place = slice(part * TILE, (part + 1) * TILE)
        block = spectra[:inner, place, :].reshape(inner * TILE, elems)
        coupled = dot3(table[part], *split(block)).reshape(rim, TILE, elems)
        parts.append(spectra[inner:, place, :] - coupled)
    residual = jnp.concatenate(parts, axis=1)
    line = jnp.concatenate([stack_split(residual[j]) for j in range(rim)], axis=1)
    sums = fold(dot(line, where[...]))
    sums_out[...] = sums[:share]
    sums_own[...] = sums[share:]


def far_kernel(keep, first, second, lead, rest, solved, spectral, *, devices):
    rows, share, elems = first.shape
    inner = keep.shape[0]
    left = dft_blocks(lax.axis_index("mode"), devices, share, (0,), (CORES, CORES + 1))
    group = left.shape[1] // (2 * share)
    for start in range(0, rows, group):
        part = range(start, min(start + group, rows))
        block = jnp.concatenate([x for k in part for x in (first[k], second[k])], axis=0)
        out = dot3(corner(left, share * len(part), 2 * share * len(part)), *split(block))
        spectral[start : start + len(part)] = keep[start : start + len(part)] + out.reshape(-1, share, elems)
    for part in range(share // TILE):
        place = slice(part * TILE, (part + 1) * TILE)
        block = dot3(lead[part], *split(octet(spectral[...], part)))
        block = block + dot3(rest[part], *split(keep[rows:, place, :].reshape(-1, elems)))
        solved[:, place, :] = block[: inner * TILE].reshape(inner, TILE, elems)


def back_kernel(sums, *refs, codes):
    neighbours = len(codes)
    near = refs[:neighbours]
    sides, partners, inverse, slots, pull, solved, interior, interface = refs[neighbours:]
    share, unknowns = sums.shape
    inner, _, elems = interior.shape
    rim = slots.shape[0]
    group = lax.axis_index("ex") * lax.axis_size("ey") + lax.axis_index("ey")
    octets = [slice(start, start + TILE) for start in range(0, share, TILE)]
    assembled = [sums[place] for place in octets]
    for i in range(neighbours):
        code = jnp.int32(codes[i][0])
        for g, other in enumerate(codes[i][1:], 1):
            code = jnp.where(group == g, other, code)
        picked = chosen([near[i][place] for place in octets], partners[...])
        assembled = [part + jnp.where(sides[...] == code, new, 0.0) for part, new in zip(assembled, picked)]
    values = []
    for place, part in zip(octets, assembled):
        lines = []
        for r in range(TILE):
            line = jnp.sum(inverse[place.start + r] * part[r : r + 1, :], axis=1).reshape(1, unknowns)
            interface[place.start + r] = line
            lines.append(line)
        values.append(jnp.concatenate(lines, axis=0))
    boundary = [chosen(values, slots[j : j + 1, :]) for j in range(rim)]
    for part, place in enumerate(octets):
        block = jnp.concatenate([blocks[part] for blocks in boundary], axis=0)
        lifted = dot3(pull[part], *split(block))[: inner * TILE].reshape(inner, TILE, elems)
        interior[:, place, :] = solved[:, place, :] - lifted


def final_kernel(base, received, rest, out, interior, ready):
    inner, share, elems = interior.shape
    octets = range(share // TILE)
    blocks = [split(octet(received[...], part)) for part in octets]
    height = rest.shape[1] // 2
    size = -(-inner // RUNS)
    size += size % 2
    moves = []
    for i, first in enumerate(range(0, inner, size)):
        nodes = slice(first, min(first + size, inner))
        count = nodes.stop - first
        tall = (count + count % 2) * TILE
        for part in octets:
            place = slice(part * TILE, (part + 1) * TILE)
            high, low = (rest[part, start + first * TILE : start + first * TILE + tall, :] for start in (0, height))
            product = dot(high, blocks[part][0]) + dot(low, blocks[part][0]) + dot(high, blocks[part][1])
            interior[nodes, place, :] = base[nodes, place, :] + product[: count * TILE].reshape(-1, TILE, elems)
        moves.append(pltpu.make_async_copy(interior.at[nodes], out.at[nodes], ready.at[i]))
        moves[-1].start()
    for move in moves:
        move.wait()


VMEM = pl.BlockSpec(memory_space=pltpu.VMEM)
ANY = pl.BlockSpec(memory_space=pl.ANY)
SMEM = pl.BlockSpec(memory_space=pltpu.SMEM)


def shape(*dims, dtype=f32):
    return jax.ShapeDtypeStruct(dims, dtype)


def kernel_call(body, outs, ins, name, micros, scratch=(), out_specs=None):
    in_specs, arrays = [], []
    for item in ins:
        place, array = item if isinstance(item, tuple) else ("", item)
        in_specs.append({"smem": SMEM, "any": ANY}.get(place, VMEM))
        if place in ("any", "hbm", "vmem"):
            array = pltpu.with_memory_space_constraint(array, pltpu.VMEM if place == "vmem" else pltpu.HBM)
        arrays.append(array)
    return pl.pallas_call(
        body,
        out_shape=outs,
        in_specs=in_specs,
        out_specs=out_specs or ((VMEM,) * len(outs) if isinstance(outs, tuple) else VMEM),
        scratch_shapes=scratch,
        compiler_params=pltpu.CompilerParams(vmem_limit_bytes=LIMIT),
        cost_estimate=pl.CostEstimate(flops=0, transcendentals=0, bytes_accessed=int(micros * 3e6)),
        name=name,
    )(*arrays)


def exchanges(block):
    wide, tall = lax.axis_size("ex"), lax.axis_size("ey")
    group = lambda x, y: x * tall + y
    rounds = []
    for first in range(min(2, tall - 1)):
        pairs = {group(x, y): group(x, y + 1) for x in range(wide) for y in range(first, tall - 1, 2)}
        rounds.append(pairs)
    if len(rounds) == 2:
        busy = set(rounds[1]) | set(rounds[1].values())
        for y in range(tall):
            for x in range(0, wide - 1, 2):
                if not {group(x, y), group(x + 1, y)} & busy:
                    rounds[1][group(x, y)] = group(x + 1, y)
    for first in range(min(2, wide - 1)):
        rounds.append({group(x, y): group(x + 1, y) for x in range(first, wide - 1, 2) for y in range(tall)})
    got, known = [], set()
    for pairs in rounds:
        moves = [*pairs.items(), *((b, a) for a, b in pairs.items())]
        code = [-1] * (wide * tall)
        for a, b in moves:
            if (a, b) not in known:
                known.add((a, b))
                near = abs(a - b) == 1
                code[b] = (3 if near else 1) + (1 if a < b else 0)
        got.append((lax.ppermute(block, ("ex", "ey"), moves), tuple(code)))
    return got


def paired(forcing, eigen_basis, eigen_values, coupling, inverse_blocks, slots, sides, partners):
    inner_nodes, rim_nodes = node_lists()
    share, nodes, elems = forcing.shape
    unknowns = inverse_blocks.shape[1]
    modes = lax.axis_size("mode")
    inner, rim = len(inner_nodes), len(rim_nodes)
    side = round(math.sqrt(nodes))
    raw_rows = inner * RAW_SHARE // 100
    line = side - 2
    runs = [
        (int(inner_nodes[first]), min(line, raw_rows - first)) for first in range(0, raw_rows, line)
    ]
    rest_rows = inner - raw_rows
    octets = share // TILE
    mates = [(i, i ^ 1) for i in range(modes)]
    across = [(i, i ^ CORES) for i in range(modes)]
    planes = jnp.transpose(forcing, (1, 0, 2))
    small = [eigen_basis, eigen_values, coupling, slots]
    own_raw, *small = kernel_call(
        functools.partial(take_kernel, wanted=runs),
        (shape(raw_rows, share, elems), *[jax.ShapeDtypeStruct(x.shape, x.dtype) for x in small]),
        [("any", planes), *[("any", x) for x in small]],
        "raw_rows",
        0.5,
        [pltpu.SemaphoreType.DMA((len(small) + len(runs),))],
    )
    eigen_basis, eigen_values, coupling, slots_held = small
    basis, values = ("smem", eigen_basis), ("smem", eigen_values)
    planes, own_raw = lax.optimization_barrier((planes, own_raw))
    first = lax.ppermute(own_raw, "mode", across)
    mate_planes = lax.ppermute(planes, "mode", mates)
    tall = 2 * TILE
    padded = inner + inner % 2
    table, lead, rest, pull, where, own_planes = kernel_call(
        functools.partial(tables_kernel, devices=modes),
        (
            shape(2 * octets, tall * rim, inner * TILE, dtype=bf16),
            shape(octets, tall * padded, raw_rows * TILE, dtype=bf16),
            shape(octets, tall * padded, rest_rows * TILE, dtype=bf16),
            shape(octets, tall * padded, rim * TILE, dtype=bf16),
            shape(rim * elems, unknowns, dtype=bf16),
            shape(*planes.shape),
        ),
        [basis, values, coupling, ("any", planes), slots_held],
        "tables",
        2.5,
        [pltpu.VMEM((share, -(-(inner + rim) // TILE) * TILE, inner + rim), f32), pltpu.SemaphoreType.DMA],
    )
    sums_out, sums_own, send, keep = kernel_call(
        functools.partial(
            near_kernel,
            devices=modes,
            inner_nodes=[int(node) for node in inner_nodes],
            rim_nodes=[int(node) for node in rim_nodes],
        ),
        (
            shape(share, unknowns),
            shape(share, unknowns),
            shape(rest_rows, share, elems),
            shape(inner, share, elems),
        ),
        [own_planes, mate_planes, where, table],
        "near_spectra",
        3.0,
        [pltpu.VMEM((nodes, 2 * share, elems), f32)],
    )
    sums_in, send = lax.optimization_barrier((lax.ppermute(sums_out, "mode", across), send))
    sums = sums_own + sums_in
    received = lax.ppermute(send, "mode", across)
    second = lax.ppermute(first, "mode", mates)
    solved = kernel_call(
        functools.partial(far_kernel, devices=modes),
        shape(inner, share, elems),
        [keep, first, second, lead, rest],
        "far_spectra",
        1.5,
        [pltpu.VMEM((raw_rows, share, elems), f32)],
    )
    got = exchanges(sums)
    base, interface = kernel_call(
        functools.partial(back_kernel, codes=[codes for _, codes in got]),
        (shape(inner, share, elems), shape(share, 1, unknowns)),
        [sums, *[block for block, _ in got], sides, partners, inverse_blocks, slots, pull, solved],
        "back_solve",
        2.0,
    )
    interior = kernel_call(
        final_kernel,
        shape(inner, share, elems),
        [base, ("vmem", received), rest],
        "interior_solve",
        1.0,
        [pltpu.VMEM((inner, share, elems), f32), pltpu.SemaphoreType.DMA((RUNS,))],
        out_specs=ANY,
    )
    return (jnp.transpose(interior, (1, 0, 2)), interface)


def extended(block, sides, width):
    for axis, dim in sides:
        count = lax.axis_size(axis)
        forward = [(i, i + 1) for i in range(count - 1)]
        backward = [(target, source) for source, target in forward]
        low = lax.ppermute(
            lax.slice_in_dim(block, block.shape[dim] - width, None, axis=dim), axis, forward
        )
        high = lax.ppermute(lax.slice_in_dim(block, 0, width, axis=dim), axis, backward)
        block = jnp.concatenate([low, block, high], axis=dim)
    return block


def wave_numbers(row_ids, count):
    return jnp.where(row_ids == 1, count // 2, row_ids // 2)


def dft_table(count):
    row_ids = jnp.arange(count, dtype=jnp.int32)
    wave_ids = wave_numbers(row_ids, count)
    phase_ids = wave_ids[:, None] * row_ids[None, :] % count
    angles = 2.0 * math.pi / count * phase_ids.astype(jnp.float32)
    odd_rows = (row_ids % 2 == 1) & (row_ids != 1)
    scales = jnp.where(row_ids <= 1, math.sqrt(1.0 / count), math.sqrt(2.0 / count)).astype(
        jnp.float32
    )
    return jnp.where(odd_rows[:, None], jnp.sin(angles), jnp.cos(angles)) * scales[:, None]


def mode_shifts(row_ids, count):
    waves = wave_numbers(row_ids, count).astype(jnp.float32) * wave_unit
    return helm_base + waves * waves


def fast_solve(values, eigen_basis, eigen_values, shifts):
    kron_basis = jnp.kron(eigen_basis, eigen_basis)
    pair_sums = (eigen_values[:, None] + eigen_values[None, :]).reshape(-1)
    spectra = jnp.einsum("ji,rje->rie", kron_basis, values, precision=lax.Precision.HIGHEST)
    spectra = spectra / (pair_sums[None, :, None] + shifts[:, None, None])
    return jnp.einsum("ij,rje->rie", kron_basis, spectra, precision=lax.Precision.HIGHEST)


def general(forcing, eigen_basis, eigen_values, coupling, inverse_blocks, slots, sides, partners):
    inner_nodes, rim_nodes = node_lists()
    plane_dev = forcing.shape[0]
    elem_dev = forcing.shape[2]
    unknowns = inverse_blocks.shape[1]
    modes_axis = lax.axis_size("mode")
    plane_count = modes_axis * plane_dev
    table = dft_table(plane_count)
    row_ids = lax.axis_index("mode") * plane_dev + jnp.arange(plane_dev, dtype=jnp.int32)
    shifts = mode_shifts(row_ids, plane_count)
    onehot = (slots.reshape(-1)[:, None] == jnp.arange(unknowns, dtype=jnp.int32)[None, :]).astype(
        jnp.float32
    )
    inner_width = len(inner_nodes) * elem_dev
    rim_planes = forcing[:, rim_nodes, :].reshape(plane_dev, -1)
    condensed = jnp.dot(rim_planes, onehot, precision=lax.Precision.HIGHEST)
    payload = jnp.concatenate(
        [forcing[:, inner_nodes, :].reshape(plane_dev, -1), condensed], axis=1
    )
    total_width = payload.shape[1]
    sectioned = payload.reshape(plane_dev, modes_axis, total_width // modes_axis)
    spectra = jnp.einsum(
        "rp,pkc->rkc",
        table,
        lax.all_to_all(sectioned, "mode", split_axis=1, concat_axis=0, tiled=True),
        precision=lax.Precision.HIGHEST,
    )
    spectral = lax.all_to_all(spectra, "mode", split_axis=0, concat_axis=1, tiled=True).reshape(
        plane_dev, total_width
    )
    inner_part = spectral[:, :inner_width].reshape(plane_dev, len(inner_nodes), elem_dev)
    condensed_hat = spectral[:, inner_width:]
    solved = fast_solve(inner_part, eigen_basis, eigen_values, shifts)
    coupled = jnp.einsum("ji,rie->rje", coupling, solved, precision=lax.Precision.HIGHEST)
    local_sums = condensed_hat - jnp.dot(
        coupled.reshape(plane_dev, -1), onehot, precision=lax.Precision.HIGHEST
    )
    padded = extended(local_sums.reshape(1, 1, -1), (("ex", 0), ("ey", 1)), 1)
    neighbours = (
        padded[2, 1].reshape(plane_dev, unknowns),
        padded[0, 1].reshape(plane_dev, unknowns),
        padded[1, 2].reshape(plane_dev, unknowns),
        padded[1, 0].reshape(plane_dev, unknowns),
    )
    assembled = local_sums
    for side_code, neighbour in enumerate(neighbours):
        picked = jnp.take(neighbour, partners[0], axis=1)
        assembled = assembled + jnp.where(
            (sides[0] == side_code + 1)[None, :], picked, jnp.zeros_like(picked)
        )
    interface = jnp.einsum("rst,rt->rs", inverse_blocks, assembled, precision=lax.Precision.HIGHEST)
    boundary = jnp.dot(interface, onehot.T, precision=lax.Precision.HIGHEST).reshape(
        plane_dev, len(rim_nodes), elem_dev
    )
    lifted = jnp.einsum("ji,rje->rie", coupling, boundary, precision=lax.Precision.HIGHEST)
    interior = solved - fast_solve(lifted, eigen_basis, eigen_values, shifts)
    return (interior, interface[:, None, :])


def on_device(*args):
    modes = lax.axis_size("mode")
    if modes == CORES * CORES:
        return paired(*args)
    return general(*args)


def solution(mesh):
    placed = (
        P("mode", None, ("ex", "ey")),
        P(),
        P(),
        P(),
        P("mode", None, None),
        P(None, ("ex", "ey")),
        P(("ex", "ey"), None),
        P(("ex", "ey"), None),
    )
    return jax.shard_map(
        on_device,
        mesh=mesh,
        in_specs=placed,
        out_specs=(P("mode", None, ("ex", "ey")), P("mode", ("ex", "ey"), None)),
        check_vma=False,
    )
```

```python
import functools
import math

import jax
import jax.numpy as jnp
import numpy as np
from jax import lax
from jax.experimental import pallas as pl
from jax.experimental.pallas import tpu as pltpu
from jax.sharding import PartitionSpec as P

helm_base = 0.5
wave_unit = 1.0 / 64.0
f32, bf16 = jnp.float32, jnp.bfloat16
TILE = 8
CORES = 2
SPAN = 256
RUNS = 4
RAW_SHARE = 51
LIMIT = 12 * 2**20


def is_inner(node_id):
    return 1 <= node_id // 9 <= 7 and 1 <= node_id % 9 <= 7


def node_lists():
    inner_nodes = np.array([node_id for node_id in range(81) if is_inner(node_id)], dtype=np.int32)
    rim_nodes = np.array(
        [node_id for node_id in range(81) if not is_inner(node_id)], dtype=np.int32
    )
    return (inner_nodes, rim_nodes)


def split(values):
    high = values.astype(bf16)
    return high, (values - high.astype(f32)).astype(bf16)


def stack_split(values):
    return jnp.concatenate(split(values), axis=0)


def dot(left, right):
    return jnp.dot(left, right, preferred_element_type=f32)


def exact(left, right):
    return jnp.dot(left, right, preferred_element_type=f32, precision=lax.Precision.HIGHEST)


def dot_t(left, right):
    return lax.dot_general(left, right, (((1,), (1,)), ((), ())), preferred_element_type=f32)


def fold(values):
    half = values.shape[0] // 2
    return values[:half] + values[half:]


def dot3(left, high, low):
    return fold(dot(left, high)) + dot(left[: left.shape[0] // 2], low)


def iota(shape, dim):
    return lax.broadcasted_iota(jnp.int32, shape, dim)


def chosen(blocks, line):
    lanes = 128
    width = blocks[0].shape[1]
    out = [[] for _ in blocks]
    for start in range(0, line.shape[1], lanes):
        index = jnp.broadcast_to(line[:, start : start + lanes], (TILE, lanes))
        place = index & (lanes - 1)
        beyond = [index >= first for first in range(lanes, width, lanes)]
        for block, parts in zip(blocks, out):
            found = jnp.take_along_axis(block[:, :lanes], place, axis=1)
            for i, mask in enumerate(beyond):
                first = (i + 1) * lanes
                found = jnp.where(mask, jnp.take_along_axis(block[:, first : first + lanes], place, axis=1), found)
            parts.append(found)
    return [jnp.concatenate(parts, axis=1) for parts in out]


def member(line, unknowns):
    return jnp.where(iota((unknowns, line.shape[1]), 0) == line, 1.0, 0.0).astype(bf16)


def weighted(scalars, blocks):
    total = scalars[0] * blocks[0]
    for scalar, block in zip(scalars[1:], blocks[1:]):
        total = total + scalar * block
    return total


def kron_matrix(basis):
    size = basis.shape[0]
    count = size * size

    def digits(index):
        lead = jnp.zeros_like(index)
        for step in range(1, size):
            lead = lead + (index >= step * size).astype(jnp.int32)
        return lead, index - lead * size

    def spread(row_digit, col_digit):
        out = jnp.zeros((count, count), f32)
        for i in range(size):
            line = jnp.zeros((1, count), f32)
            for j in range(size):
                line = jnp.where(col_digit == j, basis[i, j], line)
            out = jnp.where(row_digit == i, line, out)
        return out

    (a, b), (c, d) = digits(iota((count, 1), 0)), digits(iota((1, count), 1))
    return spread(a, c) * spread(b, d)


def wave_of(row, count):
    return jnp.where(row == 1, count // 2, row // 2)


def dft_blocks(device, devices, share, rows_of, cols_of):
    count = devices * share
    tall, width = share * len(rows_of), share * len(cols_of)
    copies = SPAN // width

    def index_of(ids, offsets):
        part = ids // share
        owner = jnp.where(part == 0, device ^ offsets[0], 0)
        for i, offset in enumerate(offsets[1:]):
            owner = jnp.where(part == i + 1, device ^ offset, owner)
        return owner * share + ids % share

    row = index_of(iota((tall, SPAN), 0), rows_of)
    plane = index_of(iota((tall, SPAN), 1) % width, cols_of)
    angle = 2.0 * math.pi / count * (wave_of(row, count) * plane % count).astype(f32)
    odd = (row % 2 == 1) & (row != 1)
    scale = jnp.where(row <= 1, math.sqrt(1.0 / count), math.sqrt(2.0 / count))
    block = jnp.where(odd, jnp.sin(angle), jnp.cos(angle)) * scale
    full = jnp.concatenate([block] * copies, axis=0)
    same = iota(full.shape, 0) // tall == iota(full.shape, 1) // width
    return stack_split(jnp.where(same, full, 0.0))


def corner(left, rows, cols):
    height = left.shape[0] // 2
    if (rows, cols) == (height, left.shape[1]):
        return left
    return jnp.concatenate([left[:rows, :cols], left[height : height + rows, :cols]], axis=0)


def octet(block, part):
    rows, _, elems = block.shape
    return block[:, part * TILE : (part + 1) * TILE, :].reshape(rows * TILE, elems)


def take_kernel(nodes, *refs, wanted):
    count = (len(refs) - 2) // 2
    sources, out, copies, ready = refs[:count], refs[count], refs[count + 1 : -1], refs[-1]
    moves = [pltpu.make_async_copy(source, copy, ready.at[i]) for i, (source, copy) in enumerate(zip(sources, copies))]
    first = 0
    runs = []
    for node, length in wanted:
        run = pltpu.make_async_copy(nodes.at[node : node + length], out.at[first : first + length], ready.at[count + len(runs)])
        runs.append(run)
        first += length
    for move in runs + moves:
        move.start()
    for move in runs + moves:
        move.wait()


def per_mode(left, right, values, owner, share, devices, modes):
    size = values.shape[0]
    n = iota(right.shape, 0)
    sums = jnp.zeros(n.shape, f32)
    for c in range(size):
        sums = sums + jnp.where((n >= c * size) & (n < (c + 1) * size), values[c], 0.0)
        for d in range(size):
            sums = sums + jnp.where(n == c * size + d, values[d], 0.0)
    rows = left.shape[0] // 2
    for r in range(share):
        wave = wave_of(owner * share + r, devices * share).astype(f32) * wave_unit
        modes[r, :rows, :] = dot3(left, *split(right / (sums + (helm_base + wave * wave))))


def widened(modes, part, rows, cols):
    block = jnp.transpose(modes[part * TILE : (part + 1) * TILE], (1, 0, 2))[:rows, :, :cols]
    spread = jnp.where(iota((cols, cols * TILE), 0) == iota((cols, cols * TILE), 1) // TILE, 1.0, 0.0).astype(bf16)
    same = (iota((TILE, cols * TILE), 0) == iota((TILE, cols * TILE), 1) % TILE)[None]
    out = []
    for half in split(block.reshape(rows * TILE, cols)):
        full = dot(half, spread).reshape(rows, TILE, cols * TILE)
        out.append(jnp.where(same, full, 0.0).reshape(rows * TILE, cols * TILE).astype(bf16))
    return out


def tables_kernel(
    basis, values, coupling, planes, slots, table, lead, rest, pull, where, held, modes, ready, *, devices
):
    move = pltpu.make_async_copy(planes, held, ready)
    move.start()
    rim, inner = coupling.shape
    elems = slots.shape[1]
    octets, _, first = lead.shape
    edge = inner * TILE
    columns = slots[...].astype(f32).T
    ids = iota((elems, where.shape[1]), 1).astype(f32)
    for j in range(rim):
        where[j * elems : (j + 1) * elems, :] = jnp.where(ids == columns[:, j : j + 1], 1.0, 0.0).astype(bf16)
    kron = kron_matrix(basis)
    couple = exact(coupling[...], kron)
    device = lax.axis_index("mode")
    share = octets * TILE
    spare = lead.shape[1] // (2 * TILE) - inner
    both = jnp.concatenate([couple, kron, jnp.zeros((modes.shape[1] - rim - inner, inner), f32)], axis=0)
    right = jnp.concatenate([kron, couple], axis=0).T
    per_mode(stack_split(couple), right, values, device ^ CORES, share, devices, modes)
    for part in range(octets):
        table[part] = jnp.concatenate(widened(modes, part, rim, inner), axis=0)
    per_mode(stack_split(both), right, values, device, share, devices, modes)
    top = rim * TILE
    for part in range(octets):
        halves = widened(modes, part, rim + inner + spare, rim + inner)

        def put(out, place, rows, cols):
            height = out.shape[1] // 2
            for i, half in enumerate(halves):
                out[place, i * height : (i + 1) * height, :] = half[rows, cols]

        put(table, octets + part, slice(0, top), slice(0, edge))
        put(lead, part, slice(top, None), slice(0, first))
        put(rest, part, slice(top, None), slice(first, edge))
        put(pull, part, slice(top, None), slice(edge, None))
    move.wait()


def near_kernel(
    own, mate, where, table, sums_out, sums_own, send, keep, spectra, *, devices, inner_nodes, rim_nodes
):
    _, share, elems = own.shape
    pair = 2 * share
    inner, rim = len(inner_nodes), len(rim_nodes)
    raw_rows = inner - send.shape[0]
    left = dft_blocks(lax.axis_index("mode"), devices, share, (CORES, 0), (0, 1))
    group = left.shape[1] // pair
    base = 0
    for nodes in (inner_nodes, rim_nodes):
        for first in range(0, len(nodes), group):
            part = nodes[first : first + group]
            block = jnp.concatenate([ref[node] for node in part for ref in (own, mate)], axis=0)
            rows = block.shape[0]
            out = dot3(corner(left, rows, rows), *split(block)).reshape(len(part), pair, elems)
            spectra[base + first : base + first + len(part)] = out
        base += len(nodes)
    send[...] = spectra[raw_rows:inner, :share, :]
    keep[...] = spectra[:inner, share:, :]
    parts = []
    for part in range(pair // TILE):
        place = slice(part * TILE, (part + 1) * TILE)
        block = spectra[:inner, place, :].reshape(inner * TILE, elems)
        coupled = dot3(table[part], *split(block)).reshape(rim, TILE, elems)
        parts.append(spectra[inner:, place, :] - coupled)
    residual = jnp.concatenate(parts, axis=1)
    line = jnp.concatenate([stack_split(residual[j]) for j in range(rim)], axis=1)
    sums = fold(dot(line, where[...]))
    sums_out[...] = sums[:share]
    sums_own[...] = sums[share:]


def far_kernel(keep, first, second, lead, rest, solved, spectral, *, devices):
    rows, share, elems = first.shape
    inner = keep.shape[0]
    left = dft_blocks(lax.axis_index("mode"), devices, share, (0,), (CORES, CORES + 1))
    group = left.shape[1] // (2 * share)
    for start in range(0, rows, group):
        part = range(start, min(start + group, rows))
        block = jnp.concatenate([x for k in part for x in (first[k], second[k])], axis=0)
        out = dot3(corner(left, share * len(part), 2 * share * len(part)), *split(block))
        spectral[start : start + len(part)] = keep[start : start + len(part)] + out.reshape(-1, share, elems)
    for part in range(share // TILE):
        place = slice(part * TILE, (part + 1) * TILE)
        block = dot3(lead[part], *split(octet(spectral[...], part)))
        block = block + dot3(rest[part], *split(keep[rows:, place, :].reshape(-1, elems)))
        solved[:, place, :] = block[: inner * TILE].reshape(inner, TILE, elems)


def back_kernel(sums, *refs, codes):
    neighbours = len(codes)
    near = refs[:neighbours]
    sides, partners, inverse, slots, pull, solved, interior, interface = refs[neighbours:]
    share, unknowns = sums.shape
    inner, _, elems = interior.shape
    rim = slots.shape[0]
    group = lax.axis_index("ex") * lax.axis_size("ey") + lax.axis_index("ey")
    octets = [slice(start, start + TILE) for start in range(0, share, TILE)]
    assembled = [sums[place] for place in octets]
    for i in range(neighbours):
        code = jnp.int32(codes[i][0])
        for g, other in enumerate(codes[i][1:], 1):
            code = jnp.where(group == g, other, code)
        picked = chosen([near[i][place] for place in octets], partners[...])
        assembled = [part + jnp.where(sides[...] == code, new, 0.0) for part, new in zip(assembled, picked)]
    values = []
    for place, part in zip(octets, assembled):
        lines = []
        for r in range(TILE):
            line = jnp.sum(inverse[place.start + r] * part[r : r + 1, :], axis=1).reshape(1, unknowns)
            interface[place.start + r] = line
            lines.append(line)
        values.append(jnp.concatenate(lines, axis=0))
    boundary = [chosen(values, slots[j : j + 1, :]) for j in range(rim)]
    for part, place in enumerate(octets):
        block = jnp.concatenate([blocks[part] for blocks in boundary], axis=0)
        lifted = dot3(pull[part], *split(block))[: inner * TILE].reshape(inner, TILE, elems)
        interior[:, place, :] = solved[:, place, :] - lifted


def final_kernel(base, received, rest, out, interior, ready):
    inner, share, elems = interior.shape
    octets = range(share // TILE)
    blocks = [split(octet(received[...], part)) for part in octets]
    height = rest.shape[1] // 2
    size = -(-inner // RUNS)
    size += size % 2
    moves = []
    for i, first in enumerate(range(0, inner, size)):
        nodes = slice(first, min(first + size, inner))
        count = nodes.stop - first
        tall = (count + count % 2) * TILE
        for part in octets:
            place = slice(part * TILE, (part + 1) * TILE)
            high, low = (rest[part, start + first * TILE : start + first * TILE + tall, :] for start in (0, height))
            product = dot(high, blocks[part][0]) + dot(low, blocks[part][0]) + dot(high, blocks[part][1])
            interior[nodes, place, :] = base[nodes, place, :] + product[: count * TILE].reshape(-1, TILE, elems)
        moves.append(pltpu.make_async_copy(interior.at[nodes], out.at[nodes], ready.at[i]))
        moves[-1].start()
    for move in moves:
        move.wait()


VMEM = pl.BlockSpec(memory_space=pltpu.VMEM)
ANY = pl.BlockSpec(memory_space=pl.ANY)
SMEM = pl.BlockSpec(memory_space=pltpu.SMEM)


def shape(*dims, dtype=f32):
    return jax.ShapeDtypeStruct(dims, dtype)


def kernel_call(body, outs, ins, name, micros, scratch=(), out_specs=None):
    in_specs, arrays = [], []
    for item in ins:
        place, array = item if isinstance(item, tuple) else ("", item)
        in_specs.append({"smem": SMEM, "any": ANY}.get(place, VMEM))
        if place in ("any", "hbm", "vmem"):
            array = pltpu.with_memory_space_constraint(array, pltpu.VMEM if place == "vmem" else pltpu.HBM)
        arrays.append(array)
    return pl.pallas_call(
        body,
        out_shape=outs,
        in_specs=in_specs,
        out_specs=out_specs or ((VMEM,) * len(outs) if isinstance(outs, tuple) else VMEM),
        scratch_shapes=scratch,
        compiler_params=pltpu.CompilerParams(vmem_limit_bytes=LIMIT),
        cost_estimate=pl.CostEstimate(flops=0, transcendentals=0, bytes_accessed=int(micros * 3e6)),
        name=name,
    )(*arrays)


def exchanges(block):
    wide, tall = lax.axis_size("ex"), lax.axis_size("ey")
    group = lambda x, y: x * tall + y
    rounds = []
    for first in range(min(2, tall - 1)):
        pairs = {group(x, y): group(x, y + 1) for x in range(wide) for y in range(first, tall - 1, 2)}
        rounds.append(pairs)
    if len(rounds) == 2:
        busy = set(rounds[1]) | set(rounds[1].values())
        for y in range(tall):
            for x in range(0, wide - 1, 2):
                if not {group(x, y), group(x + 1, y)} & busy:
                    rounds[1][group(x, y)] = group(x + 1, y)
    for first in range(min(2, wide - 1)):
        rounds.append({group(x, y): group(x + 1, y) for x in range(first, wide - 1, 2) for y in range(tall)})
    got, known = [], set()
    for pairs in rounds:
        moves = [*pairs.items(), *((b, a) for a, b in pairs.items())]
        code = [-1] * (wide * tall)
        for a, b in moves:
            if (a, b) not in known:
                known.add((a, b))
                near = abs(a - b) == 1
                code[b] = (3 if near else 1) + (1 if a < b else 0)
        got.append((lax.ppermute(block, ("ex", "ey"), moves), tuple(code)))
    return got


def paired(forcing, eigen_basis, eigen_values, coupling, inverse_blocks, slots, sides, partners):
    inner_nodes, rim_nodes = node_lists()
    share, nodes, elems = forcing.shape
    unknowns = inverse_blocks.shape[1]
    modes = lax.axis_size("mode")
    inner, rim = len(inner_nodes), len(rim_nodes)
    side = round(math.sqrt(nodes))
    raw_rows = inner * RAW_SHARE // 100
    line = side - 2
    runs = [
        (int(inner_nodes[first]), min(line, raw_rows - first)) for first in range(0, raw_rows, line)
    ]
    rest_rows = inner - raw_rows
    octets = share // TILE
    mates = [(i, i ^ 1) for i in range(modes)]
    across = [(i, i ^ CORES) for i in range(modes)]
    planes = jnp.transpose(forcing, (1, 0, 2))
    small = [eigen_basis, eigen_values, coupling, slots]
    own_raw, *small = kernel_call(
        functools.partial(take_kernel, wanted=runs),
        (shape(raw_rows, share, elems), *[jax.ShapeDtypeStruct(x.shape, x.dtype) for x in small]),
        [("any", planes), *[("any", x) for x in small]],
        "raw_rows",
        0.5,
        [pltpu.SemaphoreType.DMA((len(small) + len(runs),))],
    )
    eigen_basis, eigen_values, coupling, slots_held = small
    basis, values = ("smem", eigen_basis), ("smem", eigen_values)
    planes, own_raw = lax.optimization_barrier((planes, own_raw))
    first = lax.ppermute(own_raw, "mode", across)
    mate_planes = lax.ppermute(planes, "mode", mates)
    tall = 2 * TILE
    padded = inner + inner % 2
    table, lead, rest, pull, where, own_planes = kernel_call(
        functools.partial(tables_kernel, devices=modes),
        (
            shape(2 * octets, tall * rim, inner * TILE, dtype=bf16),
            shape(octets, tall * padded, raw_rows * TILE, dtype=bf16),
            shape(octets, tall * padded, rest_rows * TILE, dtype=bf16),
            shape(octets, tall * padded, rim * TILE, dtype=bf16),
            shape(rim * elems, unknowns, dtype=bf16),
            shape(*planes.shape),
        ),
        [basis, values, coupling, ("any", planes), slots_held],
        "tables",
        2.5,
        [pltpu.VMEM((share, -(-(padded + rim) // (2 * TILE)) * 2 * TILE, inner + rim), f32), pltpu.SemaphoreType.DMA],
    )
    sums_out, sums_own, send, keep = kernel_call(
        functools.partial(
            near_kernel,
            devices=modes,
            inner_nodes=[int(node) for node in inner_nodes],
            rim_nodes=[int(node) for node in rim_nodes],
        ),
        (
            shape(share, unknowns),
            shape(share, unknowns),
            shape(rest_rows, share, elems),
            shape(inner, share, elems),
        ),
        [own_planes, mate_planes, where, table],
        "near_spectra",
        3.0,
        [pltpu.VMEM((nodes, 2 * share, elems), f32)],
    )
    sums_in, send = lax.optimization_barrier((lax.ppermute(sums_out, "mode", across), send))
    sums = sums_own + sums_in
    received = lax.ppermute(send, "mode", across)
    second = lax.ppermute(first, "mode", mates)
    solved = kernel_call(
        functools.partial(far_kernel, devices=modes),
        shape(inner, share, elems),
        [keep, first, second, lead, rest],
        "far_spectra",
        1.5,
        [pltpu.VMEM((raw_rows, share, elems), f32)],
    )
    got = exchanges(sums)
    base, interface = kernel_call(
        functools.partial(back_kernel, codes=[codes for _, codes in got]),
        (shape(inner, share, elems), shape(share, 1, unknowns)),
        [sums, *[block for block, _ in got], sides, partners, inverse_blocks, slots, pull, solved],
        "back_solve",
        2.0,
    )
    interior = kernel_call(
        final_kernel,
        shape(inner, share, elems),
        [base, ("vmem", received), rest],
        "interior_solve",
        1.0,
        [pltpu.VMEM((inner, share, elems), f32), pltpu.SemaphoreType.DMA((RUNS,))],
        out_specs=ANY,
    )
    return (jnp.transpose(interior, (1, 0, 2)), interface)


def extended(block, sides, width):
    for axis, dim in sides:
        count = lax.axis_size(axis)
        forward = [(i, i + 1) for i in range(count - 1)]
        backward = [(target, source) for source, target in forward]
        low = lax.ppermute(
            lax.slice_in_dim(block, block.shape[dim] - width, None, axis=dim), axis, forward
        )
        high = lax.ppermute(lax.slice_in_dim(block, 0, width, axis=dim), axis, backward)
        block = jnp.concatenate([low, block, high], axis=dim)
    return block


def wave_numbers(row_ids, count):
    return jnp.where(row_ids == 1, count // 2, row_ids // 2)


def dft_table(count):
    row_ids = jnp.arange(count, dtype=jnp.int32)
    wave_ids = wave_numbers(row_ids, count)
    phase_ids = wave_ids[:, None] * row_ids[None, :] % count
    angles = 2.0 * math.pi / count * phase_ids.astype(jnp.float32)
    odd_rows = (row_ids % 2 == 1) & (row_ids != 1)
    scales = jnp.where(row_ids <= 1, math.sqrt(1.0 / count), math.sqrt(2.0 / count)).astype(
        jnp.float32
    )
    return jnp.where(odd_rows[:, None], jnp.sin(angles), jnp.cos(angles)) * scales[:, None]


def mode_shifts(row_ids, count):
    waves = wave_numbers(row_ids, count).astype(jnp.float32) * wave_unit
    return helm_base + waves * waves


def fast_solve(values, eigen_basis, eigen_values, shifts):
    kron_basis = jnp.kron(eigen_basis, eigen_basis)
    pair_sums = (eigen_values[:, None] + eigen_values[None, :]).reshape(-1)
    spectra = jnp.einsum("ji,rje->rie", kron_basis, values, precision=lax.Precision.HIGHEST)
    spectra = spectra / (pair_sums[None, :, None] + shifts[:, None, None])
    return jnp.einsum("ij,rje->rie", kron_basis, spectra, precision=lax.Precision.HIGHEST)


def general(forcing, eigen_basis, eigen_values, coupling, inverse_blocks, slots, sides, partners):
    inner_nodes, rim_nodes = node_lists()
    plane_dev = forcing.shape[0]
    elem_dev = forcing.shape[2]
    unknowns = inverse_blocks.shape[1]
    modes_axis = lax.axis_size("mode")
    plane_count = modes_axis * plane_dev
    table = dft_table(plane_count)
    row_ids = lax.axis_index("mode") * plane_dev + jnp.arange(plane_dev, dtype=jnp.int32)
    shifts = mode_shifts(row_ids, plane_count)
    onehot = (slots.reshape(-1)[:, None] == jnp.arange(unknowns, dtype=jnp.int32)[None, :]).astype(
        jnp.float32
    )
    inner_width = len(inner_nodes) * elem_dev
    rim_planes = forcing[:, rim_nodes, :].reshape(plane_dev, -1)
    condensed = jnp.dot(rim_planes, onehot, precision=lax.Precision.HIGHEST)
    payload = jnp.concatenate(
        [forcing[:, inner_nodes, :].reshape(plane_dev, -1), condensed], axis=1
    )
    total_width = payload.shape[1]
    sectioned = payload.reshape(plane_dev, modes_axis, total_width // modes_axis)
    spectra = jnp.einsum(
        "rp,pkc->rkc",
        table,
        lax.all_to_all(sectioned, "mode", split_axis=1, concat_axis=0, tiled=True),
        precision=lax.Precision.HIGHEST,
    )
    spectral = lax.all_to_all(spectra, "mode", split_axis=0, concat_axis=1, tiled=True).reshape(
        plane_dev, total_width
    )
    inner_part = spectral[:, :inner_width].reshape(plane_dev, len(inner_nodes), elem_dev)
    condensed_hat = spectral[:, inner_width:]
    solved = fast_solve(inner_part, eigen_basis, eigen_values, shifts)
    coupled = jnp.einsum("ji,rie->rje", coupling, solved, precision=lax.Precision.HIGHEST)
    local_sums = condensed_hat - jnp.dot(
        coupled.reshape(plane_dev, -1), onehot, precision=lax.Precision.HIGHEST
    )
    padded = extended(local_sums.reshape(1, 1, -1), (("ex", 0), ("ey", 1)), 1)
    neighbours = (
        padded[2, 1].reshape(plane_dev, unknowns),
        padded[0, 1].reshape(plane_dev, unknowns),
        padded[1, 2].reshape(plane_dev, unknowns),
        padded[1, 0].reshape(plane_dev, unknowns),
    )
    assembled = local_sums
    for side_code, neighbour in enumerate(neighbours):
        picked = jnp.take(neighbour, partners[0], axis=1)
        assembled = assembled + jnp.where(
            (sides[0] == side_code + 1)[None, :], picked, jnp.zeros_like(picked)
        )
    interface = jnp.einsum("rst,rt->rs", inverse_blocks, assembled, precision=lax.Precision.HIGHEST)
    boundary = jnp.dot(interface, onehot.T, precision=lax.Precision.HIGHEST).reshape(
        plane_dev, len(rim_nodes), elem_dev
    )
    lifted = jnp.einsum("ji,rje->rie", coupling, boundary, precision=lax.Precision.HIGHEST)
    interior = solved - fast_solve(lifted, eigen_basis, eigen_values, shifts)
    return (interior, interface[:, None, :])


def on_device(*args):
    modes = lax.axis_size("mode")
    if modes == CORES * CORES:
        return paired(*args)
    return general(*args)


def solution(mesh):
    placed = (
        P("mode", None, ("ex", "ey")),
        P(),
        P(),
        P(),
        P("mode", None, None),
        P(None, ("ex", "ey")),
        P(("ex", "ey"), None),
        P(("ex", "ey"), None),
    )
    return jax.shard_map(
        on_device,
        mesh=mesh,
        in_specs=placed,
        out_specs=(P("mode", None, ("ex", "ey")), P("mode", ("ex", "ey"), None)),
        check_vma=False,
    )
```

```python
import functools
import math

import jax
import jax.numpy as jnp
import numpy as np
from jax import lax
from jax.experimental import pallas as pl
from jax.experimental.pallas import tpu as pltpu
from jax.sharding import PartitionSpec as P

helm_base = 0.5
wave_unit = 1.0 / 64.0
f32, bf16 = jnp.float32, jnp.bfloat16
TILE = 8
CORES = 2
SPAN = 256
RUNS = 4
RAW_SHARE = 51
LIMIT = 12 * 2**20


def is_inner(node_id):
    return 1 <= node_id // 9 <= 7 and 1 <= node_id % 9 <= 7


def node_lists():
    inner_nodes = np.array([node_id for node_id in range(81) if is_inner(node_id)], dtype=np.int32)
    rim_nodes = np.array(
        [node_id for node_id in range(81) if not is_inner(node_id)], dtype=np.int32
    )
    return (inner_nodes, rim_nodes)


def split(values):
    high = values.astype(bf16)
    return high, (values - high.astype(f32)).astype(bf16)


def stack_split(values):
    return jnp.concatenate(split(values), axis=0)


def dot(left, right):
    return jnp.dot(left, right, preferred_element_type=f32)


def exact(left, right):
    return jnp.dot(left, right, preferred_element_type=f32, precision=lax.Precision.HIGHEST)


def dot_t(left, right):
    return lax.dot_general(left, right, (((1,), (1,)), ((), ())), preferred_element_type=f32)


def fold(values):
    half = values.shape[0] // 2
    return values[:half] + values[half:]


def dot3(left, high, low):
    return fold(dot(left, high)) + dot(left[: left.shape[0] // 2], low)


def iota(shape, dim):
    return lax.broadcasted_iota(jnp.int32, shape, dim)


def chosen(blocks, line):
    lanes = 128
    width = blocks[0].shape[1]
    out = [[] for _ in blocks]
    for start in range(0, line.shape[1], lanes):
        index = jnp.broadcast_to(line[:, start : start + lanes], (TILE, lanes))
        place = index & (lanes - 1)
        beyond = [index >= first for first in range(lanes, width, lanes)]
        for block, parts in zip(blocks, out):
            found = jnp.take_along_axis(block[:, :lanes], place, axis=1)
            for i, mask in enumerate(beyond):
                first = (i + 1) * lanes
                found = jnp.where(mask, jnp.take_along_axis(block[:, first : first + lanes], place, axis=1), found)
            parts.append(found)
    return [jnp.concatenate(parts, axis=1) for parts in out]


def member(line, unknowns):
    return jnp.where(iota((unknowns, line.shape[1]), 0) == line, 1.0, 0.0).astype(bf16)


def weighted(scalars, blocks):
    total = scalars[0] * blocks[0]
    for scalar, block in zip(scalars[1:], blocks[1:]):
        total = total + scalar * block
    return total


def kron_matrix(basis):
    size = basis.shape[0]
    count = size * size

    def digits(index):
        lead = jnp.zeros_like(index)
        for step in range(1, size):
            lead = lead + (index >= step * size).astype(jnp.int32)
        return lead, index - lead * size

    def spread(row_digit, col_digit):
        out = jnp.zeros((count, count), f32)
        for i in range(size):
            line = jnp.zeros((1, count), f32)
            for j in range(size):
                line = jnp.where(col_digit == j, basis[i, j], line)
            out = jnp.where(row_digit == i, line, out)
        return out

    (a, b), (c, d) = digits(iota((count, 1), 0)), digits(iota((1, count), 1))
    return spread(a, c) * spread(b, d)


def wave_of(row, count):
    return jnp.where(row == 1, count // 2, row // 2)


def dft_blocks(device, devices, share, rows_of, cols_of):
    count = devices * share
    tall, width = share * len(rows_of), share * len(cols_of)
    copies = SPAN // width

    def index_of(ids, offsets):
        part = ids // share
        owner = jnp.where(part == 0, device ^ offsets[0], 0)
        for i, offset in enumerate(offsets[1:]):
            owner = jnp.where(part == i + 1, device ^ offset, owner)
        return owner * share + ids % share

    row = index_of(iota((tall, SPAN), 0), rows_of)
    plane = index_of(iota((tall, SPAN), 1) % width, cols_of)
    angle = 2.0 * math.pi / count * (wave_of(row, count) * plane % count).astype(f32)
    odd = (row % 2 == 1) & (row != 1)
    scale = jnp.where(row <= 1, math.sqrt(1.0 / count), math.sqrt(2.0 / count))
    block = jnp.where(odd, jnp.sin(angle), jnp.cos(angle)) * scale
    full = jnp.concatenate([block] * copies, axis=0)
    same = iota(full.shape, 0) // tall == iota(full.shape, 1) // width
    return stack_split(jnp.where(same, full, 0.0))


def corner(left, rows, cols):
    height = left.shape[0] // 2
    if (rows, cols) == (height, left.shape[1]):
        return left
    return jnp.concatenate([left[:rows, :cols], left[height : height + rows, :cols]], axis=0)


def octet(block, part):
    rows, _, elems = block.shape
    return block[:, part * TILE : (part + 1) * TILE, :].reshape(rows * TILE, elems)


def take_kernel(nodes, *refs, wanted):
    count = (len(refs) - 2) // 2
    sources, out, copies, ready = refs[:count], refs[count], refs[count + 1 : -1], refs[-1]
    moves = [pltpu.make_async_copy(source, copy, ready.at[i]) for i, (source, copy) in enumerate(zip(sources, copies))]
    first = 0
    runs = []
    for node, length in wanted:
        run = pltpu.make_async_copy(nodes.at[node : node + length], out.at[first : first + length], ready.at[count + len(runs)])
        runs.append(run)
        first += length
    for move in runs + moves:
        move.start()
    for move in runs + moves:
        move.wait()


def per_mode(left, right, values, owner, share, devices, modes):
    size = values.shape[0]
    n = iota(right.shape, 0)
    sums = jnp.zeros(n.shape, f32)
    for c in range(size):
        sums = sums + jnp.where((n >= c * size) & (n < (c + 1) * size), values[c], 0.0)
        for d in range(size):
            sums = sums + jnp.where(n == c * size + d, values[d], 0.0)
    rows = left.shape[0] // 2
    for r in range(share):
        wave = wave_of(owner * share + r, devices * share).astype(f32) * wave_unit
        modes[r, :rows, :] = dot3(left, *split(right / (sums + (helm_base + wave * wave))))


def widened(modes, part, rows, cols):
    block = jnp.transpose(modes[part * TILE : (part + 1) * TILE], (1, 0, 2))[:rows, :, :cols]
    spread = jnp.where(iota((cols, cols * TILE), 0) == iota((cols, cols * TILE), 1) // TILE, 1.0, 0.0).astype(bf16)
    same = (iota((TILE, cols * TILE), 0) == iota((TILE, cols * TILE), 1) % TILE)[None]
    out = []
    for half in split(block.reshape(rows * TILE, cols)):
        full = dot(half, spread).reshape(rows, TILE, cols * TILE)
        out.append(jnp.where(same, full, 0.0).reshape(rows * TILE, cols * TILE).astype(bf16))
    return out


def tables_kernel(
    basis, values, coupling, planes, slots, table, lead, rest, pull, where, held, modes, ready, *, devices
):
    move = pltpu.make_async_copy(planes, held, ready)
    move.start()
    rim, inner = coupling.shape
    elems = slots.shape[1]
    octets, _, first = lead.shape
    edge = inner * TILE
    columns = slots[...].astype(f32).T
    ids = iota((elems, where.shape[1]), 1).astype(f32)
    for j in range(rim):
        where[j * elems : (j + 1) * elems, :] = jnp.where(ids == columns[:, j : j + 1], 1.0, 0.0).astype(bf16)
    kron = kron_matrix(basis)
    couple = exact(coupling[...], kron)
    device = lax.axis_index("mode")
    share = octets * TILE
    spare = lead.shape[1] // (2 * TILE) - inner
    both = jnp.concatenate([couple, kron, jnp.zeros((modes.shape[1] - rim - inner, inner), f32)], axis=0)
    right = jnp.concatenate([kron, couple], axis=0).T
    per_mode(stack_split(couple), right, values, device ^ CORES, share, devices, modes)
    for part in range(octets):
        table[part] = jnp.concatenate(widened(modes, part, rim, inner), axis=0)
    per_mode(stack_split(both), right, values, device, share, devices, modes)
    top = rim * TILE
    for part in range(octets):
        halves = widened(modes, part, rim + inner + spare, rim + inner)

        def put(out, place, rows, cols):
            height = out.shape[1] // 2
            for i, half in enumerate(halves):
                out[place, i * height : (i + 1) * height, :] = half[rows, cols]

        put(table, octets + part, slice(0, top), slice(0, edge))
        put(lead, part, slice(top, None), slice(0, first))
        put(rest, part, slice(top, None), slice(first, edge))
        put(pull, part, slice(top, None), slice(edge, None))
    move.wait()


def near_kernel(
    own, mate, where, table, sums_out, sums_own, send, keep, spectra, *, devices, inner_nodes, rim_nodes
):
    _, share, elems = own.shape
    pair = 2 * share
    inner, rim = len(inner_nodes), len(rim_nodes)
    raw_rows = inner - send.shape[0]
    left = dft_blocks(lax.axis_index("mode"), devices, share, (CORES, 0), (0, 1))
    group = left.shape[1] // pair
    base = 0
    for nodes in (inner_nodes, rim_nodes):
        for first in range(0, len(nodes), group):
            part = nodes[first : first + group]
            block = jnp.concatenate([ref[node] for node in part for ref in (own, mate)], axis=0)
            rows = block.shape[0]
            out = dot3(corner(left, rows, rows), *split(block)).reshape(len(part), pair, elems)
            spectra[base + first : base + first + len(part)] = out
        base += len(nodes)
    send[...] = spectra[raw_rows:inner, :share, :]
    keep[...] = spectra[:inner, share:, :]
    parts = []
    for part in range(pair // TILE):
        place = slice(part * TILE, (part + 1) * TILE)
        block = spectra[:inner, place, :].reshape(inner * TILE, elems)
        coupled = dot3(table[part], *split(block)).reshape(rim, TILE, elems)
        parts.append(spectra[inner:, place, :] - coupled)
    residual = jnp.concatenate(parts, axis=1)
    line = jnp.concatenate([stack_split(residual[j]) for j in range(rim)], axis=1)
    sums = fold(dot(line, where[...]))
    sums_out[...] = sums[:share]
    sums_own[...] = sums[share:]


def far_kernel(keep, first, second, lead, rest, solved, spectral, *, devices):
    rows, share, elems = first.shape
    inner = keep.shape[0]
    left = dft_blocks(lax.axis_index("mode"), devices, share, (0,), (CORES, CORES + 1))
    group = left.shape[1] // (2 * share)
    for start in range(0, rows, group):
        part = range(start, min(start + group, rows))
        block = jnp.concatenate([x for k in part for x in (first[k], second[k])], axis=0)
        out = dot3(corner(left, share * len(part), 2 * share * len(part)), *split(block))
        spectral[start : start + len(part)] = keep[start : start + len(part)] + out.reshape(-1, share, elems)
    for part in range(share // TILE):
        place = slice(part * TILE, (part + 1) * TILE)
        block = dot3(lead[part], *split(octet(spectral[...], part)))
        block = block + dot3(rest[part], *split(keep[rows:, place, :].reshape(-1, elems)))
        solved[:, place, :] = block[: inner * TILE].reshape(inner, TILE, elems)


def back_kernel(sums, *refs, codes):
    neighbours = len(codes)
    near = refs[:neighbours]
    sides, partners, inverse, slots, pull, solved, interior, interface = refs[neighbours:]
    share, unknowns = sums.shape
    inner, _, elems = interior.shape
    rim = slots.shape[0]
    group = lax.axis_index("ex") * lax.axis_size("ey") + lax.axis_index("ey")
    octets = [slice(start, start + TILE) for start in range(0, share, TILE)]
    assembled = [sums[place] for place in octets]
    for i in range(neighbours):
        code = jnp.int32(codes[i][0])
        for g, other in enumerate(codes[i][1:], 1):
            code = jnp.where(group == g, other, code)
        picked = chosen([near[i][place] for place in octets], partners[...])
        assembled = [part + jnp.where(sides[...] == code, new, 0.0) for part, new in zip(assembled, picked)]
    values = []
    for place, part in zip(octets, assembled):
        lines = []
        for r in range(TILE):
            line = jnp.sum(inverse[place.start + r] * part[r : r + 1, :], axis=1).reshape(1, unknowns)
            interface[place.start + r] = line
            lines.append(line)
        values.append(jnp.concatenate(lines, axis=0))
    boundary = [chosen(values, slots[j : j + 1, :]) for j in range(rim)]
    for part, place in enumerate(octets):
        block = jnp.concatenate([blocks[part] for blocks in boundary], axis=0)
        lifted = dot3(pull[part], *split(block))[: inner * TILE].reshape(inner, TILE, elems)
        interior[:, place, :] = solved[:, place, :] - lifted


def final_kernel(base, received, rest, out, interior, ready):
    inner, share, elems = interior.shape
    octets = range(share // TILE)
    blocks = [split(octet(received[...], part)) for part in octets]
    height = rest.shape[1] // 2
    size = -(-inner // RUNS)
    size += size % 2
    moves = []
    for i, first in enumerate(range(0, inner, size)):
        nodes = slice(first, min(first + size, inner))
        count = nodes.stop - first
        tall = (count + count % 2) * TILE
        for part in octets:
            place = slice(part * TILE, (part + 1) * TILE)
            high, low = (rest[part, start + first * TILE : start + first * TILE + tall, :] for start in (0, height))
            product = dot(high, blocks[part][0]) + dot(low, blocks[part][0]) + dot(high, blocks[part][1])
            interior[nodes, place, :] = base[nodes, place, :] + product[: count * TILE].reshape(-1, TILE, elems)
        moves.append(pltpu.make_async_copy(interior.at[nodes], out.at[nodes], ready.at[i]))
        moves[-1].start()
    for move in moves:
        move.wait()


VMEM = pl.BlockSpec(memory_space=pltpu.VMEM)
ANY = pl.BlockSpec(memory_space=pl.ANY)
SMEM = pl.BlockSpec(memory_space=pltpu.SMEM)


def shape(*dims, dtype=f32):
    return jax.ShapeDtypeStruct(dims, dtype)


def kernel_call(body, outs, ins, name, micros, scratch=(), out_specs=None):
    in_specs, arrays = [], []
    for item in ins:
        place, array = item if isinstance(item, tuple) else ("", item)
        in_specs.append({"smem": SMEM, "any": ANY}.get(place, VMEM))
        if place in ("any", "hbm", "vmem"):
            array = pltpu.with_memory_space_constraint(array, pltpu.VMEM if place == "vmem" else pltpu.HBM)
        arrays.append(array)
    return pl.pallas_call(
        body,
        out_shape=outs,
        in_specs=in_specs,
        out_specs=out_specs or ((VMEM,) * len(outs) if isinstance(outs, tuple) else VMEM),
        scratch_shapes=scratch,
        compiler_params=pltpu.CompilerParams(vmem_limit_bytes=LIMIT),
        cost_estimate=pl.CostEstimate(flops=0, transcendentals=0, bytes_accessed=int(micros * 3e6)),
        name=name,
    )(*arrays)


def exchanges(block):
    wide, tall = lax.axis_size("ex"), lax.axis_size("ey")
    group = lambda x, y: x * tall + y
    rounds = []
    for first in range(min(2, tall - 1)):
        pairs = {group(x, y): group(x, y + 1) for x in range(wide) for y in range(first, tall - 1, 2)}
        rounds.append(pairs)
    if len(rounds) == 2:
        busy = set(rounds[1]) | set(rounds[1].values())
        for y in range(tall):
            for x in range(0, wide - 1, 2):
                if not {group(x, y), group(x + 1, y)} & busy:
                    rounds[1][group(x, y)] = group(x + 1, y)
    for first in range(min(2, wide - 1)):
        rounds.append({group(x, y): group(x + 1, y) for x in range(first, wide - 1, 2) for y in range(tall)})
    got, known = [], set()
    for pairs in rounds:
        moves = [*pairs.items(), *((b, a) for a, b in pairs.items())]
        code = [-1] * (wide * tall)
        for a, b in moves:
            if (a, b) not in known:
                known.add((a, b))
                near = abs(a - b) == 1
                code[b] = (3 if near else 1) + (1 if a < b else 0)
        got.append((lax.ppermute(block, ("ex", "ey"), moves), tuple(code)))
    return got


def paired(forcing, eigen_basis, eigen_values, coupling, inverse_blocks, slots, sides, partners):
    inner_nodes, rim_nodes = node_lists()
    share, nodes, elems = forcing.shape
    unknowns = inverse_blocks.shape[1]
    modes = lax.axis_size("mode")
    inner, rim = len(inner_nodes), len(rim_nodes)
    side = round(math.sqrt(nodes))
    raw_rows = inner * RAW_SHARE // 100
    line = side - 2
    runs = [
        (int(inner_nodes[first]), min(line, raw_rows - first)) for first in range(0, raw_rows, line)
    ]
    rest_rows = inner - raw_rows
    octets = share // TILE
    mates = [(i, i ^ 1) for i in range(modes)]
    across = [(i, i ^ CORES) for i in range(modes)]
    planes = jnp.transpose(forcing, (1, 0, 2))
    small = [eigen_basis, eigen_values, coupling, slots]
    own_raw, *small = kernel_call(
        functools.partial(take_kernel, wanted=runs),
        (shape(raw_rows, share, elems), *[jax.ShapeDtypeStruct(x.shape, x.dtype) for x in small]),
        [("any", planes), *[("any", x) for x in small]],
        "raw_rows",
        0.5,
        [pltpu.SemaphoreType.DMA((len(small) + len(runs),))],
    )
    eigen_basis, eigen_values, coupling, slots_held = small
    basis, values = ("smem", eigen_basis), ("smem", eigen_values)
    first = lax.ppermute(own_raw, "mode", across)
    mate_planes = lax.ppermute(planes, "mode", mates)
    tall = 2 * TILE
    padded = inner + inner % 2
    table, lead, rest, pull, where, own_planes = kernel_call(
        functools.partial(tables_kernel, devices=modes),
        (
            shape(2 * octets, tall * rim, inner * TILE, dtype=bf16),
            shape(octets, tall * padded, raw_rows * TILE, dtype=bf16),
            shape(octets, tall * padded, rest_rows * TILE, dtype=bf16),
            shape(octets, tall * padded, rim * TILE, dtype=bf16),
            shape(rim * elems, unknowns, dtype=bf16),
            shape(*planes.shape),
        ),
        [basis, values, coupling, ("any", planes), slots_held],
        "tables",
        2.5,
        [pltpu.VMEM((share, -(-(padded + rim) // (2 * TILE)) * 2 * TILE, inner + rim), f32), pltpu.SemaphoreType.DMA],
    )
    sums_out, sums_own, send, keep = kernel_call(
        functools.partial(
            near_kernel,
            devices=modes,
            inner_nodes=[int(node) for node in inner_nodes],
            rim_nodes=[int(node) for node in rim_nodes],
        ),
        (
            shape(share, unknowns),
            shape(share, unknowns),
            shape(rest_rows, share, elems),
            shape(inner, share, elems),
        ),
        [own_planes, mate_planes, where, table],
        "near_spectra",
        3.0,
        [pltpu.VMEM((nodes, 2 * share, elems), f32)],
    )
    sums_in, send = lax.optimization_barrier((lax.ppermute(sums_out, "mode", across), send))
    sums = sums_own + sums_in
    received = lax.ppermute(send, "mode", across)
    second = lax.ppermute(first, "mode", mates)
    solved = kernel_call(
        functools.partial(far_kernel, devices=modes),
        shape(inner, share, elems),
        [keep, first, second, lead, rest],
        "far_spectra",
        1.5,
        [pltpu.VMEM((raw_rows, share, elems), f32)],
    )
    got = exchanges(sums)
    base, interface = kernel_call(
        functools.partial(back_kernel, codes=[codes for _, codes in got]),
        (shape(inner, share, elems), shape(share, 1, unknowns)),
        [sums, *[block for block, _ in got], sides, partners, inverse_blocks, slots, pull, solved],
        "back_solve",
        2.0,
    )
    interior = kernel_call(
        final_kernel,
        shape(inner, share, elems),
        [base, ("vmem", received), rest],
        "interior_solve",
        1.0,
        [pltpu.VMEM((inner, share, elems), f32), pltpu.SemaphoreType.DMA((RUNS,))],
        out_specs=ANY,
    )
    return (jnp.transpose(interior, (1, 0, 2)), interface)


def extended(block, sides, width):
    for axis, dim in sides:
        count = lax.axis_size(axis)
        forward = [(i, i + 1) for i in range(count - 1)]
        backward = [(target, source) for source, target in forward]
        low = lax.ppermute(
            lax.slice_in_dim(block, block.shape[dim] - width, None, axis=dim), axis, forward
        )
        high = lax.ppermute(lax.slice_in_dim(block, 0, width, axis=dim), axis, backward)
        block = jnp.concatenate([low, block, high], axis=dim)
    return block


def wave_numbers(row_ids, count):
    return jnp.where(row_ids == 1, count // 2, row_ids // 2)


def dft_table(count):
    row_ids = jnp.arange(count, dtype=jnp.int32)
    wave_ids = wave_numbers(row_ids, count)
    phase_ids = wave_ids[:, None] * row_ids[None, :] % count
    angles = 2.0 * math.pi / count * phase_ids.astype(jnp.float32)
    odd_rows = (row_ids % 2 == 1) & (row_ids != 1)
    scales = jnp.where(row_ids <= 1, math.sqrt(1.0 / count), math.sqrt(2.0 / count)).astype(
        jnp.float32
    )
    return jnp.where(odd_rows[:, None], jnp.sin(angles), jnp.cos(angles)) * scales[:, None]


def mode_shifts(row_ids, count):
    waves = wave_numbers(row_ids, count).astype(jnp.float32) * wave_unit
    return helm_base + waves * waves


def fast_solve(values, eigen_basis, eigen_values, shifts):
    kron_basis = jnp.kron(eigen_basis, eigen_basis)
    pair_sums = (eigen_values[:, None] + eigen_values[None, :]).reshape(-1)
    spectra = jnp.einsum("ji,rje->rie", kron_basis, values, precision=lax.Precision.HIGHEST)
    spectra = spectra / (pair_sums[None, :, None] + shifts[:, None, None])
    return jnp.einsum("ij,rje->rie", kron_basis, spectra, precision=lax.Precision.HIGHEST)


def general(forcing, eigen_basis, eigen_values, coupling, inverse_blocks, slots, sides, partners):
    inner_nodes, rim_nodes = node_lists()
    plane_dev = forcing.shape[0]
    elem_dev = forcing.shape[2]
    unknowns = inverse_blocks.shape[1]
    modes_axis = lax.axis_size("mode")
    plane_count = modes_axis * plane_dev
    table = dft_table(plane_count)
    row_ids = lax.axis_index("mode") * plane_dev + jnp.arange(plane_dev, dtype=jnp.int32)
    shifts = mode_shifts(row_ids, plane_count)
    onehot = (slots.reshape(-1)[:, None] == jnp.arange(unknowns, dtype=jnp.int32)[None, :]).astype(
        jnp.float32
    )
    inner_width = len(inner_nodes) * elem_dev
    rim_planes = forcing[:, rim_nodes, :].reshape(plane_dev, -1)
    condensed = jnp.dot(rim_planes, onehot, precision=lax.Precision.HIGHEST)
    payload = jnp.concatenate(
        [forcing[:, inner_nodes, :].reshape(plane_dev, -1), condensed], axis=1
    )
    total_width = payload.shape[1]
    sectioned = payload.reshape(plane_dev, modes_axis, total_width // modes_axis)
    spectra = jnp.einsum(
        "rp,pkc->rkc",
        table,
        lax.all_to_all(sectioned, "mode", split_axis=1, concat_axis=0, tiled=True),
        precision=lax.Precision.HIGHEST,
    )
    spectral = lax.all_to_all(spectra, "mode", split_axis=0, concat_axis=1, tiled=True).reshape(
        plane_dev, total_width
    )
    inner_part = spectral[:, :inner_width].reshape(plane_dev, len(inner_nodes), elem_dev)
    condensed_hat = spectral[:, inner_width:]
    solved = fast_solve(inner_part, eigen_basis, eigen_values, shifts)
    coupled = jnp.einsum("ji,rie->rje", coupling, solved, precision=lax.Precision.HIGHEST)
    local_sums = condensed_hat - jnp.dot(
        coupled.reshape(plane_dev, -1), onehot, precision=lax.Precision.HIGHEST
    )
    padded = extended(local_sums.reshape(1, 1, -1), (("ex", 0), ("ey", 1)), 1)
    neighbours = (
        padded[2, 1].reshape(plane_dev, unknowns),
        padded[0, 1].reshape(plane_dev, unknowns),
        padded[1, 2].reshape(plane_dev, unknowns),
        padded[1, 0].reshape(plane_dev, unknowns),
    )
    assembled = local_sums
    for side_code, neighbour in enumerate(neighbours):
        picked = jnp.take(neighbour, partners[0], axis=1)
        assembled = assembled + jnp.where(
            (sides[0] == side_code + 1)[None, :], picked, jnp.zeros_like(picked)
        )
    interface = jnp.einsum("rst,rt->rs", inverse_blocks, assembled, precision=lax.Precision.HIGHEST)
    boundary = jnp.dot(interface, onehot.T, precision=lax.Precision.HIGHEST).reshape(
        plane_dev, len(rim_nodes), elem_dev
    )
    lifted = jnp.einsum("ji,rje->rie", coupling, boundary, precision=lax.Precision.HIGHEST)
    interior = solved - fast_solve(lifted, eigen_basis, eigen_values, shifts)
    return (interior, interface[:, None, :])


def on_device(*args):
    modes = lax.axis_size("mode")
    if modes == CORES * CORES:
        return paired(*args)
    return general(*args)


def solution(mesh):
    placed = (
        P("mode", None, ("ex", "ey")),
        P(),
        P(),
        P(),
        P("mode", None, None),
        P(None, ("ex", "ey")),
        P(("ex", "ey"), None),
        P(("ex", "ey"), None),
    )
    return jax.shard_map(
        on_device,
        mesh=mesh,
        in_specs=placed,
        out_specs=(P("mode", None, ("ex", "ey")), P("mode", ("ex", "ey"), None)),
        check_vma=False,
    )
```
